32 devices in a mesh: row: 4 (over x, core), col: 8 (over z, y).
Axes of the slice: x: 2, y: 2, z: 4, core: 2. Of those that a mesh axis runs over, the one named last changes fastest.
Arguments:
- density_factor: bfloat16 [131072, 256], P(('row', 'col'))
- onsite: float32 [131072], P(('row', 'col')), may hold values from -4 to 4
- neighbour_ids: int32 [256, 8], P(('row', 'col')), may hold values from 0 to 255, as said below
- neighbour_count: int32 [256], P(('row', 'col')), may hold values from 1 to 8, as said below
- coupling_type: int32 [256, 8], P(('row', 'col')), may hold values from 0 to 3
- coupling_blocks: bfloat16 [4, 512, 512], replicated, may hold values from -0.25 to 0.25
- bath_pattern: int32 [256], P(('row', 'col')), may hold values from 0 to 3
- bath_blocks: bfloat16 [4, 512, 512], replicated, may hold values from -0.25 to 0.25
Outputs:
- new_factor: bfloat16 [131072, 256], P(('row', 'col'))
The draws below stay inside these ranges and needn't reach their ends.
Inputs may be any that keep to these rules, and one draw needn't show every extreme that they name: `neighbour_ids`: every neighbour of block b lies among the 64 blocks that share b's index of row, at most half of 64 blocks from b when that group is taken as a loop, and is never b itself; some block has a neighbour exactly half of 64 blocks away. Only the first neighbour_count[b] slots of block b's lists are used; some block uses all 8.
All inputs are finite; a program needn't handle non-finite values.
Results may differ from the reference program's by a relative error of at most 0.0056.
Values may be sent and summed in bfloat16 or wider, within the bound.
No kernel may reach another device: no remote copies, remote signals or barrier semaphores. Data moves between devices by JAX's collectives and lax.ppermute only.
A program may use at most 192 MiB of HBM per device.

```python
import jax
import jax.numpy as jnp
from jax import lax

BLK = 512
RANK = 256
NT = 4
NB = 4
KMAX = 8
SWEEPS = 2
NBLK = 256
NST = 131072
GROUP = 64


def draw_density_factor(key, part):
    keys = jax.random.split(key, 3)
    positions = jnp.arange(NST, dtype=jnp.float32)[:, None]
    rising = 1.0 + 2.0 * positions / NST
    row_scale = jnp.exp(jax.random.uniform(keys[1], (NST, 1), jnp.float32) * jnp.log(10.0))
    col_scale = jnp.exp(jax.random.uniform(keys[2], (1, RANK), jnp.float32) * jnp.log(3.0))
    values = jnp.clip(jax.random.normal(keys[0], (NST, RANK), jnp.float32), -6.0, 6.0)
    return (values * row_scale * col_scale * rising * 0.125).astype(jnp.bfloat16)


def draw_neighbour_ids(key, part):
    first_key, second_key = jax.random.split(key)
    blocks = jnp.arange(NBLK, dtype=jnp.int32)[:, None]
    reach = GROUP // 2
    distance = jax.random.randint(first_key, (NBLK, KMAX), 1, reach + 1)
    direction = jax.random.randint(second_key, (NBLK, KMAX), 0, 2) * 2 - 1
    offset = (distance * direction).at[0, 0].set(reach)
    group_start = blocks // GROUP * GROUP
    return (group_start + (blocks - group_start + offset) % GROUP).astype(jnp.int32)


def draw_neighbour_count(key, part):
    counts = jax.random.randint(key, (NBLK,), 1, KMAX + 1)
    return counts.at[0].set(KMAX).astype(jnp.int32)


def plant(values, own_key, smallest, largest):
    dims = values.shape
    spot = [jax.random.randint(jax.random.fold_in(own_key, axis), (), 0, dims[axis]) for axis in range(len(dims))]
    values = values.at[tuple(spot)].set(smallest)
    longest = dims.index(max(dims))
    spot[longest] = (spot[longest] + 1) % dims[longest]
    return values.at[tuple(spot)].set(largest)


def level_of(stream_key, dims, shards, low, top_value):
    factor_of, own = 1.0, jax.random.fold_in(stream_key, 6)
    for dim, blocks in shards:
        heights = jnp.exp(jax.random.uniform(jax.random.fold_in(own, dim), (blocks,), jnp.float32, low / len(shards), top_value / len(shards)))
        factor_of = factor_of * jnp.repeat(heights, dims[dim] // blocks).reshape([-1 if axis == dim else 1 for axis in range(len(dims))])
    return factor_of


def gaussian(rng, extent, spread, bound, cuts=(), kind=jnp.bfloat16):
    factor_of = level_of(rng, extent, cuts, -0.22, 0.18) if cuts else 1.0
    result = jax.random.normal(rng, extent, jnp.float32) * spread * factor_of
    return jnp.minimum(jnp.maximum(result, -bound), bound).astype(kind)


def setup_inputs(seed: int = 0) -> dict:
    seeds = jax.random.split(jax.random.key(seed), 9)
    return {
        "density_factor": draw_density_factor(jax.random.fold_in(seeds[8], 71), 0),
        "onsite": gaussian(seeds[1], (NST,), 1.0, 4.0, ((0, 32),), jnp.float32),
        "neighbour_ids": draw_neighbour_ids(jax.random.fold_in(seeds[8], 71), 0),
        "neighbour_count": draw_neighbour_count(jax.random.fold_in(seeds[8], 71), 0),
        "coupling_type": plant(jax.random.randint(seeds[4], (NBLK, KMAX), 0, NT), jax.random.fold_in(seeds[4], 1), 0, NT - 1).astype(jnp.int32),
        "coupling_blocks": gaussian(seeds[5], (NT, BLK, BLK), BLK ** -0.5, 0.25),
        "bath_pattern": plant(jax.random.randint(seeds[6], (NBLK,), 0, NB), jax.random.fold_in(seeds[6], 1), 0, NB - 1).astype(jnp.int32),
        "bath_blocks": gaussian(seeds[7], (NB, BLK, BLK), BLK ** -0.5, 0.25),
    }


time_step = 0.25

def orthonormal_steps(gram):
    basis = jnp.eye(2 * RANK, RANK, dtype=jnp.float32)
    for sweep in range(SWEEPS):
        image = jnp.dot(gram, basis, precision=lax.Precision.HIGHEST)
        inner = jnp.dot(image.T, image, precision=lax.Precision.HIGHEST)
        factor = jnp.linalg.cholesky(inner)
        basis = lax.linalg.triangular_solve(factor, image, left_side=False, lower=True, transpose_a=True)
    return basis

def reference(density_factor, onsite, neighbour_ids, neighbour_count, coupling_type, coupling_blocks, bath_pattern, bath_blocks):
    row_blocks = density_factor.reshape(NBLK, BLK, RANK)
    slot_index = jnp.arange(KMAX, dtype=jnp.int32)
    kind_index = jnp.arange(NT, dtype=jnp.int32)
    coupling_wide = coupling_blocks.astype(jnp.float32)

    def one_block(items):
        ids, count, kinds, bath_kind, own_rows = items
        slot_live = (slot_index < count).astype(jnp.float32)
        weights = (kinds[:, None] == kind_index[None, :]).astype(jnp.float32) * slot_live[:, None]
        fetched = row_blocks[ids].astype(jnp.float32)
        summed = jnp.einsum('kt,kir->tir', weights, fetched).astype(jnp.bfloat16)
        coupled = jnp.einsum('tij,tjr->ir', coupling_wide, summed.astype(jnp.float32))
        bathed = jnp.dot(bath_blocks[bath_kind].astype(jnp.float32), own_rows.astype(jnp.float32), preferred_element_type=jnp.float32).astype(jnp.bfloat16)
        return (coupled, bathed)
    coupled, bathed = lax.map(one_block, (neighbour_ids, neighbour_count, coupling_type, bath_pattern, row_blocks))
    coupled = coupled.reshape(NST, RANK)
    bathed = bathed.reshape(NST, RANK)
    factor_wide = density_factor.astype(jnp.float32)
    moved = (factor_wide - time_step * (onsite[:, None] * factor_wide + coupled)).astype(jnp.bfloat16)
    stacked = jnp.concatenate([moved, bathed], axis=1)
    gram = lax.dot_general(stacked.astype(jnp.float32), stacked.astype(jnp.float32), (((0,), (0,)), ((), ())), preferred_element_type=jnp.float32)
    rotation = orthonormal_steps(gram).astype(jnp.bfloat16)
    return jnp.dot(stacked.astype(jnp.float32), rotation.astype(jnp.float32), preferred_element_type=jnp.float32).astype(jnp.bfloat16)
```

```python
import jax
import jax.numpy as jnp
from jax import lax
from jax.experimental import pallas as pl
from jax.experimental.pallas import tpu as pltpu
from jax.sharding import PartitionSpec as P

SWEEPS = 2
time_step = 0.25
PANEL = 64
HIGHEST = lax.Precision.HIGHEST


def bath_kernel(pattern_ref, bath_ref, own_ref, energy_ref, bathed_ref, base_ref, gram_ref):
    own = own_ref[...]
    bathed = jnp.dot(bath_ref[0], own, preferred_element_type=jnp.float32).astype(jnp.bfloat16)
    bathed_ref[...] = bathed
    wide = own.astype(jnp.float32)
    base_ref[...] = wide - time_step * (energy_ref[...] * wide)
    part = lax.dot_general(
        bathed, bathed, (((0,), (0,)), ((), ())), preferred_element_type=jnp.float32
    )

    @pl.when(pl.program_id(0) == 0)
    def _():
        gram_ref[...] = part

    @pl.when(pl.program_id(0) > 0)
    def _():
        gram_ref[...] += part


def bath_part(own, energy, bath_pattern, bath_blocks):
    blocks = bath_pattern.shape[0]
    block_rows = bath_blocks.shape[1]
    rows, rank = own.shape
    return pl.pallas_call(
        bath_kernel,
        grid_spec=pltpu.PrefetchScalarGridSpec(
            num_scalar_prefetch=1,
            grid=(blocks,),
            in_specs=[
                pl.BlockSpec((1, block_rows, block_rows), lambda b, kind: (kind[b], 0, 0)),
                pl.BlockSpec((block_rows, rank), lambda b, kind: (b, 0)),
                pl.BlockSpec((block_rows, 1), lambda b, kind: (b, 0)),
            ],
            out_specs=[
                pl.BlockSpec((block_rows, rank), lambda b, kind: (b, 0)),
                pl.BlockSpec((block_rows, rank), lambda b, kind: (b, 0)),
                pl.BlockSpec((rank, rank), lambda b, kind: (0, 0)),
            ],
        ),
        out_shape=[
            jax.ShapeDtypeStruct((rows, rank), jnp.bfloat16),
            jax.ShapeDtypeStruct((rows, rank), jnp.float32),
            jax.ShapeDtypeStruct((rank, rank), jnp.float32),
        ],
        compiler_params=pltpu.CompilerParams(vmem_limit_bytes=24 * 2**20),
        name="bath",
    )(bath_pattern, bath_blocks, own, energy)


def couple_kernel(
    ids_ref, count_ref, kind_ref,
    gathered_ref, coupling_ref, base_ref, bathed_ref,
    moved_ref, gram_ref,
    held, total, sems,
):
    blocks, slots = ids_ref.shape
    block_rows = held.shape[2]
    b = pl.program_id(0)

    def copy(block, slot):
        start = pl.multiple_of(ids_ref[block, slot] * block_rows, block_rows)
        return pltpu.make_async_copy(
            gathered_ref.at[pl.ds(start, block_rows), :],
            held.at[lax.rem(block, 2), slot],
            sems.at[lax.rem(block, 2), slot],
        )

    def fetch(block):
        def one(slot, carry):
            copy(block, slot).start()
            return carry

        lax.fori_loop(0, count_ref[block], one, 0)

    @pl.when(b == 0)
    def _():
        fetch(0)

    @pl.when(b + 1 < blocks)
    def _():
        fetch(b + 1)

    def product(slot):
        copy(b, slot).wait()
        return jnp.dot(
            coupling_ref[kind_ref[b, slot]],
            held[lax.rem(b, 2), slot],
            preferred_element_type=jnp.float32,
        )

    total[...] = product(0)

    def add(slot, carry):
        total[...] += product(slot)
        return carry

    lax.fori_loop(1, count_ref[b], add, 0)
    moved = (base_ref[...] - time_step * total[...]).astype(jnp.bfloat16)
    moved_ref[...] = moved
    both = jnp.concatenate([moved, bathed_ref[...]], axis=1)
    part = lax.dot_general(
        moved, both, (((0,), (0,)), ((), ())), preferred_element_type=jnp.float32
    )

    @pl.when(b == 0)
    def _():
        gram_ref[...] = part

    @pl.when(b > 0)
    def _():
        gram_ref[...] += part


def couple_part(ids, count, kind, gathered, coupling_blocks, base, bathed):
    blocks, slots = ids.shape
    kinds, block_rows, _ = coupling_blocks.shape
    rows, rank = base.shape
    return pl.pallas_call(
        couple_kernel,
        grid_spec=pltpu.PrefetchScalarGridSpec(
            num_scalar_prefetch=3,
            grid=(blocks,),
            in_specs=[
                pl.BlockSpec(memory_space=pl.ANY),
                pl.BlockSpec((kinds, block_rows, block_rows), lambda b, *_: (0, 0, 0)),
                pl.BlockSpec((block_rows, rank), lambda b, *_: (b, 0)),
                pl.BlockSpec((block_rows, rank), lambda b, *_: (b, 0)),
            ],
            out_specs=[
                pl.BlockSpec((block_rows, rank), lambda b, *_: (b, 0)),
                pl.BlockSpec((rank, 2 * rank), lambda b, *_: (0, 0)),
            ],
            scratch_shapes=[
                pltpu.VMEM((2, slots, block_rows, rank), jnp.bfloat16),
                pltpu.VMEM((block_rows, rank), jnp.float32),
                pltpu.SemaphoreType.DMA((2, slots)),
            ],
        ),
        out_shape=[
            jax.ShapeDtypeStruct((rows, rank), jnp.bfloat16),
            jax.ShapeDtypeStruct((rank, 2 * rank), jnp.float32),
        ],
        compiler_params=pltpu.CompilerParams(vmem_limit_bytes=40 * 2**20),
        name="couple",
    )(ids, count, kind, gathered, coupling_blocks, base, bathed)


def inverse_factor(square):
    n = square.shape[0]
    eye = (
        lax.broadcasted_iota(jnp.int32, (n, n), 0) == lax.broadcasted_iota(jnp.int32, (n, n), 1)
    ).astype(jnp.float32)
    work = jnp.concatenate([square, eye], axis=1)
    bands = [work[8 * i : 8 * i + 8, :] for i in range(n // 8)]
    sublane = lax.broadcasted_iota(jnp.int32, (8, 2 * n), 0)
    lane = lax.broadcasted_iota(jnp.int32, (8, 2 * n), 1)
    for j in range(n):
        g, r = divmod(j, 8)
        row = bands[g][r : r + 1, :]
        scaled = row / row[:, j : j + 1]
        for i in range(g, n // 8):
            column = bands[i][:, j : j + 1]
            change = column * scaled
            if i == g:
                change = jnp.where(sublane > r, change, 0.0)
            bands[i] = bands[i] - change
    out = []
    for i in range(n // 8):
        pivot = jnp.sum(jnp.where(lane == sublane + 8 * i, bands[i], 0.0), axis=1, keepdims=True)
        out.append(bands[i][:, n:] * lax.rsqrt(pivot))
    return jnp.concatenate(out, axis=0)


def finish_kernel(
    upper_ref, corner_ref, moved_hbm, bathed_hbm, out_hbm,
    gram, work, moved, bathed, out, in_sems, out_sems,
):
    rank = upper_ref.shape[0]
    load_moved = pltpu.make_async_copy(moved_hbm, moved, in_sems.at[0])
    load_bathed = pltpu.make_async_copy(bathed_hbm, bathed, in_sems.at[1])
    load_moved.start()
    load_bathed.start()

    gram[:rank, :] = upper_ref[...]
    gram[rank:, :rank] = upper_ref[:, rank:].T
    gram[rank:, rank:] = corner_ref[...]
    for sweep in range(SWEEPS):
        if sweep == 0:
            image = gram[:rank, :]
        else:
            image = jnp.dot(
                work[:, rank:], gram[...], precision=HIGHEST, preferred_element_type=jnp.float32
            )
        work[:, rank:] = image
        work[:, :rank] = lax.dot_general(
            image, image, (((1,), (1,)), ((), ())),
            precision=HIGHEST, preferred_element_type=jnp.float32,
        )
        for k in range(rank // PANEL):
            low, high = k * PANEL, (k + 1) * PANEL
            inverse = inverse_factor(work[low:high, low:high])
            first = high // 128 * 128
            panel = jnp.dot(
                inverse, work[low:high, first:], precision=HIGHEST, preferred_element_type=jnp.float32
            )
            work[low:high, first:] = panel
            if high < rank:
                work[high:, first:] -= lax.dot_general(
                    panel[:, high - first : rank - first], panel, (((0,), (0,)), ((), ())),
                    precision=HIGHEST, preferred_element_type=jnp.float32,
                )
    rotation = work[:, rank:].astype(jnp.bfloat16)
    load_moved.wait()
    load_bathed.wait()
    pieces = out_sems.shape[0]
    size = moved.shape[0] // pieces

    def store(piece):
        rows = pl.ds(pl.multiple_of(piece * size, size), size)
        return pltpu.make_async_copy(out.at[rows, :], out_hbm.at[rows, :], out_sems.at[piece])

    def one(piece, carry):
        rows = pl.ds(pl.multiple_of(piece * size, size), size)
        value = lax.dot_general(
            moved[rows, :], rotation[:, :rank], (((1,), (1,)), ((), ())),
            preferred_element_type=jnp.float32,
        )
        value += lax.dot_general(
            bathed[rows, :], rotation[:, rank:], (((1,), (1,)), ((), ())),
            preferred_element_type=jnp.float32,
        )
        out[rows, :] = value.astype(jnp.bfloat16)
        store(piece).start()
        return carry

    lax.fori_loop(0, pieces, one, 0)

    def drain(piece, carry):
        store(piece).wait()
        return carry

    lax.fori_loop(0, pieces, drain, 0)


def finish_part(upper, corner, moved, bathed):
    rows, rank = moved.shape
    return pl.pallas_call(
        finish_kernel,
        in_specs=[
            pl.BlockSpec(memory_space=pltpu.VMEM),
            pl.BlockSpec(memory_space=pltpu.VMEM),
            pl.BlockSpec(memory_space=pl.ANY),
            pl.BlockSpec(memory_space=pl.ANY),
        ],
        out_specs=pl.BlockSpec(memory_space=pl.ANY),
        out_shape=jax.ShapeDtypeStruct((rows, rank), jnp.bfloat16),
        scratch_shapes=[
            pltpu.VMEM((2 * rank, 2 * rank), jnp.float32),
            pltpu.VMEM((rank, 3 * rank), jnp.float32),
            pltpu.VMEM((rows, rank), jnp.bfloat16),
            pltpu.VMEM((rows, rank), jnp.bfloat16),
            pltpu.VMEM((rows, rank), jnp.bfloat16),
            pltpu.SemaphoreType.DMA((2,)),
            pltpu.SemaphoreType.DMA((8,)),
        ],
        compiler_params=pltpu.CompilerParams(vmem_limit_bytes=40 * 2**20),
        name="finish",
    )(upper, corner, moved, bathed)


def shards(
    density_factor,
    onsite,
    neighbour_ids,
    neighbour_count,
    coupling_type,
    coupling_blocks,
    bath_pattern,
    bath_blocks,
):
    blocks, slots = neighbour_ids.shape
    group_blocks = lax.axis_size("col") * blocks
    in_group = neighbour_ids - lax.axis_index("row") * group_blocks
    gathered = lax.all_gather(density_factor, "col", axis=0, tiled=True)
    bathed, base, corner = bath_part(
        density_factor, onsite.reshape(-1, 1), bath_pattern, bath_blocks
    )
    moved, upper = couple_part(
        in_group, neighbour_count, coupling_type, gathered, coupling_blocks, base, bathed
    )
    upper, corner = lax.psum((upper, corner), ("row", "col"))
    return finish_part(upper, corner, moved, bathed)


def solution(mesh):
    placed = (
        P(("row", "col"), None),
        P(("row", "col")),
        P(("row", "col"), None),
        P(("row", "col")),
        P(("row", "col"), None),
        P(),
        P(("row", "col")),
        P(),
    )
    return jax.shard_map(
        shards, mesh=mesh, in_specs=placed, out_specs=P(("row", "col"), None), check_vma=False
    )
```

```python
import jax
import jax.numpy as jnp
from jax import lax
from jax.experimental import pallas as pl
from jax.experimental.pallas import tpu as pltpu
from jax.sharding import PartitionSpec as P

SWEEPS = 2
time_step = 0.25
PANEL = 64
HIGHEST = lax.Precision.HIGHEST


def bath_kernel(pattern_ref, bath_ref, own_ref, energy_ref, bathed_ref, base_ref, gram_ref):
    own = own_ref[...]
    bathed = jnp.dot(bath_ref[0], own, preferred_element_type=jnp.float32).astype(jnp.bfloat16)
    bathed_ref[...] = bathed
    wide = own.astype(jnp.float32)
    base_ref[...] = wide - time_step * (energy_ref[...] * wide)
    part = lax.dot_general(
        bathed, bathed, (((0,), (0,)), ((), ())), preferred_element_type=jnp.float32
    )

    @pl.when(pl.program_id(0) == 0)
    def _():
        gram_ref[...] = part

    @pl.when(pl.program_id(0) > 0)
    def _():
        gram_ref[...] += part


def bath_part(own, energy, bath_pattern, bath_blocks):
    blocks = bath_pattern.shape[0]
    block_rows = bath_blocks.shape[1]
    rows, rank = own.shape
    return pl.pallas_call(
        bath_kernel,
        grid_spec=pltpu.PrefetchScalarGridSpec(
            num_scalar_prefetch=1,
            grid=(blocks,),
            in_specs=[
                pl.BlockSpec((1, block_rows, block_rows), lambda b, kind: (kind[b], 0, 0)),
                pl.BlockSpec((block_rows, rank), lambda b, kind: (b, 0)),
                pl.BlockSpec((block_rows, 1), lambda b, kind: (b, 0)),
            ],
            out_specs=[
                pl.BlockSpec((block_rows, rank), lambda b, kind: (b, 0)),
                pl.BlockSpec((block_rows, rank), lambda b, kind: (b, 0)),
                pl.BlockSpec((rank, rank), lambda b, kind: (0, 0)),
            ],
        ),
        out_shape=[
            jax.ShapeDtypeStruct((rows, rank), jnp.bfloat16),
            jax.ShapeDtypeStruct((rows, rank), jnp.float32),
            jax.ShapeDtypeStruct((rank, rank), jnp.float32),
        ],
        compiler_params=pltpu.CompilerParams(vmem_limit_bytes=24 * 2**20),
        name="bath",
    )(bath_pattern, bath_blocks, own, energy)


def couple_kernel(
    origin_ref, offset_ref, count_ref, kind_ref, *refs
):
    sources = refs[:-8]
    coupling_ref, base_ref, bathed_ref, moved_ref, gram_ref, held, total, sems = refs[-8:]
    blocks, slots = origin_ref.shape
    block_rows = held.shape[2]
    b = pl.program_id(0)

    def copy(source, block, slot):
        start = pl.multiple_of(offset_ref[block, slot] * block_rows, block_rows)
        return pltpu.make_async_copy(
            source.at[pl.ds(start, block_rows), :],
            held.at[lax.rem(block, 2), slot],
            sems.at[lax.rem(block, 2), slot],
        )

    def fetch(block):
        def one(slot, carry):
            for place, source in enumerate(sources):
                @pl.when(origin_ref[block, slot] == place)
                def _():
                    copy(source, block, slot).start()
            return carry

        lax.fori_loop(0, count_ref[block], one, 0)

    @pl.when(b == 0)
    def _():
        fetch(0)

    @pl.when(b + 1 < blocks)
    def _():
        fetch(b + 1)

    def product(slot):
        copy(sources[0], b, slot).wait()
        return jnp.dot(
            coupling_ref[kind_ref[b, slot]],
            held[lax.rem(b, 2), slot],
            preferred_element_type=jnp.float32,
        )

    total[...] = product(0)

    def add(slot, carry):
        total[...] += product(slot)
        return carry

    lax.fori_loop(1, count_ref[b], add, 0)
    moved = (base_ref[...] - time_step * total[...]).astype(jnp.bfloat16)
    moved_ref[...] = moved
    both = jnp.concatenate([moved, bathed_ref[...]], axis=1)
    part = lax.dot_general(
        moved, both, (((0,), (0,)), ((), ())), preferred_element_type=jnp.float32
    )

    @pl.when(b == 0)
    def _():
        gram_ref[...] = part

    @pl.when(b > 0)
    def _():
        gram_ref[...] += part


def couple_part(origin, offset, count, kind, sources, coupling_blocks, base, bathed):
    blocks, slots = origin.shape
    kinds, block_rows, _ = coupling_blocks.shape
    rows, rank = base.shape
    return pl.pallas_call(
        couple_kernel,
        grid_spec=pltpu.PrefetchScalarGridSpec(
            num_scalar_prefetch=4,
            grid=(blocks,),
            in_specs=[
                *[pl.BlockSpec(memory_space=pl.ANY) for _ in sources],
                pl.BlockSpec((kinds, block_rows, block_rows), lambda b, *_: (0, 0, 0)),
                pl.BlockSpec((block_rows, rank), lambda b, *_: (b, 0)),
                pl.BlockSpec((block_rows, rank), lambda b, *_: (b, 0)),
            ],
            out_specs=[
                pl.BlockSpec((block_rows, rank), lambda b, *_: (b, 0)),
                pl.BlockSpec((rank, 2 * rank), lambda b, *_: (0, 0)),
            ],
            scratch_shapes=[
                pltpu.VMEM((2, slots, block_rows, rank), jnp.bfloat16),
                pltpu.VMEM((block_rows, rank), jnp.float32),
                pltpu.SemaphoreType.DMA((2, slots)),
            ],
        ),
        out_shape=[
            jax.ShapeDtypeStruct((rows, rank), jnp.bfloat16),
            jax.ShapeDtypeStruct((rank, 2 * rank), jnp.float32),
        ],
        compiler_params=pltpu.CompilerParams(vmem_limit_bytes=40 * 2**20),
        name="couple",
    )(origin, offset, count, kind, *sources, coupling_blocks, base, bathed)


def inverse_factor(square):
    n = square.shape[0]
    eye = (
        lax.broadcasted_iota(jnp.int32, (n, n), 0) == lax.broadcasted_iota(jnp.int32, (n, n), 1)
    ).astype(jnp.float32)
    work = jnp.concatenate([square, eye], axis=1)
    bands = [work[8 * i : 8 * i + 8, :] for i in range(n // 8)]
    sublane = lax.broadcasted_iota(jnp.int32, (8, 2 * n), 0)
    lane = lax.broadcasted_iota(jnp.int32, (8, 2 * n), 1)
    for j in range(n):
        g, r = divmod(j, 8)
        row = bands[g][r : r + 1, :]
        scaled = row / row[:, j : j + 1]
        for i in range(g, n // 8):
            column = bands[i][:, j : j + 1]
            change = column * scaled
            if i == g:
                change = jnp.where(sublane > r, change, 0.0)
            bands[i] = bands[i] - change
    out = []
    for i in range(n // 8):
        pivot = jnp.sum(jnp.where(lane == sublane + 8 * i, bands[i], 0.0), axis=1, keepdims=True)
        out.append(bands[i][:, n:] * lax.rsqrt(pivot))
    return jnp.concatenate(out, axis=0)


def finish_kernel(
    upper_ref, corner_ref, moved_hbm, bathed_hbm, out_hbm,
    gram, work, moved, bathed, out, in_sems, out_sems,
):
    rank = upper_ref.shape[0]
    load_moved = pltpu.make_async_copy(moved_hbm, moved, in_sems.at[0])
    load_bathed = pltpu.make_async_copy(bathed_hbm, bathed, in_sems.at[1])
    load_moved.start()
    load_bathed.start()

    gram[:rank, :] = upper_ref[...]
    gram[rank:, :rank] = upper_ref[:, rank:].T
    gram[rank:, rank:] = corner_ref[...]
    for sweep in range(SWEEPS):
        if sweep == 0:
            image = gram[:rank, :]
        else:
            image = jnp.dot(
                work[:, rank:], gram[...], precision=HIGHEST, preferred_element_type=jnp.float32
            )
        work[:, rank:] = image
        work[:, :rank] = lax.dot_general(
            image, image, (((1,), (1,)), ((), ())),
            precision=HIGHEST, preferred_element_type=jnp.float32,
        )
        for k in range(rank // PANEL):
            low, high = k * PANEL, (k + 1) * PANEL
            inverse = inverse_factor(work[low:high, low:high])
            first = high // 128 * 128
            panel = jnp.dot(
                inverse, work[low:high, first:], precision=HIGHEST, preferred_element_type=jnp.float32
            )
            work[low:high, first:] = panel
            if high < rank:
                work[high:, first:] -= lax.dot_general(
                    panel[:, high - first : rank - first], panel, (((0,), (0,)), ((), ())),
                    precision=HIGHEST, preferred_element_type=jnp.float32,
                )
    rotation = work[:, rank:].astype(jnp.bfloat16)
    load_moved.wait()
    load_bathed.wait()
    pieces = out_sems.shape[0]
    size = moved.shape[0] // pieces

    def store(piece):
        rows = pl.ds(pl.multiple_of(piece * size, size), size)
        return pltpu.make_async_copy(out.at[rows, :], out_hbm.at[rows, :], out_sems.at[piece])

    def one(piece, carry):
        rows = pl.ds(pl.multiple_of(piece * size, size), size)
        value = lax.dot_general(
            moved[rows, :], rotation[:, :rank], (((1,), (1,)), ((), ())),
            preferred_element_type=jnp.float32,
        )
        value += lax.dot_general(
            bathed[rows, :], rotation[:, rank:], (((1,), (1,)), ((), ())),
            preferred_element_type=jnp.float32,
        )
        out[rows, :] = value.astype(jnp.bfloat16)
        store(piece).start()
        return carry

    lax.fori_loop(0, pieces, one, 0)

    def drain(piece, carry):
        store(piece).wait()
        return carry

    lax.fori_loop(0, pieces, drain, 0)


def finish_part(upper, corner, moved, bathed):
    rows, rank = moved.shape
    return pl.pallas_call(
        finish_kernel,
        in_specs=[
            pl.BlockSpec(memory_space=pltpu.VMEM),
            pl.BlockSpec(memory_space=pltpu.VMEM),
            pl.BlockSpec(memory_space=pl.ANY),
            pl.BlockSpec(memory_space=pl.ANY),
        ],
        out_specs=pl.BlockSpec(memory_space=pl.ANY),
        out_shape=jax.ShapeDtypeStruct((rows, rank), jnp.bfloat16),
        scratch_shapes=[
            pltpu.VMEM((2 * rank, 2 * rank), jnp.float32),
            pltpu.VMEM((rank, 3 * rank), jnp.float32),
            pltpu.VMEM((rows, rank), jnp.bfloat16),
            pltpu.VMEM((rows, rank), jnp.bfloat16),
            pltpu.VMEM((rows, rank), jnp.bfloat16),
            pltpu.SemaphoreType.DMA((2,)),
            pltpu.SemaphoreType.DMA((8,)),
        ],
        compiler_params=pltpu.CompilerParams(vmem_limit_bytes=40 * 2**20),
        name="finish",
    )(upper, corner, moved, bathed)


def ring_order(count):
    wide = 2
    while 4 * wide * wide <= count:
        wide *= 2
    tall = count // wide
    walk = [0]
    for r in range(tall):
        across = range(1, wide)
        walk += [r * wide + c for c in (across if r % 2 == 0 else reversed(across))]
    return walk + [r * wide for r in range(tall - 1, 0, -1)]


def ring_gather(own):
    order = ring_order(lax.axis_size("col"))
    following = order[1:] + order[:1]
    forward = list(zip(order, following))
    back = list(zip(following, order))
    half = own.shape[0] // 2
    ahead, behind = own[:half], own[half:]
    first, second = [], []
    for _ in order[1:]:
        ahead = lax.ppermute(ahead, "col", forward)
        behind = lax.ppermute(behind, "col", back)
        first.append(ahead)
        second.append(behind)
    return [own] + first + second


def ring_place(ids, blocks):
    count = lax.axis_size("col")
    order = ring_order(count)
    place = jnp.asarray([order.index(c) for c in range(count)], jnp.int32)
    mine = place[lax.axis_index("col")]
    owner, within = ids // blocks, ids % blocks
    theirs = jnp.sum(
        jnp.where(owner[..., None] == jnp.arange(count, dtype=jnp.int32), place, 0), axis=-1
    )
    second = within >= blocks // 2
    step = jnp.where(second, theirs - mine, mine - theirs) % count
    origin = jnp.where(step == 0, 0, step + jnp.where(second, count - 1, 0))
    offset = jnp.where((step > 0) & second, within - blocks // 2, within)
    return origin, offset


def swap(value, axis, stride):
    count = lax.axis_size(axis)
    return lax.ppermute(value, axis, [(i, i ^ stride) for i in range(count)])


def sum_everywhere(value):
    place = lax.axis_index("row")
    strides = []
    stride = 1
    while stride < lax.axis_size("row"):
        strides.append(stride)
        stride *= 2
    for stride in strides:
        half = value.shape[0] // 2
        upper = (place // stride) % 2
        keep = lax.dynamic_slice_in_dim(value, upper * half, half, 0)
        give = lax.dynamic_slice_in_dim(value, (1 - upper) * half, half, 0)
        value = keep + swap(give, "row", stride)
    stride = 1
    while stride < lax.axis_size("col"):
        value = value + swap(value, "col", stride)
        stride *= 2
    for stride in reversed(strides):
        upper = (place // stride) % 2
        other = swap(value, "row", stride)
        value = jnp.where(
            upper == 0,
            jnp.concatenate([value, other], axis=0),
            jnp.concatenate([other, value], axis=0),
        )
    return value


def shards(
    density_factor,
    onsite,
    neighbour_ids,
    neighbour_count,
    coupling_type,
    coupling_blocks,
    bath_pattern,
    bath_blocks,
):
    blocks, slots = neighbour_ids.shape
    group_blocks = lax.axis_size("col") * blocks
    in_group = neighbour_ids - lax.axis_index("row") * group_blocks
    sources = ring_gather(density_factor)
    origin, offset = ring_place(in_group, blocks)
    bathed, base, corner = bath_part(
        density_factor, onsite.reshape(-1, 1), bath_pattern, bath_blocks
    )
    corner = lax.psum(corner, ("row", "col"))
    moved, upper = couple_part(
        origin, offset, neighbour_count, coupling_type, sources, coupling_blocks, base, bathed
    )
    upper = sum_everywhere(upper)
    return finish_part(upper, corner, moved, bathed)


def solution(mesh):
    placed = (
        P(("row", "col"), None),
        P(("row", "col")),
        P(("row", "col"), None),
        P(("row", "col")),
        P(("row", "col"), None),
        P(),
        P(("row", "col")),
        P(),
    )
    return jax.shard_map(
        shards, mesh=mesh, in_specs=placed, out_specs=P(("row", "col"), None), check_vma=False
    )
```

```python
import jax
import jax.numpy as jnp
from jax import lax
from jax.experimental import pallas as pl
from jax.experimental.pallas import tpu as pltpu
from jax.sharding import PartitionSpec as P

SWEEPS = 2
time_step = 0.25
PANEL = 64
HIGHEST = lax.Precision.HIGHEST


def bath_kernel(pattern_ref, bath_ref, own_ref, energy_ref, bathed_ref, base_ref, gram_ref):
    own = own_ref[...]
    bathed = jnp.dot(bath_ref[0], own, preferred_element_type=jnp.float32).astype(jnp.bfloat16)
    bathed_ref[...] = bathed
    wide = own.astype(jnp.float32)
    base_ref[...] = wide - time_step * (energy_ref[...] * wide)
    part = lax.dot_general(
        bathed, bathed, (((0,), (0,)), ((), ())), preferred_element_type=jnp.float32
    )

    @pl.when(pl.program_id(0) == 0)
    def _():
        gram_ref[...] = part

    @pl.when(pl.program_id(0) > 0)
    def _():
        gram_ref[...] += part


def bath_part(own, energy, bath_pattern, bath_blocks):
    blocks = bath_pattern.shape[0]
    block_rows = bath_blocks.shape[1]
    rows, rank = own.shape
    return pl.pallas_call(
        bath_kernel,
        grid_spec=pltpu.PrefetchScalarGridSpec(
            num_scalar_prefetch=1,
            grid=(blocks,),
            in_specs=[
                pl.BlockSpec((1, block_rows, block_rows), lambda b, kind: (kind[b], 0, 0)),
                pl.BlockSpec((block_rows, rank), lambda b, kind: (b, 0)),
                pl.BlockSpec((block_rows, 1), lambda b, kind: (b, 0)),
            ],
            out_specs=[
                pl.BlockSpec((block_rows, rank), lambda b, kind: (b, 0)),
                pl.BlockSpec((block_rows, rank), lambda b, kind: (b, 0)),
                pl.BlockSpec((rank, rank), lambda b, kind: (0, 0)),
            ],
        ),
        out_shape=[
            jax.ShapeDtypeStruct((rows, rank), jnp.bfloat16),
            jax.ShapeDtypeStruct((rows, rank), jnp.float32),
            jax.ShapeDtypeStruct((rank, rank), jnp.float32),
        ],
        compiler_params=pltpu.CompilerParams(vmem_limit_bytes=16 * 2**20),
        name="bath",
    )(bath_pattern, bath_blocks, own, energy)


def gather_products(origin_ref, offset_ref, first_ref, count_ref, kind_ref, sources, coupling_ref, held, sems, total):
    blocks, slots = origin_ref.shape
    block_rows = held.shape[2]
    b = pl.program_id(0)
    group = 1
    while group * group < len(sources):
        group += 1

    def copy(source, block, slot):
        start = pl.multiple_of(offset_ref[block, slot] * block_rows, block_rows)
        return pltpu.make_async_copy(
            source.at[pl.ds(start, block_rows), :],
            held.at[lax.rem(block, 2), slot],
            sems.at[lax.rem(block, 2), slot],
        )

    def fetch(block):
        def one(slot, carry):
            origin = origin_ref[block, slot]
            for low in range(0, len(sources), group):
                high = min(low + group, len(sources))

                @pl.when((origin >= low) & (origin < high))
                def _():
                    for place in range(low, high):
                        @pl.when(origin == place)
                        def _():
                            copy(sources[place], block, slot).start()
            return carry

        lax.fori_loop(first_ref[block], first_ref[block] + count_ref[block], one, 0)

    @pl.when(b == 0)
    def _():
        fetch(0)

    @pl.when(b + 1 < blocks)
    def _():
        fetch(b + 1)

    def add(slot, carry):
        copy(sources[0], b, slot).wait()
        total[...] -= time_step * jnp.dot(
            coupling_ref[kind_ref[b, slot]],
            held[lax.rem(b, 2), slot],
            preferred_element_type=jnp.float32,
        )
        return carry

    lax.fori_loop(first_ref[b], first_ref[b] + count_ref[b], add, 0)


def early_kernel(origin_ref, offset_ref, first_ref, count_ref, kind_ref, *refs):
    sources = refs[:-5]
    coupling_ref, base_ref, total_ref, held, sems = refs[-5:]
    total_ref[...] = base_ref[...]
    gather_products(
        origin_ref, offset_ref, first_ref, count_ref, kind_ref, sources, coupling_ref, held, sems, total_ref
    )


def late_kernel(origin_ref, offset_ref, first_ref, count_ref, kind_ref, *refs):
    sources = refs[:-8]
    coupling_ref, base_ref, bathed_ref, moved_ref, gram_ref, total, held, sems = refs[-8:]
    b = pl.program_id(0)
    total[...] = base_ref[...]
    gather_products(
        origin_ref, offset_ref, first_ref, count_ref, kind_ref, sources, coupling_ref, held, sems, total
    )
    moved = total[...].astype(jnp.bfloat16)
    moved_ref[...] = moved
    both = jnp.concatenate([moved, bathed_ref[...]], axis=1)
    part = lax.dot_general(
        moved, both, (((0,), (0,)), ((), ())), preferred_element_type=jnp.float32
    )

    @pl.when(b == 0)
    def _():
        gram_ref[...] = part

    @pl.when(b > 0)
    def _():
        gram_ref[...] += part


def early_part(lists, sources, coupling_blocks, base):
    blocks, slots = lists[0].shape
    kinds, block_rows, _ = coupling_blocks.shape
    rows, rank = base.shape
    tile = pl.BlockSpec((block_rows, rank), lambda b, *_: (b, 0))
    return pl.pallas_call(
        early_kernel,
        grid_spec=pltpu.PrefetchScalarGridSpec(
            num_scalar_prefetch=5,
            grid=(blocks,),
            in_specs=[
                *[pl.BlockSpec(memory_space=pl.ANY) for _ in sources],
                pl.BlockSpec((kinds, block_rows, block_rows), lambda b, *_: (0, 0, 0)),
                tile,
            ],
            out_specs=tile,
            scratch_shapes=[
                pltpu.VMEM((2, slots, block_rows, rank), jnp.bfloat16),
                pltpu.SemaphoreType.DMA((2, slots)),
            ],
        ),
        out_shape=jax.ShapeDtypeStruct((rows, rank), jnp.float32),
        compiler_params=pltpu.CompilerParams(vmem_limit_bytes=16 * 2**20),
        cost_estimate=pl.CostEstimate(
            flops=blocks * slots * block_rows * block_rows * rank,
            bytes_accessed=blocks * slots * block_rows * rank * 2,
            transcendentals=0,
        ),
        name="couple_early",
    )(*lists, *sources, coupling_blocks, base)


def late_part(lists, sources, coupling_blocks, base, bathed):
    blocks, slots = lists[0].shape
    kinds, block_rows, _ = coupling_blocks.shape
    rows, rank = base.shape
    tile = pl.BlockSpec((block_rows, rank), lambda b, *_: (b, 0))
    return pl.pallas_call(
        late_kernel,
        grid_spec=pltpu.PrefetchScalarGridSpec(
            num_scalar_prefetch=5,
            grid=(blocks,),
            in_specs=[
                *[pl.BlockSpec(memory_space=pl.ANY) for _ in sources],
                pl.BlockSpec((kinds, block_rows, block_rows), lambda b, *_: (0, 0, 0)),
                tile,
                tile,
            ],
            out_specs=[tile, pl.BlockSpec((rank, 2 * rank), lambda b, *_: (0, 0))],
            scratch_shapes=[
                pltpu.VMEM((block_rows, rank), jnp.float32),
                pltpu.VMEM((2, slots, block_rows, rank), jnp.bfloat16),
                pltpu.SemaphoreType.DMA((2, slots)),
            ],
        ),
        out_shape=[
            jax.ShapeDtypeStruct((rows, rank), jnp.bfloat16),
            jax.ShapeDtypeStruct((rank, 2 * rank), jnp.float32),
        ],
        compiler_params=pltpu.CompilerParams(vmem_limit_bytes=20 * 2**20),
        name="couple_late",
    )(*lists, *sources, coupling_blocks, base, bathed)


def inverse_factor(square):
    n = square.shape[0]
    eye = (
        lax.broadcasted_iota(jnp.int32, (n, n), 0) == lax.broadcasted_iota(jnp.int32, (n, n), 1)
    ).astype(jnp.float32)
    work = jnp.concatenate([square, eye], axis=1)
    bands = [work[8 * i : 8 * i + 8, :] for i in range(n // 8)]
    sublane = lax.broadcasted_iota(jnp.int32, (8, 2 * n), 0)
    out = []
    for g in range(n // 8):
        below = range(g, n // 8)
        columns = {
            i: [jnp.broadcast_to(bands[i][:, 8 * g + r : 8 * g + r + 1], (8, 2 * n)) for r in range(8)]
            for i in below
        }
        diagonal = jnp.zeros((8, 2 * n), jnp.float32)
        for r in range(8):
            pivots = [columns[g][q][r : r + 1, :] for q in range(r, 8)]
            scale = 1.0 / pivots[0]
            diagonal = jnp.where(sublane == r, columns[g][r], diagonal)
            row = bands[g][r : r + 1, :]
            for i in below:
                share = columns[i][r] * scale
                if i == g:
                    share = jnp.where(sublane > r, share, 0.0)
                for q in range(r + 1, 8):
                    columns[i][q] = columns[i][q] - share * pivots[q - r]
                bands[i] = bands[i] - share * row
        out.append(bands[g][:, n:] * lax.rsqrt(diagonal)[:, n:])
    return jnp.concatenate(out, axis=0)


def finish_kernel(
    upper_ref, corner_ref, moved_hbm, bathed_hbm, out_hbm,
    gram, work, moved, bathed, out, in_sems, out_sems,
):
    rank = upper_ref.shape[0]
    load_moved = pltpu.make_async_copy(moved_hbm, moved, in_sems.at[0])
    load_bathed = pltpu.make_async_copy(bathed_hbm, bathed, in_sems.at[1])
    load_moved.start()
    load_bathed.start()

    gram[:rank, :] = upper_ref[...]
    gram[rank:, :rank] = upper_ref[:, rank:].T
    gram[rank:, rank:] = corner_ref[...]
    for sweep in range(SWEEPS):
        if sweep == 0:
            image = gram[:rank, :]
        else:
            image = jnp.dot(
                work[:, rank:], gram[...], precision=HIGHEST, preferred_element_type=jnp.float32
            )
        work[:, rank:] = image
        work[:, :rank] = lax.dot_general(
            image, image, (((1,), (1,)), ((), ())),
            precision=HIGHEST, preferred_element_type=jnp.float32,
        )
        for k in range(rank // PANEL):
            low, high = k * PANEL, (k + 1) * PANEL
            inverse = inverse_factor(work[low:high, low:high])
            first = high // 128 * 128
            panel = jnp.dot(
                inverse, work[low:high, first:], precision=HIGHEST, preferred_element_type=jnp.float32
            )
            work[low:high, first:] = panel
            if high < rank:
                work[high:, first:] -= lax.dot_general(
                    panel[:, high - first : rank - first], panel, (((0,), (0,)), ((), ())),
                    precision=HIGHEST, preferred_element_type=jnp.float32,
                )
    rotation = work[:, rank:].astype(jnp.bfloat16)
    load_moved.wait()
    load_bathed.wait()
    pieces = out_sems.shape[0]
    size = moved.shape[0] // pieces

    def store(piece):
        rows = pl.ds(pl.multiple_of(piece * size, size), size)
        return pltpu.make_async_copy(out.at[rows, :], out_hbm.at[rows, :], out_sems.at[piece])

    def one(piece, carry):
        rows = pl.ds(pl.multiple_of(piece * size, size), size)
        value = lax.dot_general(
            moved[rows, :], rotation[:, :rank], (((1,), (1,)), ((), ())),
            preferred_element_type=jnp.float32,
        )
        value += lax.dot_general(
            bathed[rows, :], rotation[:, rank:], (((1,), (1,)), ((), ())),
            preferred_element_type=jnp.float32,
        )
        out[rows, :] = value.astype(jnp.bfloat16)
        store(piece).start()
        return carry

    lax.fori_loop(0, pieces, one, 0)

    def drain(piece, carry):
        store(piece).wait()
        return carry

    lax.fori_loop(0, pieces, drain, 0)


def finish_part(upper, corner, moved, bathed):
    rows, rank = moved.shape
    return pl.pallas_call(
        finish_kernel,
        in_specs=[
            pl.BlockSpec(memory_space=pltpu.VMEM),
            pl.BlockSpec(memory_space=pltpu.VMEM),
            pl.BlockSpec(memory_space=pl.ANY),
            pl.BlockSpec(memory_space=pl.ANY),
        ],
        out_specs=pl.BlockSpec(memory_space=pl.ANY),
        out_shape=jax.ShapeDtypeStruct((rows, rank), jnp.bfloat16),
        scratch_shapes=[
            pltpu.VMEM((2 * rank, 2 * rank), jnp.float32),
            pltpu.VMEM((rank, 3 * rank), jnp.float32),
            pltpu.VMEM((rows, rank), jnp.bfloat16),
            pltpu.VMEM((rows, rank), jnp.bfloat16),
            pltpu.VMEM((rows, rank), jnp.bfloat16),
            pltpu.SemaphoreType.DMA((2,)),
            pltpu.SemaphoreType.DMA((8,)),
        ],
        compiler_params=pltpu.CompilerParams(vmem_limit_bytes=24 * 2**20),
        name="finish",
    )(upper, corner, moved, bathed)


def ring_order(count):
    wide = 2
    while 4 * wide * wide <= count:
        wide *= 2
    tall = count // wide
    walk = [0]
    for r in range(tall):
        across = range(1, wide)
        walk += [r * wide + c for c in (across if r % 2 == 0 else reversed(across))]
    return walk + [r * wide for r in range(tall - 1, 0, -1)]


PIECES = 4


def tie(one, other):
    return lax.optimization_barrier((one, other))


def ring_gather(own, side, stages):
    order = ring_order(lax.axis_size("col"))
    following = order[1:] + order[:1]
    forward = list(zip(order, following))
    back = list(zip(following, order))
    size = own.shape[0] // PIECES
    pieces = [own[i * size : (i + 1) * size] for i in range(PIECES)]
    stages = list(stages)
    steps = []
    for step in range(1, len(order)):
        if step > 1 and side is not None:
            pieces[0], side = tie(pieces[0], side)
        pieces = [
            lax.ppermute(piece, "col", forward if i < PIECES // 2 else back)
            for i, piece in enumerate(pieces)
        ]
        if step > 1:
            for _ in range(2):
                if stages:
                    side = stages.pop(0)(side)
        steps.append(list(pieces))
    for stage in stages:
        side = stage(side)
    return steps, side


def slot_lists(ids, counts, kinds):
    blocks, slots = ids.shape
    count = lax.axis_size("col")
    order = ring_order(count)
    place = jnp.asarray([order.index(c) for c in range(count)], jnp.int32)
    col = jnp.arange(count, dtype=jnp.int32)
    mine = jnp.sum(jnp.where(col == lax.axis_index("col"), place, 0))
    owner, within = ids // blocks, ids % blocks
    theirs = jnp.sum(jnp.where(owner[..., None] == col, place, 0), axis=-1)
    in_piece = blocks // PIECES
    piece = within // in_piece
    step = jnp.where(piece >= PIECES // 2, theirs - mine, mine - theirs) % count
    last = step == count - 1
    origin = jnp.where(last, piece, jnp.where(step == 0, 0, 1 + (step - 1) * PIECES + piece))
    offset = jnp.where(step == 0, within, within % in_piece)
    slot = jnp.arange(slots, dtype=jnp.int32)
    used = slot[None, :] < counts[:, None]
    key = jnp.where(used, jnp.where(last, slots, 0), 2 * slots) + slot
    rank = jnp.sum((key[:, None, :] < key[:, :, None]).astype(jnp.int32), axis=-1)
    at = rank[:, :, None] == slot
    def arrange(values):
        return jnp.sum(jnp.where(at, values[:, :, None], 0), axis=1)

    late = jnp.sum((used & last).astype(jnp.int32), axis=1)
    early = counts - late
    origin, offset, kinds = arrange(origin), arrange(offset), arrange(kinds)
    return (origin, offset, jnp.zeros_like(early), early, kinds), (origin, offset, early, late, kinds)


def swap(value, axis, stride):
    count = lax.axis_size(axis)
    return lax.ppermute(value, axis, [(i, i ^ stride) for i in range(count)])


def sum_stages():
    place = lax.axis_index("row")

    def halve(stride):
        def step(value):
            half = value.shape[0] // 2
            upper = (place // stride) % 2
            keep = lax.dynamic_slice_in_dim(value, upper * half, half, 0)
            give = lax.dynamic_slice_in_dim(value, (1 - upper) * half, half, 0)
            return keep + swap(give, "row", stride)

        return step

    def exchange(stride):
        return lambda value: value + swap(value, "col", stride)

    def double(stride):
        def step(value):
            upper = (place // stride) % 2
            other = swap(value, "row", stride)
            return jnp.where(
                upper == 0,
                jnp.concatenate([value, other], axis=0),
                jnp.concatenate([other, value], axis=0),
            )

        return step

    row_strides = [1 << i for i in range(lax.axis_size("row").bit_length() - 1)]
    col_strides = [1 << i for i in range(lax.axis_size("col").bit_length() - 1)]
    return (
        [halve(stride) for stride in row_strides]
        + [exchange(stride) for stride in col_strides]
        + [double(stride) for stride in reversed(row_strides)]
    )


def shards(
    density_factor,
    onsite,
    neighbour_ids,
    neighbour_count,
    coupling_type,
    coupling_blocks,
    bath_pattern,
    bath_blocks,
):
    blocks, slots = neighbour_ids.shape
    group_blocks = lax.axis_size("col") * blocks
    in_group = neighbour_ids - lax.axis_index("row") * group_blocks
    early, late = slot_lists(in_group, neighbour_count, coupling_type)
    bathed, base, corner = bath_part(
        density_factor, onsite.reshape(-1, 1), bath_pattern, bath_blocks
    )
    steps, corner = ring_gather(density_factor, corner, sum_stages())
    ready = [density_factor] + [piece for step in steps[:-1] for piece in step]
    total = early_part(early, ready, coupling_blocks, base)
    moved, upper = late_part(late, steps[-1], coupling_blocks, total, bathed)
    for stage in sum_stages():
        upper = stage(upper)
    return finish_part(upper, corner, moved, bathed)


def solution(mesh):
    placed = (
        P(("row", "col"), None),
        P(("row", "col")),
        P(("row", "col"), None),
        P(("row", "col")),
        P(("row", "col"), None),
        P(),
        P(("row", "col")),
        P(),
    )
    return jax.shard_map(
        shards, mesh=mesh, in_specs=placed, out_specs=P(("row", "col"), None), check_vma=False
    )
```

```python
import jax
import jax.numpy as jnp
from jax import lax
from jax.experimental import pallas as pl
from jax.experimental.pallas import tpu as pltpu
from jax.sharding import PartitionSpec as P

SWEEPS = 2
time_step = 0.25
PANEL = 64
HIGHEST = lax.Precision.HIGHEST


def bath_kernel(pattern_ref, bath_ref, own_ref, energy_ref, bathed_ref, base_ref, gram_ref):
    own = own_ref[...]
    bathed = jnp.dot(bath_ref[0], own, preferred_element_type=jnp.float32).astype(jnp.bfloat16)
    bathed_ref[...] = bathed
    wide = own.astype(jnp.float32)
    base_ref[...] = wide - time_step * (energy_ref[...] * wide)
    part = lax.dot_general(
        bathed, bathed, (((0,), (0,)), ((), ())), preferred_element_type=jnp.float32
    )

    @pl.when(pl.program_id(0) == 0)
    def _():
        gram_ref[...] = part

    @pl.when(pl.program_id(0) > 0)
    def _():
        gram_ref[...] += part


def bath_part(own, energy, bath_pattern, bath_blocks):
    blocks = bath_pattern.shape[0]
    block_rows = bath_blocks.shape[1]
    rows, rank = own.shape
    return pl.pallas_call(
        bath_kernel,
        grid_spec=pltpu.PrefetchScalarGridSpec(
            num_scalar_prefetch=1,
            grid=(blocks,),
            in_specs=[
                pl.BlockSpec((1, block_rows, block_rows), lambda b, kind: (kind[b], 0, 0)),
                pl.BlockSpec((block_rows, rank), lambda b, kind: (b, 0)),
                pl.BlockSpec((block_rows, 1), lambda b, kind: (b, 0)),
            ],
            out_specs=[
                pl.BlockSpec((block_rows, rank), lambda b, kind: (b, 0)),
                pl.BlockSpec((block_rows, rank), lambda b, kind: (b, 0)),
                pl.BlockSpec((rank, rank), lambda b, kind: (0, 0)),
            ],
        ),
        out_shape=[
            jax.ShapeDtypeStruct((rows, rank), jnp.bfloat16),
            jax.ShapeDtypeStruct((rows, rank), jnp.float32),
            jax.ShapeDtypeStruct((rank, rank), jnp.float32),
        ],
        compiler_params=pltpu.CompilerParams(vmem_limit_bytes=16 * 2**20),
        name="bath",
    )(bath_pattern, bath_blocks, own, energy)


def gather_products(origin_ref, offset_ref, first_ref, count_ref, kind_ref, sources, coupling_ref, held, sems, total):
    blocks, slots = origin_ref.shape
    block_rows = held.shape[2]
    b = pl.program_id(0)
    group = 1
    while group * group < len(sources):
        group += 1

    def copy(source, block, slot):
        start = pl.multiple_of(offset_ref[block, slot] * block_rows, block_rows)
        return pltpu.make_async_copy(
            source.at[pl.ds(start, block_rows), :],
            held.at[lax.rem(block, 2), slot],
            sems.at[lax.rem(block, 2), slot],
        )

    def fetch(block):
        def one(slot, carry):
            origin = origin_ref[block, slot]
            for low in range(0, len(sources), group):
                high = min(low + group, len(sources))

                @pl.when((origin >= low) & (origin < high))
                def _():
                    for place in range(low, high):
                        @pl.when(origin == place)
                        def _():
                            copy(sources[place], block, slot).start()
            return carry

        lax.fori_loop(first_ref[block], first_ref[block] + count_ref[block], one, 0)

    @pl.when(b == 0)
    def _():
        fetch(0)

    @pl.when(b + 1 < blocks)
    def _():
        fetch(b + 1)

    def add(slot, carry):
        copy(sources[0], b, slot).wait()
        total[...] -= time_step * jnp.dot(
            coupling_ref[kind_ref[b, slot]],
            held[lax.rem(b, 2), slot],
            preferred_element_type=jnp.float32,
        )
        return carry

    lax.fori_loop(first_ref[b], first_ref[b] + count_ref[b], add, 0)


def early_kernel(origin_ref, offset_ref, first_ref, count_ref, kind_ref, *refs):
    sources = refs[:-5]
    coupling_ref, base_ref, total_ref, held, sems = refs[-5:]
    total_ref[...] = base_ref[...]
    gather_products(
        origin_ref, offset_ref, first_ref, count_ref, kind_ref, sources, coupling_ref, held, sems, total_ref
    )


def late_kernel(origin_ref, offset_ref, first_ref, count_ref, kind_ref, *refs):
    sources = refs[:-8]
    coupling_ref, base_ref, bathed_ref, moved_ref, gram_ref, total, held, sems = refs[-8:]
    b = pl.program_id(0)
    total[...] = base_ref[...]
    gather_products(
        origin_ref, offset_ref, first_ref, count_ref, kind_ref, sources, coupling_ref, held, sems, total
    )
    moved = total[...].astype(jnp.bfloat16)
    moved_ref[...] = moved
    both = jnp.concatenate([moved, bathed_ref[...]], axis=1)
    part = lax.dot_general(
        moved, both, (((0,), (0,)), ((), ())), preferred_element_type=jnp.float32
    )

    @pl.when(b == 0)
    def _():
        gram_ref[...] = part

    @pl.when(b > 0)
    def _():
        gram_ref[...] += part


def early_part(lists, sources, coupling_blocks, base):
    blocks, slots = lists[0].shape
    kinds, block_rows, _ = coupling_blocks.shape
    rows, rank = base.shape
    tile = pl.BlockSpec((block_rows, rank), lambda b, *_: (b, 0))
    return pl.pallas_call(
        early_kernel,
        grid_spec=pltpu.PrefetchScalarGridSpec(
            num_scalar_prefetch=5,
            grid=(blocks,),
            in_specs=[
                *[pl.BlockSpec(memory_space=pl.ANY) for _ in sources],
                pl.BlockSpec((kinds, block_rows, block_rows), lambda b, *_: (0, 0, 0)),
                tile,
            ],
            out_specs=tile,
            scratch_shapes=[
                pltpu.VMEM((2, slots, block_rows, rank), jnp.bfloat16),
                pltpu.SemaphoreType.DMA((2, slots)),
            ],
        ),
        out_shape=jax.ShapeDtypeStruct((rows, rank), jnp.float32),
        compiler_params=pltpu.CompilerParams(vmem_limit_bytes=16 * 2**20),
        cost_estimate=pl.CostEstimate(
            flops=blocks * slots * block_rows * block_rows * rank,
            bytes_accessed=blocks * slots * block_rows * rank * 2,
            transcendentals=0,
        ),
        name="couple_early",
    )(*lists, *sources, coupling_blocks, base)


def late_part(lists, sources, coupling_blocks, base, bathed):
    blocks, slots = lists[0].shape
    kinds, block_rows, _ = coupling_blocks.shape
    rows, rank = base.shape
    tile = pl.BlockSpec((block_rows, rank), lambda b, *_: (b, 0))
    return pl.pallas_call(
        late_kernel,
        grid_spec=pltpu.PrefetchScalarGridSpec(
            num_scalar_prefetch=5,
            grid=(blocks,),
            in_specs=[
                *[pl.BlockSpec(memory_space=pl.ANY) for _ in sources],
                pl.BlockSpec((kinds, block_rows, block_rows), lambda b, *_: (0, 0, 0)),
                tile,
                tile,
            ],
            out_specs=[tile, pl.BlockSpec((rank, 2 * rank), lambda b, *_: (0, 0))],
            scratch_shapes=[
                pltpu.VMEM((block_rows, rank), jnp.float32),
                pltpu.VMEM((2, slots, block_rows, rank), jnp.bfloat16),
                pltpu.SemaphoreType.DMA((2, slots)),
            ],
        ),
        out_shape=[
            jax.ShapeDtypeStruct((rows, rank), jnp.bfloat16),
            jax.ShapeDtypeStruct((rank, 2 * rank), jnp.float32),
        ],
        compiler_params=pltpu.CompilerParams(vmem_limit_bytes=20 * 2**20),
        name="couple_late",
    )(*lists, *sources, coupling_blocks, base, bathed)


def inverse_factor(square):
    n = square.shape[0]
    eye = (
        lax.broadcasted_iota(jnp.int32, (n, n), 0) == lax.broadcasted_iota(jnp.int32, (n, n), 1)
    ).astype(jnp.float32)
    work = jnp.concatenate([square, eye], axis=1)
    bands = [work[8 * i : 8 * i + 8, :] for i in range(n // 8)]
    sublane = lax.broadcasted_iota(jnp.int32, (8, 2 * n), 0)
    out = []
    for g in range(n // 8):
        below = range(g, n // 8)
        columns = {
            i: [jnp.broadcast_to(bands[i][:, 8 * g + r : 8 * g + r + 1], (8, 2 * n)) for r in range(8)]
            for i in below
        }
        diagonal = jnp.zeros((8, 2 * n), jnp.float32)
        for r in range(8):
            pivots = [columns[g][q][r : r + 1, :] for q in range(r, 8)]
            scale = 1.0 / pivots[0]
            diagonal = jnp.where(sublane == r, columns[g][r], diagonal)
            row = bands[g][r : r + 1, :]
            for i in below:
                share = columns[i][r] * scale
                if i == g:
                    share = jnp.where(sublane > r, share, 0.0)
                for q in range(r + 1, 8):
                    columns[i][q] = columns[i][q] - share * pivots[q - r]
                bands[i] = bands[i] - share * row
        out.append(bands[g][:, n:] * lax.rsqrt(diagonal)[:, n:])
    return jnp.concatenate(out, axis=0)


def finish_kernel(
    order_ref, chunks_ref, moved_hbm, bathed_hbm, out_hbm,
    gram, work, moved, bathed, out, in_sems, out_sems,
):
    rank = chunks_ref.shape[0]
    load_moved = pltpu.make_async_copy(moved_hbm, moved, in_sems.at[0])
    load_bathed = pltpu.make_async_copy(bathed_hbm, bathed, in_sems.at[1])
    load_moved.start()
    load_bathed.start()

    chunks = order_ref.shape[0]
    size = rank // chunks
    for i in range(chunks):
        rows = pl.ds(pl.multiple_of(order_ref[i] * size, size), size)
        chunk = chunks_ref[i * size : (i + 1) * size, :]
        gram[rows, :] = chunk[:, : 2 * rank]
        gram[pl.ds(pl.multiple_of(rank + order_ref[i] * size, size), size), rank:] = chunk[:, 2 * rank :]
    gram[rank:, :rank] = gram[:rank, rank:].T
    for sweep in range(SWEEPS):
        if sweep == 0:
            image = gram[:rank, :]
        else:
            image = jnp.dot(
                work[:, rank:], gram[...], precision=HIGHEST, preferred_element_type=jnp.float32
            )
        work[:, rank:] = image
        work[:, :rank] = lax.dot_general(
            image, image, (((1,), (1,)), ((), ())),
            precision=HIGHEST, preferred_element_type=jnp.float32,
        )
        for k in range(rank // PANEL):
            low, high = k * PANEL, (k + 1) * PANEL
            inverse = inverse_factor(work[low:high, low:high])
            first = high // 128 * 128
            panel = jnp.dot(
                inverse, work[low:high, first:], precision=HIGHEST, preferred_element_type=jnp.float32
            )
            work[low:high, first:] = panel
            if high < rank:
                work[high:, first:] -= lax.dot_general(
                    panel[:, high - first : rank - first], panel, (((0,), (0,)), ((), ())),
                    precision=HIGHEST, preferred_element_type=jnp.float32,
                )
    rotation = work[:, rank:].astype(jnp.bfloat16)
    load_moved.wait()
    load_bathed.wait()
    pieces = out_sems.shape[0]
    size = moved.shape[0] // pieces

    def store(piece):
        rows = pl.ds(pl.multiple_of(piece * size, size), size)
        return pltpu.make_async_copy(out.at[rows, :], out_hbm.at[rows, :], out_sems.at[piece])

    def one(piece, carry):
        rows = pl.ds(pl.multiple_of(piece * size, size), size)
        value = lax.dot_general(
            moved[rows, :], rotation[:, :rank], (((1,), (1,)), ((), ())),
            preferred_element_type=jnp.float32,
        )
        value += lax.dot_general(
            bathed[rows, :], rotation[:, rank:], (((1,), (1,)), ((), ())),
            preferred_element_type=jnp.float32,
        )
        out[rows, :] = value.astype(jnp.bfloat16)
        store(piece).start()
        return carry

    lax.fori_loop(0, pieces, one, 0)

    def drain(piece, carry):
        store(piece).wait()
        return carry

    lax.fori_loop(0, pieces, drain, 0)


def finish_part(order, chunks, moved, bathed):
    rows, rank = moved.shape
    return pl.pallas_call(
        finish_kernel,
        in_specs=[
            pl.BlockSpec(memory_space=pltpu.SMEM),
            pl.BlockSpec(memory_space=pltpu.VMEM),
            pl.BlockSpec(memory_space=pl.ANY),
            pl.BlockSpec(memory_space=pl.ANY),
        ],
        out_specs=pl.BlockSpec(memory_space=pl.ANY),
        out_shape=jax.ShapeDtypeStruct((rows, rank), jnp.bfloat16),
        scratch_shapes=[
            pltpu.VMEM((2 * rank, 2 * rank), jnp.float32),
            pltpu.VMEM((rank, 3 * rank), jnp.float32),
            pltpu.VMEM((rows, rank), jnp.bfloat16),
            pltpu.VMEM((rows, rank), jnp.bfloat16),
            pltpu.VMEM((rows, rank), jnp.bfloat16),
            pltpu.SemaphoreType.DMA((2,)),
            pltpu.SemaphoreType.DMA((8,)),
        ],
        compiler_params=pltpu.CompilerParams(vmem_limit_bytes=24 * 2**20),
        name="finish",
    )(order, chunks, moved, bathed)


def ring_order(count):
    wide = 2
    while 4 * wide * wide <= count:
        wide *= 2
    tall = count // wide
    walk = [0]
    for r in range(tall):
        across = range(1, wide)
        walk += [r * wide + c for c in (across if r % 2 == 0 else reversed(across))]
    return walk + [r * wide for r in range(tall - 1, 0, -1)]


PIECES = 4


def tie(one, other):
    return lax.optimization_barrier((one, other))


def ring_gather(own, side, stages):
    order = ring_order(lax.axis_size("col"))
    following = order[1:] + order[:1]
    forward = list(zip(order, following))
    back = list(zip(following, order))
    size = own.shape[0] // PIECES
    pieces = [own[i * size : (i + 1) * size] for i in range(PIECES)]
    stages = list(stages)
    steps = []
    for step in range(1, len(order)):
        if step > 1:
            pieces[-1], side = tie(pieces[-1], side)
        pieces = [
            lax.ppermute(piece, "col", forward if i < PIECES // 2 else back)
            for i, piece in enumerate(pieces)
        ]
        if step > 1 and stages:
            side = stages.pop(0)(side)
        steps.append(list(pieces))
    for stage in stages:
        side = stage(side)
    return steps, side


def slot_lists(ids, counts, kinds):
    blocks, slots = ids.shape
    count = lax.axis_size("col")
    order = ring_order(count)
    place = jnp.asarray([order.index(c) for c in range(count)], jnp.int32)
    col = jnp.arange(count, dtype=jnp.int32)
    mine = jnp.sum(jnp.where(col == lax.axis_index("col"), place, 0))
    owner, within = ids // blocks, ids % blocks
    theirs = jnp.sum(jnp.where(owner[..., None] == col, place, 0), axis=-1)
    in_piece = blocks // PIECES
    piece = within // in_piece
    step = jnp.where(piece >= PIECES // 2, theirs - mine, mine - theirs) % count
    last = step == count - 1
    origin = jnp.where(last, piece, jnp.where(step == 0, 0, 1 + (step - 1) * PIECES + piece))
    offset = jnp.where(step == 0, within, within % in_piece)
    slot = jnp.arange(slots, dtype=jnp.int32)
    used = slot[None, :] < counts[:, None]
    key = jnp.where(used, jnp.where(last, slots, 0), 2 * slots) + slot
    rank = jnp.sum((key[:, None, :] < key[:, :, None]).astype(jnp.int32), axis=-1)
    at = rank[:, :, None] == slot
    def arrange(values):
        return jnp.sum(jnp.where(at, values[:, :, None], 0), axis=1)

    late = jnp.sum((used & last).astype(jnp.int32), axis=1)
    early = counts - late
    origin, offset, kinds = arrange(origin), arrange(offset), arrange(kinds)
    return (origin, offset, jnp.zeros_like(early), early, kinds), (origin, offset, early, late, kinds)


def swap(value, axis, stride):
    count = lax.axis_size(axis)
    return lax.ppermute(value, axis, [(i, i ^ stride) for i in range(count)])


def strides(axis):
    return [1 << i for i in range(lax.axis_size(axis).bit_length() - 1)]


def halve_over_row(value):
    place = lax.axis_index("row")
    for stride in strides("row"):
        half = value.shape[0] // 2
        upper = (place // stride) % 2
        keep = lax.dynamic_slice_in_dim(value, upper * half, half, 0)
        give = lax.dynamic_slice_in_dim(value, (1 - upper) * half, half, 0)
        value = keep + swap(give, "row", stride)
    return value


def sum_relative(value):
    count = lax.axis_size("col")
    place = lax.axis_index("col")
    size = value.shape[0] // count
    mine = lax.dynamic_slice_in_dim(value, place * size, size, 0)
    others = [
        swap(lax.dynamic_slice_in_dim(value, (place ^ k) * size, size, 0), "col", k)
        for k in range(1, count)
    ]
    for other in others:
        mine = mine + other
    value = jnp.concatenate([mine] + [swap(mine, "col", k) for k in range(1, count)], axis=0)
    for stride in reversed(strides("row")):
        value = jnp.concatenate([value, swap(value, "row", stride)], axis=0)
    return value


def chunk_order():
    row, col = lax.axis_index("row"), lax.axis_index("col")
    count = lax.axis_size("col")
    order = []
    for relative in range(lax.axis_size("row")):
        part = 0
        for i, stride in enumerate(strides("row")):
            height = len(strides("row")) - 1 - i
            bit = (relative >> height) & 1
            part = part + (((row // stride) % 2) ^ bit) * (1 << height)
        order += [part * count + (col ^ k) for k in range(count)]
    return jnp.stack(order).astype(jnp.int32)


def shards(
    density_factor,
    onsite,
    neighbour_ids,
    neighbour_count,
    coupling_type,
    coupling_blocks,
    bath_pattern,
    bath_blocks,
):
    blocks, slots = neighbour_ids.shape
    group_blocks = lax.axis_size("col") * blocks
    in_group = neighbour_ids - lax.axis_index("row") * group_blocks
    early, late = slot_lists(in_group, neighbour_count, coupling_type)
    bathed, base, corner = bath_part(
        density_factor, onsite.reshape(-1, 1), bath_pattern, bath_blocks
    )
    steps, corner = ring_gather(density_factor, corner, [halve_over_row])
    ready = [density_factor] + [piece for step in steps[:-1] for piece in step]
    total = early_part(early, ready, coupling_blocks, base)
    moved, upper = late_part(late, steps[-1], coupling_blocks, total, bathed)
    gram = sum_relative(jnp.concatenate([halve_over_row(upper), corner], axis=1))
    order = chunk_order()
    size = gram.shape[0] // order.shape[0]
    if size % 8:
        gram = gram.reshape(-1, size, gram.shape[1])
        gram = jnp.zeros_like(gram).at[order].set(gram).reshape(-1, gram.shape[2])
        order = jnp.arange(gram.shape[0] // 8, dtype=jnp.int32)
    return finish_part(order, gram, moved, bathed)


def solution(mesh):
    placed = (
        P(("row", "col"), None),
        P(("row", "col")),
        P(("row", "col"), None),
        P(("row", "col")),
        P(("row", "col"), None),
        P(),
        P(("row", "col")),
        P(),
    )
    return jax.shard_map(
        shards, mesh=mesh, in_specs=placed, out_specs=P(("row", "col"), None), check_vma=False
    )
```

```python
import jax
import jax.numpy as jnp
from jax import lax
from jax.experimental import pallas as pl
from jax.experimental.pallas import tpu as pltpu
from jax.sharding import PartitionSpec as P

SWEEPS = 2
time_step = 0.25
PANEL = 64
HIGHEST = lax.Precision.HIGHEST


def bath_kernel(pattern_ref, bath_ref, own_ref, energy_ref, bathed_ref, base_ref, gram_ref):
    own = own_ref[...]
    bathed = jnp.dot(bath_ref[0], own, preferred_element_type=jnp.float32).astype(jnp.bfloat16)
    bathed_ref[...] = bathed
    wide = own.astype(jnp.float32)
    base_ref[...] = wide - time_step * (energy_ref[...] * wide)
    part = lax.dot_general(
        bathed, bathed, (((0,), (0,)), ((), ())), preferred_element_type=jnp.float32
    )

    @pl.when(pl.program_id(0) == 0)
    def _():
        gram_ref[...] = part

    @pl.when(pl.program_id(0) > 0)
    def _():
        gram_ref[...] += part


def bath_part(own, energy, bath_pattern, bath_blocks):
    blocks = bath_pattern.shape[0]
    block_rows = bath_blocks.shape[1]
    rows, rank = own.shape
    return pl.pallas_call(
        bath_kernel,
        grid_spec=pltpu.PrefetchScalarGridSpec(
            num_scalar_prefetch=1,
            grid=(blocks,),
            in_specs=[
                pl.BlockSpec((1, block_rows, block_rows), lambda b, kind: (kind[b], 0, 0)),
                pl.BlockSpec((block_rows, rank), lambda b, kind: (b, 0)),
                pl.BlockSpec((block_rows, 1), lambda b, kind: (b, 0)),
            ],
            out_specs=[
                pl.BlockSpec((block_rows, rank), lambda b, kind: (b, 0)),
                pl.BlockSpec((block_rows, rank), lambda b, kind: (b, 0)),
                pl.BlockSpec((rank, rank), lambda b, kind: (0, 0)),
            ],
        ),
        out_shape=[
            jax.ShapeDtypeStruct((rows, rank), jnp.bfloat16),
            jax.ShapeDtypeStruct((rows, rank), jnp.float32),
            jax.ShapeDtypeStruct((rank, rank), jnp.float32),
        ],
        compiler_params=pltpu.CompilerParams(vmem_limit_bytes=16 * 2**20),
        name="bath",
    )(bath_pattern, bath_blocks, own, energy)


def gather_products(origin_ref, offset_ref, first_ref, count_ref, kind_ref, sources, coupling_ref, held, sems, total):
    blocks, slots = origin_ref.shape
    block_rows = held.shape[2]
    b = pl.program_id(0)
    group = 1
    while group * group < len(sources):
        group += 1

    def copy(source, block, slot):
        start = pl.multiple_of(offset_ref[block, slot] * block_rows, block_rows)
        return pltpu.make_async_copy(
            source.at[pl.ds(start, block_rows), :],
            held.at[lax.rem(block, 2), slot],
            sems.at[lax.rem(block, 2), slot],
        )

    def fetch(block):
        def one(slot, carry):
            origin = origin_ref[block, slot]
            for low in range(0, len(sources), group):
                high = min(low + group, len(sources))

                @pl.when((origin >= low) & (origin < high))
                def _():
                    for place in range(low, high):
                        @pl.when(origin == place)
                        def _():
                            copy(sources[place], block, slot).start()
            return carry

        lax.fori_loop(first_ref[block], first_ref[block] + count_ref[block], one, 0)

    @pl.when(b == 0)
    def _():
        fetch(0)

    @pl.when(b + 1 < blocks)
    def _():
        fetch(b + 1)

    def add(slot, carry):
        copy(sources[0], b, slot).wait()
        total[...] -= time_step * jnp.dot(
            coupling_ref[kind_ref[b, slot]],
            held[lax.rem(b, 2), slot],
            preferred_element_type=jnp.float32,
        )
        return carry

    lax.fori_loop(first_ref[b], first_ref[b] + count_ref[b], add, 0)


def early_kernel(origin_ref, offset_ref, first_ref, count_ref, kind_ref, *refs):
    sources = refs[:-5]
    coupling_ref, base_ref, total_ref, held, sems = refs[-5:]
    total_ref[...] = base_ref[...]
    gather_products(
        origin_ref, offset_ref, first_ref, count_ref, kind_ref, sources, coupling_ref, held, sems, total_ref
    )


def late_kernel(origin_ref, offset_ref, first_ref, count_ref, kind_ref, *refs):
    sources = refs[:-8]
    coupling_ref, base_ref, bathed_ref, moved_ref, gram_ref, total, held, sems = refs[-8:]
    b = pl.program_id(0)
    total[...] = base_ref[...]
    gather_products(
        origin_ref, offset_ref, first_ref, count_ref, kind_ref, sources, coupling_ref, held, sems, total
    )
    moved = total[...].astype(jnp.bfloat16)
    moved_ref[...] = moved
    both = jnp.concatenate([moved, bathed_ref[...]], axis=1)
    part = lax.dot_general(
        moved, both, (((0,), (0,)), ((), ())), preferred_element_type=jnp.float32
    )

    @pl.when(b == 0)
    def _():
        gram_ref[...] = part

    @pl.when(b > 0)
    def _():
        gram_ref[...] += part


def early_part(lists, sources, coupling_blocks, base):
    blocks, slots = lists[0].shape
    kinds, block_rows, _ = coupling_blocks.shape
    rows, rank = base.shape
    tile = pl.BlockSpec((block_rows, rank), lambda b, *_: (b, 0))
    return pl.pallas_call(
        early_kernel,
        grid_spec=pltpu.PrefetchScalarGridSpec(
            num_scalar_prefetch=5,
            grid=(blocks,),
            in_specs=[
                *[pl.BlockSpec(memory_space=pl.ANY) for _ in sources],
                pl.BlockSpec((kinds, block_rows, block_rows), lambda b, *_: (0, 0, 0)),
                tile,
            ],
            out_specs=tile,
            scratch_shapes=[
                pltpu.VMEM((2, slots, block_rows, rank), jnp.bfloat16),
                pltpu.SemaphoreType.DMA((2, slots)),
            ],
        ),
        out_shape=jax.ShapeDtypeStruct((rows, rank), jnp.float32),
        compiler_params=pltpu.CompilerParams(vmem_limit_bytes=16 * 2**20),
        cost_estimate=pl.CostEstimate(
            flops=blocks * slots * block_rows * block_rows * rank,
            bytes_accessed=blocks * slots * block_rows * rank * 2,
            transcendentals=0,
        ),
        name="couple_early",
    )(*lists, *sources, coupling_blocks, base)


def late_part(lists, sources, coupling_blocks, base, bathed):
    blocks, slots = lists[0].shape
    kinds, block_rows, _ = coupling_blocks.shape
    rows, rank = base.shape
    tile = pl.BlockSpec((block_rows, rank), lambda b, *_: (b, 0))
    return pl.pallas_call(
        late_kernel,
        grid_spec=pltpu.PrefetchScalarGridSpec(
            num_scalar_prefetch=5,
            grid=(blocks,),
            in_specs=[
                *[pl.BlockSpec(memory_space=pl.ANY) for _ in sources],
                pl.BlockSpec((kinds, block_rows, block_rows), lambda b, *_: (0, 0, 0)),
                tile,
                tile,
            ],
            out_specs=[tile, pl.BlockSpec((rank, 2 * rank), lambda b, *_: (0, 0))],
            scratch_shapes=[
                pltpu.VMEM((block_rows, rank), jnp.float32),
                pltpu.VMEM((2, slots, block_rows, rank), jnp.bfloat16),
                pltpu.SemaphoreType.DMA((2, slots)),
            ],
        ),
        out_shape=[
            jax.ShapeDtypeStruct((rows, rank), jnp.bfloat16),
            jax.ShapeDtypeStruct((rank, 2 * rank), jnp.float32),
        ],
        compiler_params=pltpu.CompilerParams(vmem_limit_bytes=20 * 2**20),
        name="couple_late",
    )(*lists, *sources, coupling_blocks, base, bathed)


def inverse_factor(square):
    n = square.shape[0]
    eye = (
        lax.broadcasted_iota(jnp.int32, (n, n), 0) == lax.broadcasted_iota(jnp.int32, (n, n), 1)
    ).astype(jnp.float32)
    work = jnp.concatenate([square, eye], axis=1)
    bands = [work[8 * i : 8 * i + 8, :] for i in range(n // 8)]
    sublane = lax.broadcasted_iota(jnp.int32, (8, 2 * n), 0)
    out = []
    for g in range(n // 8):
        below = range(g, n // 8)
        columns = {
            i: [jnp.broadcast_to(bands[i][:, 8 * g + r : 8 * g + r + 1], (8, 2 * n)) for r in range(8)]
            for i in below
        }
        diagonal = jnp.zeros((8, 2 * n), jnp.float32)
        for r in range(8):
            pivots = [columns[g][q][r : r + 1, :] for q in range(r, 8)]
            scale = pl.reciprocal(pivots[0], approx=True)
            diagonal = jnp.where(sublane == r, columns[g][r], diagonal)
            row = bands[g][r : r + 1, :]
            for i in below:
                share = columns[i][r] * scale
                if i == g:
                    share = jnp.where(sublane > r, share, 0.0)
                for q in range(r + 1, 8):
                    columns[i][q] = columns[i][q] - share * pivots[q - r]
                bands[i] = bands[i] - share * row
        out.append(bands[g][:, n:] * lax.rsqrt(diagonal)[:, n:])
    return jnp.concatenate(out, axis=0)


def finish_kernel(
    order_ref, chunks_ref, moved_hbm, bathed_hbm, out_hbm,
    gram, work, moved, bathed, out, in_sems, out_sems,
):
    rank = chunks_ref.shape[0]
    load_moved = pltpu.make_async_copy(moved_hbm, moved, in_sems.at[0])
    load_bathed = pltpu.make_async_copy(bathed_hbm, bathed, in_sems.at[1])
    load_moved.start()
    load_bathed.start()

    chunks = order_ref.shape[0]
    size = rank // chunks
    for i in range(chunks):
        rows = pl.ds(pl.multiple_of(order_ref[i] * size, size), size)
        chunk = chunks_ref[i * size : (i + 1) * size, :]
        gram[rows, :] = chunk[:, : 2 * rank]
        gram[pl.ds(pl.multiple_of(rank + order_ref[i] * size, size), size), rank:] = chunk[:, 2 * rank :]
    gram[rank:, :rank] = gram[:rank, rank:].T
    for sweep in range(SWEEPS):
        if sweep == 0:
            image = gram[:rank, :]
        else:
            image = jnp.dot(
                work[:, rank:], gram[...], precision=HIGHEST, preferred_element_type=jnp.float32
            )
        work[:, rank:] = image
        work[:, :rank] = lax.dot_general(
            image, image, (((1,), (1,)), ((), ())),
            precision=HIGHEST, preferred_element_type=jnp.float32,
        )
        for k in range(rank // PANEL):
            low, high = k * PANEL, (k + 1) * PANEL
            inverse = inverse_factor(work[low:high, low:high])
            first = high // 128 * 128
            panel = jnp.dot(
                inverse, work[low:high, first:], precision=HIGHEST, preferred_element_type=jnp.float32
            )
            work[low:high, first:] = panel
            if high < rank:
                work[high:, first:] -= lax.dot_general(
                    panel[:, high - first : rank - first], panel, (((0,), (0,)), ((), ())),
                    precision=HIGHEST, preferred_element_type=jnp.float32,
                )
    rotation = work[:, rank:].astype(jnp.bfloat16)
    load_moved.wait()
    load_bathed.wait()
    pieces = out_sems.shape[0]
    size = moved.shape[0] // pieces

    def store(piece):
        rows = pl.ds(pl.multiple_of(piece * size, size), size)
        return pltpu.make_async_copy(out.at[rows, :], out_hbm.at[rows, :], out_sems.at[piece])

    def one(piece, carry):
        rows = pl.ds(pl.multiple_of(piece * size, size), size)
        value = lax.dot_general(
            moved[rows, :], rotation[:, :rank], (((1,), (1,)), ((), ())),
            preferred_element_type=jnp.float32,
        )
        value += lax.dot_general(
            bathed[rows, :], rotation[:, rank:], (((1,), (1,)), ((), ())),
            preferred_element_type=jnp.float32,
        )
        out[rows, :] = value.astype(jnp.bfloat16)
        store(piece).start()
        return carry

    lax.fori_loop(0, pieces, one, 0)

    def drain(piece, carry):
        store(piece).wait()
        return carry

    lax.fori_loop(0, pieces, drain, 0)


def finish_part(order, chunks, moved, bathed):
    rows, rank = moved.shape
    return pl.pallas_call(
        finish_kernel,
        in_specs=[
            pl.BlockSpec(memory_space=pltpu.SMEM),
            pl.BlockSpec(memory_space=pltpu.VMEM),
            pl.BlockSpec(memory_space=pl.ANY),
            pl.BlockSpec(memory_space=pl.ANY),
        ],
        out_specs=pl.BlockSpec(memory_space=pl.ANY),
        out_shape=jax.ShapeDtypeStruct((rows, rank), jnp.bfloat16),
        scratch_shapes=[
            pltpu.VMEM((2 * rank, 2 * rank), jnp.float32),
            pltpu.VMEM((rank, 3 * rank), jnp.float32),
            pltpu.VMEM((rows, rank), jnp.bfloat16),
            pltpu.VMEM((rows, rank), jnp.bfloat16),
            pltpu.VMEM((rows, rank), jnp.bfloat16),
            pltpu.SemaphoreType.DMA((2,)),
            pltpu.SemaphoreType.DMA((8,)),
        ],
        compiler_params=pltpu.CompilerParams(vmem_limit_bytes=24 * 2**20),
        name="finish",
    )(order, chunks, moved, bathed)


def ring_order(count):
    wide = 2
    while 4 * wide * wide <= count:
        wide *= 2
    tall = count // wide
    walk = [0]
    for r in range(tall):
        across = range(1, wide)
        walk += [r * wide + c for c in (across if r % 2 == 0 else reversed(across))]
    return walk + [r * wide for r in range(tall - 1, 0, -1)]


PIECES = 4


def tie(one, other):
    return lax.optimization_barrier((one, other))


def ring_gather(own, side, stages):
    order = ring_order(lax.axis_size("col"))
    following = order[1:] + order[:1]
    forward = list(zip(order, following))
    back = list(zip(following, order))
    size = own.shape[0] // PIECES
    pieces = [own[i * size : (i + 1) * size] for i in range(PIECES)]
    stages = list(stages)
    steps = []
    for step in range(1, len(order)):
        if step > 1:
            pieces[-1], side = tie(pieces[-1], side)
        pieces = [
            lax.ppermute(piece, "col", forward if i < PIECES // 2 else back)
            for i, piece in enumerate(pieces)
        ]
        if step > 1 and stages:
            side = stages.pop(0)(side)
        steps.append(list(pieces))
    for stage in stages:
        side = stage(side)
    return steps, side


def slot_lists(ids, counts, kinds):
    blocks, slots = ids.shape
    count = lax.axis_size("col")
    order = ring_order(count)
    place = jnp.asarray([order.index(c) for c in range(count)], jnp.int32)
    col = jnp.arange(count, dtype=jnp.int32)
    mine = jnp.sum(jnp.where(col == lax.axis_index("col"), place, 0))
    owner, within = ids // blocks, ids % blocks
    theirs = jnp.sum(jnp.where(owner[..., None] == col, place, 0), axis=-1)
    in_piece = blocks // PIECES
    piece = within // in_piece
    step = jnp.where(piece >= PIECES // 2, theirs - mine, mine - theirs) % count
    last = step == count - 1
    origin = jnp.where(last, piece, jnp.where(step == 0, 0, 1 + (step - 1) * PIECES + piece))
    offset = jnp.where(step == 0, within, within % in_piece)
    slot = jnp.arange(slots, dtype=jnp.int32)
    used = slot[None, :] < counts[:, None]
    key = jnp.where(used, jnp.where(last, slots, 0), 2 * slots) + slot
    rank = jnp.sum((key[:, None, :] < key[:, :, None]).astype(jnp.int32), axis=-1)
    at = rank[:, :, None] == slot
    def arrange(values):
        return jnp.sum(jnp.where(at, values[:, :, None], 0), axis=1)

    late = jnp.sum((used & last).astype(jnp.int32), axis=1)
    early = counts - late
    origin, offset, kinds = arrange(origin), arrange(offset), arrange(kinds)
    return (origin, offset, jnp.zeros_like(early), early, kinds), (origin, offset, early, late, kinds)


def swap(value, axis, stride):
    count = lax.axis_size(axis)
    return lax.ppermute(value, axis, [(i, i ^ stride) for i in range(count)])


def strides(axis):
    return [1 << i for i in range(lax.axis_size(axis).bit_length() - 1)]


def halve_over_row(value):
    place = lax.axis_index("row")
    for stride in strides("row"):
        half = value.shape[0] // 2
        upper = (place // stride) % 2
        keep = lax.dynamic_slice_in_dim(value, upper * half, half, 0)
        give = lax.dynamic_slice_in_dim(value, (1 - upper) * half, half, 0)
        value = keep + swap(give, "row", stride)
    return value


def sum_relative(value):
    count = lax.axis_size("col")
    parts = value.reshape(count, -1, value.shape[1])
    mine = jnp.sum(lax.all_to_all(parts, "col", split_axis=0, concat_axis=0), axis=0)
    copies = jnp.broadcast_to(mine, parts.shape)
    value = lax.all_to_all(copies, "col", split_axis=0, concat_axis=0).reshape(value.shape)
    for stride in reversed(strides("row")):
        value = jnp.concatenate([value, swap(value, "row", stride)], axis=0)
    return value


def chunk_order():
    row = lax.axis_index("row")
    count = lax.axis_size("col")
    order = []
    for relative in range(lax.axis_size("row")):
        part = 0
        for i, stride in enumerate(strides("row")):
            height = len(strides("row")) - 1 - i
            bit = (relative >> height) & 1
            part = part + (((row // stride) % 2) ^ bit) * (1 << height)
        order += [part * count + k for k in range(count)]
    return jnp.stack(order).astype(jnp.int32)


def shards(
    density_factor,
    onsite,
    neighbour_ids,
    neighbour_count,
    coupling_type,
    coupling_blocks,
    bath_pattern,
    bath_blocks,
):
    blocks, slots = neighbour_ids.shape
    group_blocks = lax.axis_size("col") * blocks
    in_group = neighbour_ids - lax.axis_index("row") * group_blocks
    early, late = slot_lists(in_group, neighbour_count, coupling_type)
    bathed, base, corner = bath_part(
        density_factor, onsite.reshape(-1, 1), bath_pattern, bath_blocks
    )
    steps, corner = ring_gather(density_factor, corner, [halve_over_row])
    ready = [density_factor] + [piece for step in steps[:-1] for piece in step]
    total = early_part(early, ready, coupling_blocks, base)
    moved, upper = late_part(late, steps[-1], coupling_blocks, total, bathed)
    gram = sum_relative(jnp.concatenate([halve_over_row(upper), corner], axis=1))
    order = chunk_order()
    size = gram.shape[0] // order.shape[0]
    if size % 8:
        gram = gram.reshape(-1, size, gram.shape[1])
        gram = jnp.zeros_like(gram).at[order].set(gram).reshape(-1, gram.shape[2])
        order = jnp.arange(gram.shape[0] // 8, dtype=jnp.int32)
    return finish_part(order, gram, moved, bathed)


def solution(mesh):
    placed = (
        P(("row", "col"), None),
        P(("row", "col")),
        P(("row", "col"), None),
        P(("row", "col")),
        P(("row", "col"), None),
        P(),
        P(("row", "col")),
        P(),
    )
    return jax.shard_map(
        shards, mesh=mesh, in_specs=placed, out_specs=P(("row", "col"), None), check_vma=False
    )
```

```python
import jax
import jax.numpy as jnp
from jax import lax
from jax.experimental import pallas as pl
from jax.experimental.pallas import tpu as pltpu
from jax.sharding import PartitionSpec as P

SWEEPS = 2
time_step = 0.25
PANEL = 64
HIGHEST = lax.Precision.HIGHEST


def bath_kernel(pattern_ref, bath_ref, own_ref, bathed_ref, gram_ref):
    bathed = jnp.dot(bath_ref[0], own_ref[...], preferred_element_type=jnp.float32).astype(jnp.bfloat16)
    bathed_ref[...] = bathed
    part = lax.dot_general(
        bathed, bathed, (((0,), (0,)), ((), ())), preferred_element_type=jnp.float32
    )

    @pl.when(pl.program_id(0) == 0)
    def _():
        gram_ref[...] = part

    @pl.when(pl.program_id(0) > 0)
    def _():
        gram_ref[...] += part


def bath_part(own, bath_pattern, bath_blocks):
    blocks = bath_pattern.shape[0]
    block_rows = bath_blocks.shape[1]
    rows, rank = own.shape
    tile = pl.BlockSpec((block_rows, rank), lambda b, kind: (b, 0))
    return pl.pallas_call(
        bath_kernel,
        grid_spec=pltpu.PrefetchScalarGridSpec(
            num_scalar_prefetch=1,
            grid=(blocks,),
            in_specs=[
                pl.BlockSpec((1, block_rows, block_rows), lambda b, kind: (kind[b], 0, 0)),
                tile,
            ],
            out_specs=[tile, pl.BlockSpec((rank, rank), lambda b, kind: (0, 0))],
        ),
        out_shape=[
            jax.ShapeDtypeStruct((rows, rank), jnp.bfloat16),
            jax.ShapeDtypeStruct((rank, rank), jnp.float32),
        ],
        compiler_params=pltpu.CompilerParams(vmem_limit_bytes=12 * 2**20),
        name="bath",
    )(bath_pattern, bath_blocks, own)


def gather_products(origin_ref, offset_ref, first_ref, count_ref, kind_ref, sources, coupling_ref, held, sems, total):
    blocks, slots = origin_ref.shape
    block_rows = held.shape[2]
    b = pl.program_id(0)
    group = 1
    while group * group < len(sources):
        group += 1

    def copy(source, block, slot):
        start = pl.multiple_of(offset_ref[block, slot] * block_rows, block_rows)
        return pltpu.make_async_copy(
            source.at[pl.ds(start, block_rows), :],
            held.at[lax.rem(block, 2), slot],
            sems.at[lax.rem(block, 2), slot],
        )

    def fetch(block):
        def one(slot, carry):
            origin = origin_ref[block, slot]
            for low in range(0, len(sources), group):
                high = min(low + group, len(sources))

                @pl.when((origin >= low) & (origin < high))
                def _():
                    for place in range(low, high):
                        @pl.when(origin == place)
                        def _():
                            copy(sources[place], block, slot).start()
            return carry

        lax.fori_loop(first_ref[block], first_ref[block] + count_ref[block], one, 0)

    @pl.when(b == 0)
    def _():
        fetch(0)

    @pl.when(b + 1 < blocks)
    def _():
        fetch(b + 1)

    def add(slot, carry):
        copy(sources[0], b, slot).wait()
        total[...] -= time_step * jnp.dot(
            coupling_ref[kind_ref[b, slot]],
            held[lax.rem(b, 2), slot],
            preferred_element_type=jnp.float32,
        )
        return carry

    lax.fori_loop(first_ref[b], first_ref[b] + count_ref[b], add, 0)


def early_kernel(origin_ref, offset_ref, first_ref, count_ref, kind_ref, *refs):
    sources = refs[:-6]
    coupling_ref, own_ref, energy_ref, total_ref, held, sems = refs[-6:]
    block_rows = own_ref.shape[0]
    row = energy_ref[pl.ds(pl.program_id(0), 1), :]
    energy = jnp.broadcast_to(row, (8, block_rows)).T[:, :1]
    wide = own_ref[...].astype(jnp.float32)
    total_ref[...] = wide - time_step * (energy * wide)
    gather_products(
        origin_ref, offset_ref, first_ref, count_ref, kind_ref, sources, coupling_ref, held, sems, total_ref
    )


def late_kernel(origin_ref, offset_ref, first_ref, count_ref, kind_ref, *refs):
    sources = refs[:-8]
    coupling_ref, base_ref, bathed_ref, moved_ref, gram_ref, total, held, sems = refs[-8:]
    b = pl.program_id(0)
    total[...] = base_ref[...]
    gather_products(
        origin_ref, offset_ref, first_ref, count_ref, kind_ref, sources, coupling_ref, held, sems, total
    )
    moved = total[...].astype(jnp.bfloat16)
    moved_ref[...] = moved
    both = jnp.concatenate([moved, bathed_ref[...]], axis=1)
    part = lax.dot_general(
        moved, both, (((0,), (0,)), ((), ())), preferred_element_type=jnp.float32
    )

    @pl.when(b == 0)
    def _():
        gram_ref[...] = part

    @pl.when(b > 0)
    def _():
        gram_ref[...] += part


def early_part(lists, sources, coupling_blocks, own, onsite):
    blocks, slots = lists[0].shape
    kinds, block_rows, _ = coupling_blocks.shape
    rows, rank = own.shape
    tile = pl.BlockSpec((block_rows, rank), lambda b, *_: (b, 0))
    return pl.pallas_call(
        early_kernel,
        grid_spec=pltpu.PrefetchScalarGridSpec(
            num_scalar_prefetch=5,
            grid=(blocks,),
            in_specs=[
                *[pl.BlockSpec(memory_space=pl.ANY) for _ in sources],
                pl.BlockSpec((kinds, block_rows, block_rows), lambda b, *_: (0, 0, 0)),
                tile,
                pl.BlockSpec((blocks, block_rows), lambda b, *_: (0, 0)),
            ],
            out_specs=tile,
            scratch_shapes=[
                pltpu.VMEM((2, slots, block_rows, rank), jnp.bfloat16),
                pltpu.SemaphoreType.DMA((2, slots)),
            ],
        ),
        out_shape=jax.ShapeDtypeStruct((rows, rank), jnp.float32),
        compiler_params=pltpu.CompilerParams(vmem_limit_bytes=16 * 2**20),
        cost_estimate=pl.CostEstimate(
            flops=blocks * slots * block_rows * block_rows * rank,
            bytes_accessed=blocks * slots * block_rows * rank * 2,
            transcendentals=0,
        ),
        name="couple_early",
    )(*lists, *sources, coupling_blocks, own, onsite.reshape(blocks, block_rows))


def late_part(lists, sources, coupling_blocks, base, bathed):
    blocks, slots = lists[0].shape
    kinds, block_rows, _ = coupling_blocks.shape
    rows, rank = base.shape
    tile = pl.BlockSpec((block_rows, rank), lambda b, *_: (b, 0))
    return pl.pallas_call(
        late_kernel,
        grid_spec=pltpu.PrefetchScalarGridSpec(
            num_scalar_prefetch=5,
            grid=(blocks,),
            in_specs=[
                *[pl.BlockSpec(memory_space=pl.ANY) for _ in sources],
                pl.BlockSpec((kinds, block_rows, block_rows), lambda b, *_: (0, 0, 0)),
                tile,
                tile,
            ],
            out_specs=[tile, pl.BlockSpec((rank, 2 * rank), lambda b, *_: (0, 0))],
            scratch_shapes=[
                pltpu.VMEM((block_rows, rank), jnp.float32),
                pltpu.VMEM((2, slots, block_rows, rank), jnp.bfloat16),
                pltpu.SemaphoreType.DMA((2, slots)),
            ],
        ),
        out_shape=[
            jax.ShapeDtypeStruct((rows, rank), jnp.bfloat16),
            jax.ShapeDtypeStruct((rank, 2 * rank), jnp.float32),
        ],
        compiler_params=pltpu.CompilerParams(vmem_limit_bytes=20 * 2**20),
        name="couple_late",
    )(*lists, *sources, coupling_blocks, base, bathed)


def inverse_factor(square):
    n = square.shape[0]
    eye = (
        lax.broadcasted_iota(jnp.int32, (n, n), 0) == lax.broadcasted_iota(jnp.int32, (n, n), 1)
    ).astype(jnp.float32)
    work = jnp.concatenate([square, eye], axis=1)
    bands = [work[8 * i : 8 * i + 8, :] for i in range(n // 8)]
    sublane = lax.broadcasted_iota(jnp.int32, (8, 2 * n), 0)
    out = []
    for g in range(n // 8):
        below = range(g, n // 8)
        columns = {
            i: [jnp.broadcast_to(bands[i][:, 8 * g + r : 8 * g + r + 1], (8, 2 * n)) for r in range(8)]
            for i in below
        }
        diagonal = jnp.zeros((8, 2 * n), jnp.float32)
        for r in range(8):
            pivots = [columns[g][q][r : r + 1, :] for q in range(r, 8)]
            scale = pl.reciprocal(pivots[0], approx=True)
            diagonal = jnp.where(sublane == r, columns[g][r], diagonal)
            row = bands[g][r : r + 1, :]
            for i in below:
                share = columns[i][r] * scale
                if i == g:
                    share = jnp.where(sublane > r, share, 0.0)
                for q in range(r + 1, 8):
                    columns[i][q] = columns[i][q] - share * pivots[q - r]
                bands[i] = bands[i] - share * row
        out.append(bands[g][:, n:] * lax.rsqrt(diagonal)[:, n:])
    return jnp.concatenate(out, axis=0)


def eliminate(inner, image):
    rank = inner.shape[0]

    def product(left, right, contract):
        return lax.dot_general(
            left, right, ((contract, (0,)), ((), ())),
            precision=HIGHEST, preferred_element_type=jnp.float32,
        )

    for low in range(0, rank, PANEL):
        high = low + PANEL
        here, first = low // 128 * 128, high // 128 * 128
        inverse = inverse_factor(inner[low:high, low:high])
        panel = product(inverse, inner[low:high, here:], (1,))
        inner[low:high, here:] = panel
        share = panel[:, high - here :]
        if high < rank:
            inner[high:, first:] -= product(share, panel[:, first - here :], (0,))
        side = product(inverse, image[low:high, :], (1,))
        image[low:high, :] = side
        if high < rank:
            image[high:, :] -= product(share, side, (0,))


def finish_kernel(
    order_ref, chunks_ref, moved_hbm, bathed_hbm, out_hbm,
    gram, inner, image, moved, bathed, out, in_sems, out_sems,
):
    rank = chunks_ref.shape[0]
    load_moved = pltpu.make_async_copy(moved_hbm, moved, in_sems.at[0])
    load_bathed = pltpu.make_async_copy(bathed_hbm, bathed, in_sems.at[1])
    load_moved.start()
    load_bathed.start()

    chunks = order_ref.shape[0]
    size = rank // chunks
    for i in range(chunks):
        rows = pl.ds(pl.multiple_of(order_ref[i] * size, size), size)
        chunk = chunks_ref[i * size : (i + 1) * size, :]
        gram[rows, :] = chunk[:, : 2 * rank]
        gram[pl.ds(pl.multiple_of(rank + order_ref[i] * size, size), size), rank:] = chunk[:, 2 * rank :]
    gram[rank:, :rank] = gram[:rank, rank:].T
    later = jnp.dot(gram[:rank, :], gram[...], precision=HIGHEST, preferred_element_type=jnp.float32)
    inner[...] = later[:, :rank]
    image[:, rank:] = later[:, rank:]
    for sweep in range(1, SWEEPS):
        eliminate(inner, image.at[:, rank:])
        upper = lax.broadcasted_iota(jnp.int32, (rank, rank), 0) <= lax.broadcasted_iota(jnp.int32, (rank, rank), 1)
        image[:, :rank] = jnp.where(upper, inner[...], 0.0)
        rows = image[...]
        inner[...] = lax.dot_general(
            rows, rows, (((1,), (1,)), ((), ())),
            precision=HIGHEST, preferred_element_type=jnp.float32,
        )
    eliminate(inner, image)
    rotation = image[...].astype(jnp.bfloat16)
    load_moved.wait()
    load_bathed.wait()
    pieces = out_sems.shape[0]
    size = moved.shape[0] // pieces

    def store(piece):
        rows = pl.ds(pl.multiple_of(piece * size, size), size)
        return pltpu.make_async_copy(out.at[rows, :], out_hbm.at[rows, :], out_sems.at[piece])

    def one(piece, carry):
        rows = pl.ds(pl.multiple_of(piece * size, size), size)
        value = lax.dot_general(
            moved[rows, :], rotation[:, :rank], (((1,), (1,)), ((), ())),
            preferred_element_type=jnp.float32,
        )
        value += lax.dot_general(
            bathed[rows, :], rotation[:, rank:], (((1,), (1,)), ((), ())),
            preferred_element_type=jnp.float32,
        )
        out[rows, :] = value.astype(jnp.bfloat16)
        store(piece).start()
        return carry

    lax.fori_loop(0, pieces, one, 0)

    def drain(piece, carry):
        store(piece).wait()
        return carry

    lax.fori_loop(0, pieces, drain, 0)


def finish_part(order, chunks, moved, bathed):
    rows, rank = moved.shape
    return pl.pallas_call(
        finish_kernel,
        in_specs=[
            pl.BlockSpec(memory_space=pltpu.SMEM),
            pl.BlockSpec(memory_space=pltpu.VMEM),
            pl.BlockSpec(memory_space=pl.ANY),
            pl.BlockSpec(memory_space=pl.ANY),
        ],
        out_specs=pl.BlockSpec(memory_space=pl.ANY),
        out_shape=jax.ShapeDtypeStruct((rows, rank), jnp.bfloat16),
        scratch_shapes=[
            pltpu.VMEM((2 * rank, 2 * rank), jnp.float32),
            pltpu.VMEM((rank, rank), jnp.float32),
            pltpu.VMEM((rank, 2 * rank), jnp.float32),
            pltpu.VMEM((rows, rank), jnp.bfloat16),
            pltpu.VMEM((rows, rank), jnp.bfloat16),
            pltpu.VMEM((rows, rank), jnp.bfloat16),
            pltpu.SemaphoreType.DMA((2,)),
            pltpu.SemaphoreType.DMA((8,)),
        ],
        compiler_params=pltpu.CompilerParams(vmem_limit_bytes=24 * 2**20),
        name="finish",
    )(order, chunks, moved, bathed)


def ring_order(count):
    wide = 2
    while 4 * wide * wide <= count:
        wide *= 2
    tall = count // wide
    walk = [0]
    for r in range(tall):
        across = range(1, wide)
        walk += [r * wide + c for c in (across if r % 2 == 0 else reversed(across))]
    return walk + [r * wide for r in range(tall - 1, 0, -1)]


PIECES = 4


def tie(one, other):
    return lax.optimization_barrier((one, other))


def ring_gather(own, side, stages):
    order = ring_order(lax.axis_size("col"))
    following = order[1:] + order[:1]
    forward = list(zip(order, following))
    back = list(zip(following, order))
    size = own.shape[0] // PIECES
    pieces = [own[i * size : (i + 1) * size] for i in range(PIECES)]
    stages = list(stages)
    steps = []
    for step in range(1, len(order)):
        if step > 1:
            pieces[-1], side = tie(pieces[-1], side)
        pieces = [
            lax.ppermute(piece, "col", forward if i < PIECES // 2 else back)
            for i, piece in enumerate(pieces)
        ]
        if step > 1 and stages:
            side = stages.pop(0)(side)
        steps.append(list(pieces))
    for stage in stages:
        side = stage(side)
    return steps, side


def slot_lists(ids, counts, kinds):
    blocks, slots = ids.shape
    count = lax.axis_size("col")
    order = ring_order(count)
    place = jnp.asarray([order.index(c) for c in range(count)], jnp.int32)
    col = jnp.arange(count, dtype=jnp.int32)
    mine = jnp.sum(jnp.where(col == lax.axis_index("col"), place, 0))
    owner, within = ids // blocks, ids % blocks
    theirs = jnp.sum(jnp.where(owner[..., None] == col, place, 0), axis=-1)
    in_piece = blocks // PIECES
    piece = within // in_piece
    step = jnp.where(piece >= PIECES // 2, theirs - mine, mine - theirs) % count
    last = step == count - 1
    origin = jnp.where(last, piece, jnp.where(step == 0, 0, 1 + (step - 1) * PIECES + piece))
    offset = jnp.where(step == 0, within, within % in_piece)
    slot = jnp.arange(slots, dtype=jnp.int32)
    used = slot[None, :] < counts[:, None]
    key = jnp.where(used, jnp.where(last, slots, 0), 2 * slots) + slot
    rank = jnp.sum((key[:, None, :] < key[:, :, None]).astype(jnp.int32), axis=-1)
    at = rank[:, :, None] == slot
    def arrange(values):
        return jnp.sum(jnp.where(at, values[:, :, None], 0), axis=1)

    late = jnp.sum((used & last).astype(jnp.int32), axis=1)
    early = counts - late
    origin, offset, kinds = arrange(origin), arrange(offset), arrange(kinds)
    return (origin, offset, jnp.zeros_like(early), early, kinds), (origin, offset, early, late, kinds)


def swap(value, axis, stride):
    count = lax.axis_size(axis)
    return lax.ppermute(value, axis, [(i, i ^ stride) for i in range(count)])


def strides(axis):
    return [1 << i for i in range(lax.axis_size(axis).bit_length() - 1)]


def halvings():
    return [("row", stride) for stride in strides("row")] + [("col", 1)]


def side_of(axis, stride):
    return (lax.axis_index(axis) // stride) % 2


def halve(value, axis, stride):
    half = value.shape[0] // 2
    upper = side_of(axis, stride)
    keep = lax.dynamic_slice_in_dim(value, upper * half, half, 0)
    give = lax.dynamic_slice_in_dim(value, (1 - upper) * half, half, 0)
    return keep + swap(give, axis, stride)


def halve_over_row(value):
    for stride in strides("row"):
        value = halve(value, "row", stride)
    return value


def sum_relative(value):
    value = halve(value, "col", 1)
    for stride in strides("col")[1:]:
        value = value + swap(value, "col", stride)
    for axis, stride in reversed(halvings()):
        value = jnp.concatenate([value, swap(value, axis, stride)], axis=0)
    return value


def chunk_order():
    swaps = halvings()
    order = []
    for relative in range(1 << len(swaps)):
        part = 0
        for i, (axis, stride) in enumerate(swaps):
            height = len(swaps) - 1 - i
            part = part + (side_of(axis, stride) ^ ((relative >> height) & 1)) * (1 << height)
        order.append(part)
    return jnp.stack(order).astype(jnp.int32)


def shards(
    density_factor,
    onsite,
    neighbour_ids,
    neighbour_count,
    coupling_type,
    coupling_blocks,
    bath_pattern,
    bath_blocks,
):
    blocks, slots = neighbour_ids.shape
    group_blocks = lax.axis_size("col") * blocks
    in_group = neighbour_ids - lax.axis_index("row") * group_blocks
    early, late = slot_lists(in_group, neighbour_count, coupling_type)
    bathed, corner = bath_part(density_factor, bath_pattern, bath_blocks)
    steps, corner = ring_gather(density_factor, corner, [halve_over_row])
    ready = [density_factor] + [piece for step in steps[:-1] for piece in step]
    total = early_part(early, ready, coupling_blocks, density_factor, onsite)
    moved, upper = late_part(late, steps[-1], coupling_blocks, total, bathed)
    gram = sum_relative(jnp.concatenate([halve_over_row(upper), corner], axis=1))
    return finish_part(chunk_order(), gram, moved, bathed)


def solution(mesh):
    placed = (
        P(("row", "col"), None),
        P(("row", "col")),
        P(("row", "col"), None),
        P(("row", "col")),
        P(("row", "col"), None),
        P(),
        P(("row", "col")),
        P(),
    )
    return jax.shard_map(
        shards, mesh=mesh, in_specs=placed, out_specs=P(("row", "col"), None), check_vma=False
    )
```

```python
import jax
import jax.numpy as jnp
from jax import lax
from jax.experimental import pallas as pl
from jax.experimental.pallas import tpu as pltpu
from jax.sharding import PartitionSpec as P

SWEEPS = 2
time_step = 0.25
PANEL = 64
HIGHEST = lax.Precision.HIGHEST


def bath_kernel(pattern_ref, bath_ref, own_ref, bathed_ref, gram_ref):
    bathed = jnp.dot(bath_ref[0], own_ref[...], preferred_element_type=jnp.float32).astype(jnp.bfloat16)
    bathed_ref[...] = bathed
    part = lax.dot_general(
        bathed, bathed, (((0,), (0,)), ((), ())), preferred_element_type=jnp.float32
    )

    @pl.when(pl.program_id(0) == 0)
    def _():
        gram_ref[...] = part

    @pl.when(pl.program_id(0) > 0)
    def _():
        gram_ref[...] += part


def bath_part(own, bath_pattern, bath_blocks):
    blocks = bath_pattern.shape[0]
    block_rows = bath_blocks.shape[1]
    rows, rank = own.shape
    tile = pl.BlockSpec((block_rows, rank), lambda b, kind: (b, 0))
    return pl.pallas_call(
        bath_kernel,
        grid_spec=pltpu.PrefetchScalarGridSpec(
            num_scalar_prefetch=1,
            grid=(blocks,),
            in_specs=[
                pl.BlockSpec((1, block_rows, block_rows), lambda b, kind: (kind[b], 0, 0)),
                tile,
            ],
            out_specs=[tile, pl.BlockSpec((rank, rank), lambda b, kind: (0, 0))],
        ),
        out_shape=[
            jax.ShapeDtypeStruct((rows, rank), jnp.bfloat16),
            jax.ShapeDtypeStruct((rank, rank), jnp.float32),
        ],
        compiler_params=pltpu.CompilerParams(vmem_limit_bytes=7 * 2**20),
        name="bath",
    )(bath_pattern, bath_blocks, own)


def gather_products(origin_ref, offset_ref, first_ref, count_ref, kind_ref, sources, coupling_ref, held, sems, total):
    blocks, slots = origin_ref.shape
    block_rows = held.shape[2]
    b = pl.program_id(0)
    group = 1
    while group * group < len(sources):
        group += 1

    def copy(source, block, slot):
        start = pl.multiple_of(offset_ref[block, slot] * block_rows, block_rows)
        return pltpu.make_async_copy(
            source.at[pl.ds(start, block_rows), :],
            held.at[lax.rem(block, 2), slot],
            sems.at[lax.rem(block, 2), slot],
        )

    def fetch(block):
        def one(slot, carry):
            origin = origin_ref[block, slot]
            for low in range(0, len(sources), group):
                high = min(low + group, len(sources))

                @pl.when((origin >= low) & (origin < high))
                def _():
                    for place in range(low, high):
                        @pl.when(origin == place)
                        def _():
                            copy(sources[place], block, slot).start()
            return carry

        lax.fori_loop(first_ref[block], first_ref[block] + count_ref[block], one, 0)

    @pl.when(b == 0)
    def _():
        fetch(0)

    @pl.when(b + 1 < blocks)
    def _():
        fetch(b + 1)

    def add(slot, carry):
        copy(sources[0], b, slot).wait()
        total[...] -= time_step * jnp.dot(
            coupling_ref[kind_ref[b, slot]],
            held[lax.rem(b, 2), slot],
            preferred_element_type=jnp.float32,
        )
        return carry

    lax.fori_loop(first_ref[b], first_ref[b] + count_ref[b], add, 0)


def early_kernel(origin_ref, offset_ref, first_ref, count_ref, kind_ref, *refs):
    sources = refs[:-8]
    coupling_hbm, own_ref, energy_ref, total_ref, coupling, held, sems, coupling_sem = refs[-8:]
    block_rows = own_ref.shape[0]
    load = pltpu.make_async_copy(coupling_hbm, coupling, coupling_sem)

    @pl.when(pl.program_id(0) == 0)
    def _():
        load.start()

    row = energy_ref[pl.ds(pl.program_id(0), 1), :]
    energy = jnp.broadcast_to(row, (8, block_rows)).T[:, :1]
    wide = own_ref[...].astype(jnp.float32)
    total_ref[...] = wide - time_step * (energy * wide)

    @pl.when(pl.program_id(0) == 0)
    def _():
        load.wait()

    gather_products(
        origin_ref, offset_ref, first_ref, count_ref, kind_ref, sources, coupling, held, sems, total_ref
    )


def late_kernel(origin_ref, offset_ref, first_ref, count_ref, kind_ref, *refs):
    sources = refs[:-8]
    coupling_ref, base_ref, bathed_ref, moved_ref, gram_ref, total, held, sems = refs[-8:]
    b = pl.program_id(0)
    total[...] = base_ref[...]
    gather_products(
        origin_ref, offset_ref, first_ref, count_ref, kind_ref, sources, coupling_ref, held, sems, total
    )
    moved = total[...].astype(jnp.bfloat16)
    moved_ref[...] = moved
    both = jnp.concatenate([moved, bathed_ref[...]], axis=1)
    part = lax.dot_general(
        moved, both, (((0,), (0,)), ((), ())), preferred_element_type=jnp.float32
    )

    @pl.when(b == 0)
    def _():
        gram_ref[...] = part

    @pl.when(b > 0)
    def _():
        gram_ref[...] += part


def early_part(lists, sources, coupling_blocks, own, onsite):
    blocks, slots = lists[0].shape
    kinds, block_rows, _ = coupling_blocks.shape
    rows, rank = own.shape
    tile = pl.BlockSpec((block_rows, rank), lambda b, *_: (b, 0))
    return pl.pallas_call(
        early_kernel,
        grid_spec=pltpu.PrefetchScalarGridSpec(
            num_scalar_prefetch=5,
            grid=(blocks,),
            in_specs=[
                *[pl.BlockSpec(memory_space=pltpu.HBM) for _ in sources],
                pl.BlockSpec(memory_space=pltpu.HBM),
                tile,
                pl.BlockSpec((blocks, block_rows), lambda b, *_: (0, 0)),
            ],
            out_specs=tile,
            scratch_shapes=[
                pltpu.VMEM((kinds, block_rows, block_rows), jnp.bfloat16),
                pltpu.VMEM((2, slots, block_rows, rank), jnp.bfloat16),
                pltpu.SemaphoreType.DMA((2, slots)),
                pltpu.SemaphoreType.DMA,
            ],
        ),
        out_shape=jax.ShapeDtypeStruct((rows, rank), jnp.float32),
        compiler_params=pltpu.CompilerParams(vmem_limit_bytes=10 * 2**20),
        cost_estimate=pl.CostEstimate(
            flops=blocks * slots * block_rows * block_rows * rank,
            bytes_accessed=blocks * slots * block_rows * rank * 2,
            transcendentals=0,
        ),
        name="couple_early",
    )(*lists, *sources, coupling_blocks, own, onsite.reshape(blocks, block_rows))


def late_part(lists, sources, coupling_blocks, base, bathed):
    blocks, slots = lists[0].shape
    kinds, block_rows, _ = coupling_blocks.shape
    rows, rank = base.shape
    tile = pl.BlockSpec((block_rows, rank), lambda b, *_: (b, 0))
    return pl.pallas_call(
        late_kernel,
        grid_spec=pltpu.PrefetchScalarGridSpec(
            num_scalar_prefetch=5,
            grid=(blocks,),
            in_specs=[
                *[pl.BlockSpec(memory_space=pl.ANY) for _ in sources],
                pl.BlockSpec((kinds, block_rows, block_rows), lambda b, *_: (0, 0, 0)),
                tile,
                tile,
            ],
            out_specs=[tile, pl.BlockSpec((rank, 2 * rank), lambda b, *_: (0, 0))],
            scratch_shapes=[
                pltpu.VMEM((block_rows, rank), jnp.float32),
                pltpu.VMEM((2, slots, block_rows, rank), jnp.bfloat16),
                pltpu.SemaphoreType.DMA((2, slots)),
            ],
        ),
        out_shape=[
            jax.ShapeDtypeStruct((rows, rank), jnp.bfloat16),
            jax.ShapeDtypeStruct((rank, 2 * rank), jnp.float32),
        ],
        compiler_params=pltpu.CompilerParams(vmem_limit_bytes=14 * 2**20),
        name="couple_late",
    )(*lists, *sources, coupling_blocks, base, bathed)


def inverse_factor(square):
    n = square.shape[0]
    eye = (
        lax.broadcasted_iota(jnp.int32, (n, n), 0) == lax.broadcasted_iota(jnp.int32, (n, n), 1)
    ).astype(jnp.float32)
    work = jnp.concatenate([square, eye], axis=1)
    bands = [work[8 * i : 8 * i + 8, :] for i in range(n // 8)]
    sublane = lax.broadcasted_iota(jnp.int32, (8, 2 * n), 0)
    def spread(band, g):
        return [jnp.broadcast_to(band[:, 8 * g + r : 8 * g + r + 1], (8, 2 * n)) for r in range(8)]

    out = []
    for g in range(n // 8):
        band = bands[g]
        pivots = spread(band, g)
        diagonal = jnp.zeros((8, 2 * n), jnp.float32)
        scales = []
        for r in range(8):
            scales.append(pl.reciprocal(pivots[r][r : r + 1, :], approx=True))
            diagonal = jnp.where(sublane == r, pivots[r], diagonal)
            share = jnp.where(sublane > r, pivots[r] * scales[r], 0.0)
            for q in range(r + 1, 8):
                pivots[q] = pivots[q] - share * pivots[q][r : r + 1, :]
            band = band - share * band[r : r + 1, :]
        out.append(band[:, n:] * lax.rsqrt(diagonal)[:, n:])
        for i in range(g + 1, n // 8):
            columns = spread(bands[i], g)
            below = bands[i]
            for r in range(8):
                share = columns[r] * scales[r]
                for q in range(r + 1, 8):
                    columns[q] = columns[q] - share * pivots[q][r : r + 1, :]
                below = below - share * band[r : r + 1, :]
            bands[i] = below
    return jnp.concatenate(out, axis=0)


def eliminate(inner, image):
    rank = inner.shape[0]

    def product(left, right, contract):
        return lax.dot_general(
            left, right, ((contract, (0,)), ((), ())),
            precision=HIGHEST, preferred_element_type=jnp.float32,
        )

    for low in range(0, rank, PANEL):
        high = low + PANEL
        here, first = low // 128 * 128, high // 128 * 128
        inverse = inverse_factor(inner[low:high, low:high])
        panel = product(inverse, inner[low:high, here:], (1,))
        inner[low:high, here:] = panel
        share = panel[:, high - here :]
        if high < rank:
            inner[high:, first:] -= product(share, panel[:, first - here :], (0,))
        side = product(inverse, image[low:high, :], (1,))
        image[low:high, :] = side
        if high < rank:
            image[high:, :] -= product(share, side, (0,))


def finish_kernel(
    order_ref, chunks_ref, moved_hbm, bathed_hbm, out_hbm,
    gram, inner, image, moved, bathed, out, in_sems, out_sems,
):
    rank = chunks_ref.shape[0]
    load_moved = pltpu.make_async_copy(moved_hbm, moved, in_sems.at[0])
    load_bathed = pltpu.make_async_copy(bathed_hbm, bathed, in_sems.at[1])
    load_moved.start()
    load_bathed.start()

    chunks = order_ref.shape[0]
    size = rank // chunks
    for i in range(chunks):
        rows = pl.ds(pl.multiple_of(order_ref[i] * size, size), size)
        chunk = chunks_ref[i * size : (i + 1) * size, :]
        gram[rows, :] = chunk[:, : 2 * rank]
        gram[pl.ds(pl.multiple_of(rank + order_ref[i] * size, size), size), rank:] = chunk[:, 2 * rank :]
    gram[rank:, :rank] = gram[:rank, rank:].T
    later = jnp.dot(gram[:rank, :], gram[...], precision=HIGHEST, preferred_element_type=jnp.float32)
    inner[...] = later[:, :rank]
    image[:, rank:] = later[:, rank:]
    for sweep in range(1, SWEEPS):
        eliminate(inner, image.at[:, rank:])
        upper = lax.broadcasted_iota(jnp.int32, (rank, rank), 0) <= lax.broadcasted_iota(jnp.int32, (rank, rank), 1)
        image[:, :rank] = jnp.where(upper, inner[...], 0.0)
        rows = image[...]
        inner[...] = lax.dot_general(
            rows, rows, (((1,), (1,)), ((), ())),
            precision=HIGHEST, preferred_element_type=jnp.float32,
        )
    eliminate(inner, image)
    rotation = image[...].T.astype(jnp.bfloat16)
    load_moved.wait()
    load_bathed.wait()
    pieces = out_sems.shape[0]
    size = moved.shape[0] // pieces

    def store(piece):
        rows = pl.ds(pl.multiple_of(piece * size, size), size)
        return pltpu.make_async_copy(out.at[rows, :], out_hbm.at[rows, :], out_sems.at[piece])

    def one(piece, carry):
        rows = pl.ds(pl.multiple_of(piece * size, size), size)
        stacked = jnp.concatenate([moved[rows, :], bathed[rows, :]], axis=1)
        value = jnp.dot(stacked, rotation, preferred_element_type=jnp.float32)
        out[rows, :] = value.astype(jnp.bfloat16)
        store(piece).start()
        return carry

    lax.fori_loop(0, pieces, one, 0)

    def drain(piece, carry):
        store(piece).wait()
        return carry

    lax.fori_loop(0, pieces, drain, 0)


def finish_part(order, chunks, moved, bathed):
    rows, rank = moved.shape
    return pl.pallas_call(
        finish_kernel,
        in_specs=[
            pl.BlockSpec(memory_space=pltpu.SMEM),
            pl.BlockSpec(memory_space=pltpu.VMEM),
            pl.BlockSpec(memory_space=pltpu.HBM),
            pl.BlockSpec(memory_space=pltpu.HBM),
        ],
        out_specs=pl.BlockSpec(memory_space=pl.ANY),
        out_shape=jax.ShapeDtypeStruct((rows, rank), jnp.bfloat16),
        scratch_shapes=[
            pltpu.VMEM((2 * rank, 2 * rank), jnp.float32),
            pltpu.VMEM((rank, rank), jnp.float32),
            pltpu.VMEM((rank, 2 * rank), jnp.float32),
            pltpu.VMEM((rows, rank), jnp.bfloat16),
            pltpu.VMEM((rows, rank), jnp.bfloat16),
            pltpu.VMEM((rows, rank), jnp.bfloat16),
            pltpu.SemaphoreType.DMA((2,)),
            pltpu.SemaphoreType.DMA((8,)),
        ],
        compiler_params=pltpu.CompilerParams(vmem_limit_bytes=14 * 2**20),
        name="finish",
    )(order, chunks, moved, bathed)


def ring_order(count):
    wide = 2
    while 4 * wide * wide <= count:
        wide *= 2
    tall = count // wide
    walk = [0]
    for r in range(tall):
        across = range(1, wide)
        walk += [r * wide + c for c in (across if r % 2 == 0 else reversed(across))]
    return walk + [r * wide for r in range(tall - 1, 0, -1)]


PIECES = 4


def tie(one, other):
    return lax.optimization_barrier((one, other))


def ring_gather(own, side, stages):
    order = ring_order(lax.axis_size("col"))
    following = order[1:] + order[:1]
    forward = list(zip(order, following))
    back = list(zip(following, order))
    size = own.shape[0] // PIECES
    pieces = [own[i * size : (i + 1) * size] for i in range(PIECES)]
    stages = list(stages)
    steps = []
    for step in range(1, len(order)):
        if step > 1:
            pieces[-1], side = tie(pieces[-1], side)
        pieces = [
            lax.ppermute(piece, "col", forward if i < PIECES // 2 else back)
            for i, piece in enumerate(pieces)
        ]
        if step > 1 and stages:
            side = stages.pop(0)(side)
        steps.append(list(pieces))
    for stage in stages:
        side = stage(side)
    return steps, side


def slot_lists(ids, counts, kinds):
    blocks, slots = ids.shape
    count = lax.axis_size("col")
    order = ring_order(count)
    place = jnp.asarray([order.index(c) for c in range(count)], jnp.int32)
    col = jnp.arange(count, dtype=jnp.int32)
    mine = jnp.sum(jnp.where(col == lax.axis_index("col"), place, 0))
    owner, within = ids // blocks, ids % blocks
    theirs = jnp.sum(jnp.where(owner[..., None] == col, place, 0), axis=-1)
    in_piece = blocks // PIECES
    piece = within // in_piece
    step = jnp.where(piece >= PIECES // 2, theirs - mine, mine - theirs) % count
    last = step == count - 1
    origin = jnp.where(last, piece, jnp.where(step == 0, 0, 1 + (step - 1) * PIECES + piece))
    offset = jnp.where(step == 0, within, within % in_piece)
    slot = jnp.arange(slots, dtype=jnp.int32)
    used = slot[None, :] < counts[:, None]
    key = jnp.where(used, jnp.where(last, slots, 0), 2 * slots) + slot
    rank = jnp.sum((key[:, None, :] < key[:, :, None]).astype(jnp.int32), axis=-1)
    at = rank[:, :, None] == slot
    def arrange(values):
        return jnp.sum(jnp.where(at, values[:, :, None], 0), axis=1)

    late = jnp.sum((used & last).astype(jnp.int32), axis=1)
    early = counts - late
    origin, offset, kinds = arrange(origin), arrange(offset), arrange(kinds)
    return (origin, offset, jnp.zeros_like(early), early, kinds), (origin, offset, early, late, kinds)


def swap(value, axis, stride):
    count = lax.axis_size(axis)
    return lax.ppermute(value, axis, [(i, i ^ stride) for i in range(count)])


def strides(axis):
    return [1 << i for i in range(lax.axis_size(axis).bit_length() - 1)]


def halvings():
    return [("row", stride) for stride in strides("row")] + [("col", 1)]


def side_of(axis, stride):
    return (lax.axis_index(axis) // stride) % 2


def halve(value, axis, stride):
    half = value.shape[0] // 2
    upper = side_of(axis, stride)
    keep = lax.dynamic_slice_in_dim(value, upper * half, half, 0)
    give = lax.dynamic_slice_in_dim(value, (1 - upper) * half, half, 0)
    return keep + swap(give, axis, stride)


def halve_over_row(value):
    for stride in strides("row"):
        value = halve(value, "row", stride)
    return value


def sum_relative(value):
    value = halve(value, "col", 1)
    for stride in strides("col")[1:]:
        value = value + swap(value, "col", stride)
    for axis, stride in reversed(halvings()):
        value = jnp.concatenate([value, swap(value, axis, stride)], axis=0)
    return value


def chunk_order():
    swaps = halvings()
    order = []
    for relative in range(1 << len(swaps)):
        part = 0
        for i, (axis, stride) in enumerate(swaps):
            height = len(swaps) - 1 - i
            part = part + (side_of(axis, stride) ^ ((relative >> height) & 1)) * (1 << height)
        order.append(part)
    return jnp.stack(order).astype(jnp.int32)


def shards(
    density_factor,
    onsite,
    neighbour_ids,
    neighbour_count,
    coupling_type,
    coupling_blocks,
    bath_pattern,
    bath_blocks,
):
    blocks, slots = neighbour_ids.shape
    group_blocks = lax.axis_size("col") * blocks
    in_group = neighbour_ids - lax.axis_index("row") * group_blocks
    early, late = slot_lists(in_group, neighbour_count, coupling_type)
    bathed, corner = bath_part(density_factor, bath_pattern, bath_blocks)
    steps, corner = ring_gather(density_factor, corner, [halve_over_row])
    ready = [density_factor] + [piece for step in steps[:-1] for piece in step]
    total = early_part(early, ready, coupling_blocks, density_factor, onsite)
    moved, upper = late_part(late, steps[-1], coupling_blocks, total, bathed)
    gram = sum_relative(jnp.concatenate([halve_over_row(upper), corner], axis=1))
    return finish_part(chunk_order(), gram, moved, bathed)


def solution(mesh):
    placed = (
        P(("row", "col"), None),
        P(("row", "col")),
        P(("row", "col"), None),
        P(("row", "col")),
        P(("row", "col"), None),
        P(),
        P(("row", "col")),
        P(),
    )
    return jax.shard_map(
        shards, mesh=mesh, in_specs=placed, out_specs=P(("row", "col"), None), check_vma=False
    )
```

```python
import jax
import jax.numpy as jnp
from jax import lax
from jax.experimental import pallas as pl
from jax.experimental.pallas import tpu as pltpu
from jax.sharding import PartitionSpec as P

SWEEPS = 2
time_step = 0.25
PANEL = 64
HIGHEST = lax.Precision.HIGHEST


def bath_kernel(pattern_ref, bath_ref, own_ref, bathed_ref, gram_ref):
    bathed = jnp.dot(bath_ref[0], own_ref[...], preferred_element_type=jnp.float32).astype(jnp.bfloat16)
    bathed_ref[...] = bathed
    part = lax.dot_general(
        bathed, bathed, (((0,), (0,)), ((), ())), preferred_element_type=jnp.float32
    )

    @pl.when(pl.program_id(0) == 0)
    def _():
        gram_ref[...] = part

    @pl.when(pl.program_id(0) > 0)
    def _():
        gram_ref[...] += part


def bath_part(own, bath_pattern, bath_blocks):
    blocks = bath_pattern.shape[0]
    block_rows = bath_blocks.shape[1]
    rows, rank = own.shape
    tile = pl.BlockSpec((block_rows, rank), lambda b, kind: (b, 0))
    return pl.pallas_call(
        bath_kernel,
        grid_spec=pltpu.PrefetchScalarGridSpec(
            num_scalar_prefetch=1,
            grid=(blocks,),
            in_specs=[
                pl.BlockSpec((1, block_rows, block_rows), lambda b, kind: (kind[b], 0, 0)),
                tile,
            ],
            out_specs=[tile, pl.BlockSpec((rank, rank), lambda b, kind: (0, 0))],
        ),
        out_shape=[
            jax.ShapeDtypeStruct((rows, rank), jnp.bfloat16),
            jax.ShapeDtypeStruct((rank, rank), jnp.float32),
        ],
        compiler_params=pltpu.CompilerParams(vmem_limit_bytes=7 * 2**20),
        name="bath",
    )(bath_pattern, bath_blocks, own)


def gather_products(origin_ref, offset_ref, first_ref, count_ref, kind_ref, sources, coupling_ref, held, sems, total):
    blocks, slots = origin_ref.shape
    block_rows = held.shape[2]
    b = pl.program_id(0)
    group = 1
    while group * group < len(sources):
        group += 1

    def copy(source, block, slot):
        start = pl.multiple_of(offset_ref[block, slot] * block_rows, block_rows)
        return pltpu.make_async_copy(
            source.at[pl.ds(start, block_rows), :],
            held.at[lax.rem(block, 2), slot],
            sems.at[lax.rem(block, 2), slot],
        )

    def fetch(block):
        def one(slot, carry):
            origin = origin_ref[block, slot]
            for low in range(0, len(sources), group):
                high = min(low + group, len(sources))

                @pl.when((origin >= low) & (origin < high))
                def _():
                    for place in range(low, high):
                        @pl.when(origin == place)
                        def _():
                            copy(sources[place], block, slot).start()
            return carry

        lax.fori_loop(first_ref[block], first_ref[block] + count_ref[block], one, 0)

    @pl.when(b == 0)
    def _():
        fetch(0)

    @pl.when(b + 1 < blocks)
    def _():
        fetch(b + 1)

    def add(slot, carry):
        copy(sources[0], b, slot).wait()
        total[...] -= time_step * jnp.dot(
            coupling_ref[kind_ref[b, slot]],
            held[lax.rem(b, 2), slot],
            preferred_element_type=jnp.float32,
        )
        return carry

    lax.fori_loop(first_ref[b], first_ref[b] + count_ref[b], add, 0)


def early_kernel(origin_ref, offset_ref, first_ref, count_ref, kind_ref, *refs):
    sources = refs[:-8]
    coupling_hbm, own_ref, energy_ref, total_ref, coupling, held, sems, coupling_sem = refs[-8:]
    block_rows = own_ref.shape[0]
    load = pltpu.make_async_copy(coupling_hbm, coupling, coupling_sem)

    @pl.when(pl.program_id(0) == 0)
    def _():
        load.start()

    row = energy_ref[pl.ds(pl.program_id(0), 1), :]
    energy = jnp.broadcast_to(row, (8, block_rows)).T[:, :1]
    wide = own_ref[...].astype(jnp.float32)
    total_ref[...] = wide - time_step * (energy * wide)

    @pl.when(pl.program_id(0) == 0)
    def _():
        load.wait()

    gather_products(
        origin_ref, offset_ref, first_ref, count_ref, kind_ref, sources, coupling, held, sems, total_ref
    )


def late_kernel(origin_ref, offset_ref, first_ref, count_ref, kind_ref, *refs):
    sources = refs[:-8]
    coupling_ref, base_ref, bathed_ref, moved_ref, gram_ref, total, held, sems = refs[-8:]
    b = pl.program_id(0)
    total[...] = base_ref[...]
    gather_products(
        origin_ref, offset_ref, first_ref, count_ref, kind_ref, sources, coupling_ref, held, sems, total
    )
    moved = total[...].astype(jnp.bfloat16)
    moved_ref[...] = moved
    both = jnp.concatenate([moved, bathed_ref[...]], axis=1)
    part = lax.dot_general(
        moved, both, (((0,), (0,)), ((), ())), preferred_element_type=jnp.float32
    )

    @pl.when(b == 0)
    def _():
        gram_ref[...] = part

    @pl.when(b > 0)
    def _():
        gram_ref[...] += part


def early_part(lists, sources, coupling_blocks, own, energy):
    blocks, slots = lists[0].shape
    kinds, block_rows, _ = coupling_blocks.shape
    rows, rank = own.shape
    tile = pl.BlockSpec((block_rows, rank), lambda b, *_: (b, 0))
    return pl.pallas_call(
        early_kernel,
        grid_spec=pltpu.PrefetchScalarGridSpec(
            num_scalar_prefetch=5,
            grid=(blocks,),
            in_specs=[
                *[pl.BlockSpec(memory_space=pltpu.HBM) for _ in sources],
                pl.BlockSpec(memory_space=pltpu.HBM),
                tile,
                pl.BlockSpec((blocks, block_rows), lambda b, *_: (0, 0)),
            ],
            out_specs=tile,
            scratch_shapes=[
                pltpu.VMEM((kinds, block_rows, block_rows), jnp.bfloat16),
                pltpu.VMEM((2, slots, block_rows, rank), jnp.bfloat16),
                pltpu.SemaphoreType.DMA((2, slots)),
                pltpu.SemaphoreType.DMA,
            ],
        ),
        out_shape=jax.ShapeDtypeStruct((rows, rank), jnp.float32),
        compiler_params=pltpu.CompilerParams(vmem_limit_bytes=10 * 2**20),
        cost_estimate=pl.CostEstimate(
            flops=blocks * slots * block_rows * block_rows * rank,
            bytes_accessed=blocks * slots * block_rows * rank * 2,
            transcendentals=0,
        ),
        name="couple_early",
    )(*lists, *sources, coupling_blocks, own, energy)


def late_part(lists, sources, coupling_blocks, base, bathed):
    blocks, slots = lists[0].shape
    kinds, block_rows, _ = coupling_blocks.shape
    rows, rank = base.shape
    tile = pl.BlockSpec((block_rows, rank), lambda b, *_: (b, 0))
    return pl.pallas_call(
        late_kernel,
        grid_spec=pltpu.PrefetchScalarGridSpec(
            num_scalar_prefetch=5,
            grid=(blocks,),
            in_specs=[
                *[pl.BlockSpec(memory_space=pl.ANY) for _ in sources],
                pl.BlockSpec((kinds, block_rows, block_rows), lambda b, *_: (0, 0, 0)),
                tile,
                tile,
            ],
            out_specs=[tile, pl.BlockSpec((rank, 2 * rank), lambda b, *_: (0, 0))],
            scratch_shapes=[
                pltpu.VMEM((block_rows, rank), jnp.float32),
                pltpu.VMEM((2, slots, block_rows, rank), jnp.bfloat16),
                pltpu.SemaphoreType.DMA((2, slots)),
            ],
        ),
        out_shape=[
            jax.ShapeDtypeStruct((rows, rank), jnp.bfloat16),
            jax.ShapeDtypeStruct((rank, 2 * rank), jnp.float32),
        ],
        compiler_params=pltpu.CompilerParams(vmem_limit_bytes=14 * 2**20),
        name="couple_late",
    )(*lists, *sources, coupling_blocks, base, bathed)


def inverse_factor(square):
    n = square.shape[0]
    eye = (
        lax.broadcasted_iota(jnp.int32, (n, n), 0) == lax.broadcasted_iota(jnp.int32, (n, n), 1)
    ).astype(jnp.float32)
    work = jnp.concatenate([square, eye], axis=1)
    bands = [work[8 * i : 8 * i + 8, :] for i in range(n // 8)]
    sublane = lax.broadcasted_iota(jnp.int32, (8, 2 * n), 0)
    def spread(band, g):
        return [jnp.broadcast_to(band[:, 8 * g + r : 8 * g + r + 1], (8, 2 * n)) for r in range(8)]

    out = []
    for g in range(n // 8):
        band = bands[g]
        pivots = spread(band, g)
        diagonal = jnp.zeros((8, 2 * n), jnp.float32)
        scales = []
        for r in range(8):
            scales.append(pl.reciprocal(pivots[r][r : r + 1, :], approx=True))
            diagonal = jnp.where(sublane == r, pivots[r], diagonal)
            share = jnp.where(sublane > r, pivots[r] * scales[r], 0.0)
            for q in range(r + 1, 8):
                pivots[q] = pivots[q] - share * pivots[q][r : r + 1, :]
            band = band - share * band[r : r + 1, :]
        out.append(band[:, n:] * lax.rsqrt(diagonal)[:, n:])
        for i in range(g + 1, n // 8):
            columns = spread(bands[i], g)
            below = bands[i]
            for r in range(8):
                share = columns[r] * scales[r]
                for q in range(r + 1, 8):
                    columns[q] = columns[q] - share * pivots[q][r : r + 1, :]
                below = below - share * band[r : r + 1, :]
            bands[i] = below
    return jnp.concatenate(out, axis=0)


def eliminate(inner, image):
    rank = inner.shape[0]

    def product(left, right, contract):
        return lax.dot_general(
            left, right, ((contract, (0,)), ((), ())),
            precision=HIGHEST, preferred_element_type=jnp.float32,
        )

    for low in range(0, rank, PANEL):
        high = low + PANEL
        here, first = low // 128 * 128, high // 128 * 128
        inverse = inverse_factor(inner[low:high, low:high])
        panel = product(inverse, inner[low:high, here:], (1,))
        inner[low:high, here:] = panel
        share = panel[:, high - here :]
        if high < rank:
            inner[high:, first:] -= product(share, panel[:, first - here :], (0,))
        side = product(inverse, image[low:high, :], (1,))
        image[low:high, :] = side
        if high < rank:
            image[high:, :] -= product(share, side, (0,))


def finish_kernel(
    order_ref, chunks_ref, moved_hbm, bathed_hbm, out_hbm,
    gram, inner, image, moved, bathed, out, in_sems, out_sems,
):
    rank = chunks_ref.shape[0]
    load_moved = pltpu.make_async_copy(moved_hbm, moved, in_sems.at[0])
    load_bathed = pltpu.make_async_copy(bathed_hbm, bathed, in_sems.at[1])
    load_moved.start()
    load_bathed.start()

    chunks = order_ref.shape[0]
    size = rank // chunks
    for i in range(chunks):
        rows = pl.ds(pl.multiple_of(order_ref[i] * size, size), size)
        chunk = chunks_ref[i * size : (i + 1) * size, :]
        gram[rows, :] = chunk[:, : 2 * rank]
        gram[pl.ds(pl.multiple_of(rank + order_ref[i] * size, size), size), rank:] = chunk[:, 2 * rank :]
    gram[rank:, :rank] = gram[:rank, rank:].T
    later = jnp.dot(gram[:rank, :], gram[...], precision=HIGHEST, preferred_element_type=jnp.float32)
    inner[...] = later[:, :rank]
    image[:, rank:] = later[:, rank:]
    for sweep in range(1, SWEEPS):
        eliminate(inner, image.at[:, rank:])
        upper = lax.broadcasted_iota(jnp.int32, (rank, rank), 0) <= lax.broadcasted_iota(jnp.int32, (rank, rank), 1)
        image[:, :rank] = jnp.where(upper, inner[...], 0.0)
        rows = image[...]
        inner[...] = lax.dot_general(
            rows, rows, (((1,), (1,)), ((), ())),
            precision=HIGHEST, preferred_element_type=jnp.float32,
        )
    eliminate(inner, image)
    rotation = image[...].T.astype(jnp.bfloat16)
    load_moved.wait()
    load_bathed.wait()
    pieces = out_sems.shape[0]
    size = moved.shape[0] // pieces

    def store(piece):
        rows = pl.ds(pl.multiple_of(piece * size, size), size)
        return pltpu.make_async_copy(out.at[rows, :], out_hbm.at[rows, :], out_sems.at[piece])

    def one(piece, carry):
        rows = pl.ds(pl.multiple_of(piece * size, size), size)
        stacked = jnp.concatenate([moved[rows, :], bathed[rows, :]], axis=1)
        value = jnp.dot(stacked, rotation, preferred_element_type=jnp.float32)
        out[rows, :] = value.astype(jnp.bfloat16)
        store(piece).start()
        return carry

    lax.fori_loop(0, pieces, one, 0)

    def drain(piece, carry):
        store(piece).wait()
        return carry

    lax.fori_loop(0, pieces, drain, 0)


def finish_part(order, chunks, moved, bathed):
    rows, rank = moved.shape
    return pl.pallas_call(
        finish_kernel,
        in_specs=[
            pl.BlockSpec(memory_space=pltpu.SMEM),
            pl.BlockSpec(memory_space=pltpu.VMEM),
            pl.BlockSpec(memory_space=pltpu.HBM),
            pl.BlockSpec(memory_space=pltpu.HBM),
        ],
        out_specs=pl.BlockSpec(memory_space=pl.ANY),
        out_shape=jax.ShapeDtypeStruct((rows, rank), jnp.bfloat16),
        scratch_shapes=[
            pltpu.VMEM((2 * rank, 2 * rank), jnp.float32),
            pltpu.VMEM((rank, rank), jnp.float32),
            pltpu.VMEM((rank, 2 * rank), jnp.float32),
            pltpu.VMEM((rows, rank), jnp.bfloat16),
            pltpu.VMEM((rows, rank), jnp.bfloat16),
            pltpu.VMEM((rows, rank), jnp.bfloat16),
            pltpu.SemaphoreType.DMA((2,)),
            pltpu.SemaphoreType.DMA((8,)),
        ],
        compiler_params=pltpu.CompilerParams(vmem_limit_bytes=14 * 2**20),
        name="finish",
    )(order, chunks, moved, bathed)


def ring_order(count):
    wide = 2
    while 4 * wide * wide <= count:
        wide *= 2
    tall = count // wide
    walk = [0]
    for r in range(tall):
        across = range(1, wide)
        walk += [r * wide + c for c in (across if r % 2 == 0 else reversed(across))]
    return walk + [r * wide for r in range(tall - 1, 0, -1)]


PIECES = 4


def tie(one, other):
    return lax.optimization_barrier((one, other))


def ring_gather(own, side, stages, small):
    order = ring_order(lax.axis_size("col"))
    following = order[1:] + order[:1]
    forward = list(zip(order, following))
    back = list(zip(following, order))
    size = own.shape[0] // PIECES
    pieces = [own[i * size : (i + 1) * size] for i in range(PIECES)]
    stages = list(stages)
    steps = []
    for step in range(1, len(order)):
        if step > 1:
            pieces[-1], side = tie(pieces[-1], side)
        if step == 3:
            pieces[-1], small = tie(pieces[-1], small)
        pieces = [
            lax.ppermute(piece, "col", forward if i < PIECES // 2 else back)
            for i, piece in enumerate(pieces)
        ]
        if step > 1 and stages:
            side = stages.pop(0)(side)
        steps.append(list(pieces))
    for stage in stages:
        side = stage(side)
    return steps, side, small


def slot_lists(ids, counts, kinds):
    blocks, slots = ids.shape
    count = lax.axis_size("col")
    order = ring_order(count)
    place = jnp.asarray([order.index(c) for c in range(count)], jnp.int32)
    col = jnp.arange(count, dtype=jnp.int32)
    mine = jnp.sum(jnp.where(col == lax.axis_index("col"), place, 0))
    owner, within = ids // blocks, ids % blocks
    theirs = jnp.sum(jnp.where(owner[..., None] == col, place, 0), axis=-1)
    in_piece = blocks // PIECES
    piece = within // in_piece
    step = jnp.where(piece >= PIECES // 2, theirs - mine, mine - theirs) % count
    last = step == count - 1
    origin = jnp.where(last, piece, jnp.where(step == 0, 0, 1 + (step - 1) * PIECES + piece))
    offset = jnp.where(step == 0, within, within % in_piece)
    slot = jnp.arange(slots, dtype=jnp.int32)
    used = slot[None, :] < counts[:, None]
    key = jnp.where(used, jnp.where(last, slots, 0), 2 * slots) + slot
    rank = jnp.sum((key[:, None, :] < key[:, :, None]).astype(jnp.int32), axis=-1)
    at = rank[:, :, None] == slot
    def arrange(values):
        return jnp.sum(jnp.where(at, values[:, :, None], 0), axis=1)

    late = jnp.sum((used & last).astype(jnp.int32), axis=1)
    early = counts - late
    origin, offset, kinds = arrange(origin), arrange(offset), arrange(kinds)
    return (origin, offset, jnp.zeros_like(early), early, kinds), (origin, offset, early, late, kinds)


def swap(value, axis, stride):
    count = lax.axis_size(axis)
    return lax.ppermute(value, axis, [(i, i ^ stride) for i in range(count)])


def strides(axis):
    return [1 << i for i in range(lax.axis_size(axis).bit_length() - 1)]


def halvings():
    return [("row", stride) for stride in strides("row")] + [("col", 1)]


def side_of(axis, stride):
    return (lax.axis_index(axis) >> (stride.bit_length() - 1)) & 1


def halve(value, swapped, lower):
    half = value.shape[0] // 2
    keep = jnp.where(lower, value[:half], value[half:])
    give = jnp.where(lower, value[half:], value[:half])
    return keep + swap(give, *swapped)


def sum_relative(value, lower):
    value = halve(value, ("col", 1), lower)
    for stride in strides("col")[1:]:
        value = value + swap(value, "col", stride)
    for axis, stride in reversed(halvings()):
        value = jnp.concatenate([value, swap(value, axis, stride)], axis=0)
    return value


def chunk_order():
    swaps = halvings()
    relative = jnp.arange(1 << len(swaps), dtype=jnp.int32)
    mine = jnp.zeros_like(relative)
    for i, (axis, stride) in enumerate(swaps):
        mine = mine + (side_of(axis, stride) << (len(swaps) - 1 - i))
    return relative ^ mine


def shards(
    density_factor,
    onsite,
    neighbour_ids,
    neighbour_count,
    coupling_type,
    coupling_blocks,
    bath_pattern,
    bath_blocks,
):
    blocks, slots = neighbour_ids.shape
    group_blocks = lax.axis_size("col") * blocks
    in_group = neighbour_ids - lax.axis_index("row") * group_blocks
    early, late = slot_lists(in_group, neighbour_count, coupling_type)
    bathed, corner = bath_part(density_factor, bath_pattern, bath_blocks)
    energy = onsite.reshape(blocks, -1)
    swaps = halvings()
    lower = [side_of(axis, stride) == 0 for axis, stride in swaps]

    def over_row(value, lower):
        for swapped, chosen in zip(swaps[:-1], lower):
            value = halve(value, swapped, chosen)
        return value

    steps, corner, small = ring_gather(
        density_factor,
        corner,
        [lambda value: over_row(value, lower)],
        (early, late, energy, chunk_order(), lower),
    )
    early, late, energy, order, lower = small
    ready = [density_factor] + [piece for step in steps[:-1] for piece in step]
    total = early_part(early, ready, coupling_blocks, density_factor, energy)
    moved, upper = late_part(late, steps[-1], coupling_blocks, total, bathed)
    gram = jnp.concatenate([over_row(upper, lower), corner], axis=1)
    return finish_part(order, sum_relative(gram, lower[-1]), moved, bathed)


def solution(mesh):
    placed = (
        P(("row", "col"), None),
        P(("row", "col")),
        P(("row", "col"), None),
        P(("row", "col")),
        P(("row", "col"), None),
        P(),
        P(("row", "col")),
        P(),
    )
    return jax.shard_map(
        shards, mesh=mesh, in_specs=placed, out_specs=P(("row", "col"), None), check_vma=False
    )
```

```python
import jax
import jax.numpy as jnp
from jax import lax
from jax.experimental import pallas as pl
from jax.experimental.pallas import tpu as pltpu
from jax.sharding import PartitionSpec as P

time_step = 0.25
PANEL = 64
SMALLEST_PIVOT = 1 / 64
HIGHEST = lax.Precision.HIGHEST


def bath_kernel(pattern_ref, bath_ref, own_ref, bathed_ref, gram_ref):
    bathed = jnp.dot(bath_ref[0], own_ref[...], preferred_element_type=jnp.float32).astype(jnp.bfloat16)
    bathed_ref[...] = bathed
    part = lax.dot_general(
        bathed, bathed, (((0,), (0,)), ((), ())), preferred_element_type=jnp.float32
    )

    @pl.when(pl.program_id(0) == 0)
    def _():
        gram_ref[...] = part

    @pl.when(pl.program_id(0) > 0)
    def _():
        gram_ref[...] += part


def bath_part(own, bath_pattern, bath_blocks):
    blocks = bath_pattern.shape[0]
    block_rows = bath_blocks.shape[1]
    rows, rank = own.shape
    tile = pl.BlockSpec((block_rows, rank), lambda b, kind: (b, 0))
    return pl.pallas_call(
        bath_kernel,
        grid_spec=pltpu.PrefetchScalarGridSpec(
            num_scalar_prefetch=1,
            grid=(blocks,),
            in_specs=[
                pl.BlockSpec((1, block_rows, block_rows), lambda b, kind: (kind[b], 0, 0)),
                tile,
            ],
            out_specs=[tile, pl.BlockSpec((rank, rank), lambda b, kind: (0, 0))],
        ),
        out_shape=[
            jax.ShapeDtypeStruct((rows, rank), jnp.bfloat16),
            jax.ShapeDtypeStruct((rank, rank), jnp.float32),
        ],
        compiler_params=pltpu.CompilerParams(vmem_limit_bytes=7 * 2**20),
        name="bath",
    )(bath_pattern, bath_blocks, own)


def gather_products(origin_ref, offset_ref, first_ref, count_ref, kind_ref, sources, coupling_ref, held, sems, total):
    blocks, slots = origin_ref.shape
    block_rows = held.shape[2]
    b = pl.program_id(0)
    group = 1
    while group * group < len(sources):
        group += 1

    def copy(source, block, slot):
        start = pl.multiple_of(offset_ref[block, slot] * block_rows, block_rows)
        return pltpu.make_async_copy(
            source.at[pl.ds(start, block_rows), :],
            held.at[lax.rem(block, 2), slot],
            sems.at[lax.rem(block, 2), slot],
        )

    def fetch(block):
        def one(slot, carry):
            origin = origin_ref[block, slot]
            for low in range(0, len(sources), group):
                high = min(low + group, len(sources))

                @pl.when((origin >= low) & (origin < high))
                def _():
                    for place in range(low, high):
                        @pl.when(origin == place)
                        def _():
                            copy(sources[place], block, slot).start()
            return carry

        lax.fori_loop(first_ref[block], first_ref[block] + count_ref[block], one, 0)

    @pl.when(b == 0)
    def _():
        fetch(0)

    @pl.when(b + 1 < blocks)
    def _():
        fetch(b + 1)

    def add(slot, carry):
        copy(sources[0], b, slot).wait()
        total[...] -= time_step * jnp.dot(
            coupling_ref[kind_ref[b, slot]],
            held[lax.rem(b, 2), slot],
            preferred_element_type=jnp.float32,
        )
        return carry

    lax.fori_loop(first_ref[b], first_ref[b] + count_ref[b], add, 0)


def early_kernel(origin_ref, offset_ref, first_ref, count_ref, kind_ref, *refs):
    sources = refs[:-8]
    coupling_hbm, own_ref, energy_ref, total_ref, coupling, held, sems, coupling_sem = refs[-8:]
    block_rows = own_ref.shape[0]
    load = pltpu.make_async_copy(coupling_hbm, coupling, coupling_sem)

    @pl.when(pl.program_id(0) == 0)
    def _():
        load.start()

    row = energy_ref[pl.ds(pl.program_id(0), 1), :]
    energy = jnp.broadcast_to(row, (8, block_rows)).T[:, :1]
    wide = own_ref[...].astype(jnp.float32)
    total_ref[...] = wide - time_step * (energy * wide)

    @pl.when(pl.program_id(0) == 0)
    def _():
        load.wait()

    gather_products(
        origin_ref, offset_ref, first_ref, count_ref, kind_ref, sources, coupling, held, sems, total_ref
    )


def late_kernel(origin_ref, offset_ref, first_ref, count_ref, kind_ref, *refs):
    sources = refs[:-8]
    coupling_ref, base_ref, bathed_ref, moved_ref, gram_ref, total, held, sems = refs[-8:]
    b = pl.program_id(0)
    total[...] = base_ref[...]
    gather_products(
        origin_ref, offset_ref, first_ref, count_ref, kind_ref, sources, coupling_ref, held, sems, total
    )
    moved = total[...].astype(jnp.bfloat16)
    moved_ref[...] = moved
    both = jnp.concatenate([moved, bathed_ref[...]], axis=1)
    part = lax.dot_general(
        moved, both, (((0,), (0,)), ((), ())), preferred_element_type=jnp.float32
    )

    @pl.when(b == 0)
    def _():
        gram_ref[...] = part

    @pl.when(b > 0)
    def _():
        gram_ref[...] += part


def early_part(lists, sources, coupling_blocks, own, energy):
    blocks, slots = lists[0].shape
    kinds, block_rows, _ = coupling_blocks.shape
    rows, rank = own.shape
    tile = pl.BlockSpec((block_rows, rank), lambda b, *_: (b, 0))
    return pl.pallas_call(
        early_kernel,
        grid_spec=pltpu.PrefetchScalarGridSpec(
            num_scalar_prefetch=5,
            grid=(blocks,),
            in_specs=[
                *[pl.BlockSpec(memory_space=pltpu.HBM) for _ in sources],
                pl.BlockSpec(memory_space=pltpu.HBM),
                tile,
                pl.BlockSpec((blocks, block_rows), lambda b, *_: (0, 0)),
            ],
            out_specs=tile,
            scratch_shapes=[
                pltpu.VMEM((kinds, block_rows, block_rows), jnp.bfloat16),
                pltpu.VMEM((2, slots, block_rows, rank), jnp.bfloat16),
                pltpu.SemaphoreType.DMA((2, slots)),
                pltpu.SemaphoreType.DMA,
            ],
        ),
        out_shape=jax.ShapeDtypeStruct((rows, rank), jnp.float32),
        compiler_params=pltpu.CompilerParams(vmem_limit_bytes=10 * 2**20),
        cost_estimate=pl.CostEstimate(
            flops=blocks * slots * block_rows * block_rows * rank,
            bytes_accessed=blocks * slots * block_rows * rank * 2,
            transcendentals=0,
        ),
        name="couple_early",
    )(*lists, *sources, coupling_blocks, own, energy)


def late_part(lists, sources, coupling_blocks, base, bathed):
    blocks, slots = lists[0].shape
    kinds, block_rows, _ = coupling_blocks.shape
    rows, rank = base.shape
    tile = pl.BlockSpec((block_rows, rank), lambda b, *_: (b, 0))
    return pl.pallas_call(
        late_kernel,
        grid_spec=pltpu.PrefetchScalarGridSpec(
            num_scalar_prefetch=5,
            grid=(blocks,),
            in_specs=[
                *[pl.BlockSpec(memory_space=pl.ANY) for _ in sources],
                pl.BlockSpec((kinds, block_rows, block_rows), lambda b, *_: (0, 0, 0)),
                tile,
                tile,
            ],
            out_specs=[tile, pl.BlockSpec((rank, 2 * rank), lambda b, *_: (0, 0))],
            scratch_shapes=[
                pltpu.VMEM((block_rows, rank), jnp.float32),
                pltpu.VMEM((2, slots, block_rows, rank), jnp.bfloat16),
                pltpu.SemaphoreType.DMA((2, slots)),
            ],
        ),
        out_shape=[
            jax.ShapeDtypeStruct((rows, rank), jnp.bfloat16),
            jax.ShapeDtypeStruct((rank, 2 * rank), jnp.float32),
        ],
        compiler_params=pltpu.CompilerParams(vmem_limit_bytes=14 * 2**20),
        name="couple_late",
    )(*lists, *sources, coupling_blocks, base, bathed)


def inverse_factor(square, start, lowest):
    n = square.shape[0]
    eye = (
        lax.broadcasted_iota(jnp.int32, (n, n), 0) == lax.broadcasted_iota(jnp.int32, (n, n), 1)
    ).astype(jnp.float32)
    work = jnp.concatenate([square, eye], axis=1)
    bands = [work[8 * i : 8 * i + 8, :] for i in range(n // 8)]
    sublane = lax.broadcasted_iota(jnp.int32, (8, 2 * n), 0)
    def spread(band, g):
        return [jnp.broadcast_to(band[:, 8 * g + r : 8 * g + r + 1], (8, 2 * n)) for r in range(8)]

    out = []
    for g in range(n // 8):
        band = bands[g]
        pivots = spread(band, g)
        diagonal = jnp.zeros((8, 2 * n), jnp.float32)
        scales = []
        for r in range(8):
            scales.append(pl.reciprocal(pivots[r][r : r + 1, :], approx=True))
            diagonal = jnp.where(sublane == r, pivots[r], diagonal)
            share = jnp.where(sublane > r, pivots[r] * scales[r], 0.0)
            for q in range(r + 1, 8):
                pivots[q] = pivots[q] - share * pivots[q][r : r + 1, :]
            band = band - share * band[r : r + 1, :]
        out.append(band[:, n:] * lax.rsqrt(diagonal)[:, n:])
        lowest[...] = jnp.minimum(lowest[...], diagonal / start[8 * g : 8 * g + 8, :])
        for i in range(g + 1, n // 8):
            columns = spread(bands[i], g)
            below = bands[i]
            for r in range(8):
                share = columns[r] * scales[r]
                for q in range(r + 1, 8):
                    columns[q] = columns[q] - share * pivots[q][r : r + 1, :]
                below = below - share * band[r : r + 1, :]
            bands[i] = below
    return jnp.concatenate(out, axis=0)


def eliminate(inner, image, start, lowest):
    rank = inner.shape[0]
    diagonal = lax.broadcasted_iota(jnp.int32, (rank, rank), 0) == lax.broadcasted_iota(jnp.int32, (rank, rank), 1)
    start[...] = jnp.broadcast_to(
        jnp.sum(jnp.where(diagonal, inner[...], 0.0), axis=1, keepdims=True), start.shape
    )
    lowest[...] = jnp.ones_like(lowest)

    def product(left, right, contract):
        return lax.dot_general(
            left, right, ((contract, (0,)), ((), ())),
            precision=HIGHEST, preferred_element_type=jnp.float32,
        )

    for low in range(0, rank, PANEL):
        high = low + PANEL
        here, first = low // 128 * 128, high // 128 * 128
        inverse = inverse_factor(inner[low:high, low:high], start[low:high, :], lowest)
        panel = product(inverse, inner[low:high, here:], (1,))
        inner[low:high, here:] = panel
        share = panel[:, high - here :]
        if high < rank:
            inner[high:, first:] -= product(share, panel[:, first - here :], (0,))
        side = product(inverse, image[low:high, :], (1,))
        image[low:high, :] = side
        if high < rank:
            image[high:, :] -= product(share, side, (0,))


def finish_kernel(
    order_ref, chunks_ref, moved_hbm, bathed_hbm, out_hbm,
    gram, inner, image, start, lowest, moved, bathed, out, in_sems, out_sems,
):
    rank = chunks_ref.shape[0]
    load_moved = pltpu.make_async_copy(moved_hbm, moved, in_sems.at[0])
    load_bathed = pltpu.make_async_copy(bathed_hbm, bathed, in_sems.at[1])
    load_moved.start()
    load_bathed.start()

    chunks = order_ref.shape[0]
    size = rank // chunks
    for i in range(chunks):
        rows = pl.ds(pl.multiple_of(order_ref[i] * size, size), size)
        chunk = chunks_ref[i * size : (i + 1) * size, :]
        gram[rows, :] = chunk[:, : 2 * rank]
        gram[pl.ds(pl.multiple_of(rank + order_ref[i] * size, size), size), rank:] = chunk[:, 2 * rank :]
    gram[rank:, :rank] = gram[:rank, rank:].T
    largest = jnp.max(jnp.max(jnp.abs(gram[...]), axis=0, keepdims=True), axis=1, keepdims=True)
    gram[...] = gram[...] * (1.0 / largest)
    product = jnp.dot(gram[:rank, :], gram[...], precision=HIGHEST, preferred_element_type=jnp.float32)

    def inner_product():
        rows = image[...]
        inner[...] = lax.dot_general(
            rows, rows, (((1,), (1,)), ((), ())),
            precision=HIGHEST, preferred_element_type=jnp.float32,
        )

    image[...] = product
    inner_product()
    eliminate(inner, image, start, lowest)
    safe = jnp.min(lowest[...]) >= SMALLEST_PIVOT

    @pl.when(jnp.logical_not(safe))
    def _():
        later = jnp.dot(gram[:rank, :], gram[...], precision=HIGHEST, preferred_element_type=jnp.float32)
        inner[...] = later[:, :rank]
        image[:, rank:] = later[:, rank:]
        eliminate(inner, image.at[:, rank:], start, lowest)
        upper = lax.broadcasted_iota(jnp.int32, (rank, rank), 0) <= lax.broadcasted_iota(jnp.int32, (rank, rank), 1)
        image[:, :rank] = jnp.where(upper, inner[...], 0.0)
        inner_product()
        eliminate(inner, image, start, lowest)

    rotation = image[...].T.astype(jnp.bfloat16)
    load_moved.wait()
    load_bathed.wait()
    pieces = out_sems.shape[0]
    size = moved.shape[0] // pieces

    def store(piece):
        rows = pl.ds(pl.multiple_of(piece * size, size), size)
        return pltpu.make_async_copy(out.at[rows, :], out_hbm.at[rows, :], out_sems.at[piece])

    def one(piece, carry):
        rows = pl.ds(pl.multiple_of(piece * size, size), size)
        stacked = jnp.concatenate([moved[rows, :], bathed[rows, :]], axis=1)
        value = jnp.dot(stacked, rotation, preferred_element_type=jnp.float32)
        out[rows, :] = value.astype(jnp.bfloat16)
        store(piece).start()
        return carry

    lax.fori_loop(0, pieces, one, 0)

    def drain(piece, carry):
        store(piece).wait()
        return carry

    lax.fori_loop(0, pieces, drain, 0)


def finish_part(order, chunks, moved, bathed):
    rows, rank = moved.shape
    return pl.pallas_call(
        finish_kernel,
        in_specs=[
            pl.BlockSpec(memory_space=pltpu.SMEM),
            pl.BlockSpec(memory_space=pltpu.VMEM),
            pl.BlockSpec(memory_space=pltpu.HBM),
            pl.BlockSpec(memory_space=pltpu.HBM),
        ],
        out_specs=pl.BlockSpec(memory_space=pl.ANY),
        out_shape=jax.ShapeDtypeStruct((rows, rank), jnp.bfloat16),
        scratch_shapes=[
            pltpu.VMEM((2 * rank, 2 * rank), jnp.float32),
            pltpu.VMEM((rank, rank), jnp.float32),
            pltpu.VMEM((rank, 2 * rank), jnp.float32),
            pltpu.VMEM((rank, 2 * PANEL), jnp.float32),
            pltpu.VMEM((8, 2 * PANEL), jnp.float32),
            pltpu.VMEM((rows, rank), jnp.bfloat16),
            pltpu.VMEM((rows, rank), jnp.bfloat16),
            pltpu.VMEM((rows, rank), jnp.bfloat16),
            pltpu.SemaphoreType.DMA((2,)),
            pltpu.SemaphoreType.DMA((8,)),
        ],
        compiler_params=pltpu.CompilerParams(vmem_limit_bytes=14 * 2**20),
        name="finish",
    )(order, chunks, moved, bathed)


def ring_order(count):
    wide = 2
    while 4 * wide * wide <= count:
        wide *= 2
    tall = count // wide
    walk = [0]
    for r in range(tall):
        across = range(1, wide)
        walk += [r * wide + c for c in (across if r % 2 == 0 else reversed(across))]
    return walk + [r * wide for r in range(tall - 1, 0, -1)]


PIECES = 4


def tie(one, other):
    return lax.optimization_barrier((one, other))


def ring_gather(own, side, stages, small):
    order = ring_order(lax.axis_size("col"))
    following = order[1:] + order[:1]
    forward = list(zip(order, following))
    back = list(zip(following, order))
    size = own.shape[0] // PIECES
    last, rest = tie(own[-size:], own)
    pieces = [rest[i * size : (i + 1) * size] for i in range(PIECES - 1)] + [last]
    stages = list(stages)
    steps = []
    for step in range(1, len(order)):
        if step > 1:
            pieces[-1], side = tie(pieces[-1], side)
        if step == 3:
            pieces[-1], small = tie(pieces[-1], small)
        pieces = [
            lax.ppermute(piece, "col", forward if i < PIECES // 2 else back)
            for i, piece in enumerate(pieces)
        ]
        if step > 1 and stages:
            side = stages.pop(0)(side)
        steps.append(list(pieces))
    for stage in stages:
        side = stage(side)
    return steps, side, small


def slot_lists(ids, counts, kinds):
    blocks, slots = ids.shape
    count = lax.axis_size("col")
    order = ring_order(count)
    place = jnp.asarray([order.index(c) for c in range(count)], jnp.int32)
    col = jnp.arange(count, dtype=jnp.int32)
    mine = jnp.sum(jnp.where(col == lax.axis_index("col"), place, 0))
    owner, within = ids // blocks, ids % blocks
    theirs = jnp.sum(jnp.where(owner[..., None] == col, place, 0), axis=-1)
    in_piece = blocks // PIECES
    piece = within // in_piece
    step = jnp.where(piece >= PIECES // 2, theirs - mine, mine - theirs) % count
    last = step == count - 1
    origin = jnp.where(last, piece, jnp.where(step == 0, 0, 1 + (step - 1) * PIECES + piece))
    offset = jnp.where(step == 0, within, within % in_piece)
    slot = jnp.arange(slots, dtype=jnp.int32)
    used = slot[None, :] < counts[:, None]
    key = jnp.where(used, jnp.where(last, slots, 0), 2 * slots) + slot
    rank = jnp.sum((key[:, None, :] < key[:, :, None]).astype(jnp.int32), axis=-1)
    at = rank[:, :, None] == slot
    def arrange(values):
        return jnp.sum(jnp.where(at, values[:, :, None], 0), axis=1)

    late = jnp.sum((used & last).astype(jnp.int32), axis=1)
    early = counts - late
    origin, offset, kinds = arrange(origin), arrange(offset), arrange(kinds)
    return (origin, offset, jnp.zeros_like(early), early, kinds), (origin, offset, early, late, kinds)


def swap(value, axis, stride):
    count = lax.axis_size(axis)
    return lax.ppermute(value, axis, [(i, i ^ stride) for i in range(count)])


def strides(axis):
    return [1 << i for i in range(lax.axis_size(axis).bit_length() - 1)]


def halvings():
    return [("row", stride) for stride in strides("row")] + [("col", 1)]


def side_of(axis, stride):
    return (lax.axis_index(axis) >> (stride.bit_length() - 1)) & 1


def halve(value, swapped, lower):
    half = value.shape[0] // 2
    keep = jnp.where(lower, value[:half], value[half:])
    give = jnp.where(lower, value[half:], value[:half])
    return keep + swap(give, *swapped)


def sum_relative(value, lower):
    value = halve(value, ("col", 1), lower)
    for stride in strides("col")[1:]:
        value = value + swap(value, "col", stride)
    for axis, stride in reversed(halvings()):
        value = jnp.concatenate([value, swap(value, axis, stride)], axis=0)
    return value


def chunk_order():
    swaps = halvings()
    relative = jnp.arange(1 << len(swaps), dtype=jnp.int32)
    mine = jnp.zeros_like(relative)
    for i, (axis, stride) in enumerate(swaps):
        mine = mine + (side_of(axis, stride) << (len(swaps) - 1 - i))
    return relative ^ mine


def shards(
    density_factor,
    onsite,
    neighbour_ids,
    neighbour_count,
    coupling_type,
    coupling_blocks,
    bath_pattern,
    bath_blocks,
):
    blocks, slots = neighbour_ids.shape
    group_blocks = lax.axis_size("col") * blocks
    in_group = neighbour_ids - lax.axis_index("row") * group_blocks
    early, late = slot_lists(in_group, neighbour_count, coupling_type)
    bathed, corner = bath_part(density_factor, bath_pattern, bath_blocks)
    energy = onsite.reshape(blocks, -1)
    swaps = halvings()
    lower = [side_of(axis, stride) == 0 for axis, stride in swaps]

    def over_row(value, lower):
        for swapped, chosen in zip(swaps[:-1], lower):
            value = halve(value, swapped, chosen)
        return value

    steps, corner, small = ring_gather(
        density_factor,
        corner,
        [lambda value: over_row(value, lower)],
        (early, late, energy, chunk_order(), lower),
    )
    early, late, energy, order, lower = small
    ready = [density_factor] + [piece for step in steps[:-1] for piece in step]
    total = early_part(early, ready, coupling_blocks, density_factor, energy)
    moved, upper = late_part(late, steps[-1], coupling_blocks, total, bathed)
    gram = jnp.concatenate([over_row(upper, lower), corner], axis=1)
    return finish_part(order, sum_relative(gram, lower[-1]), moved, bathed)


def solution(mesh):
    placed = (
        P(("row", "col"), None),
        P(("row", "col")),
        P(("row", "col"), None),
        P(("row", "col")),
        P(("row", "col"), None),
        P(),
        P(("row", "col")),
        P(),
    )
    return jax.shard_map(
        shards, mesh=mesh, in_specs=placed, out_specs=P(("row", "col"), None), check_vma=False
    )
```

```python
import jax
import jax.numpy as jnp
from jax import lax
from jax.experimental import pallas as pl
from jax.experimental.pallas import tpu as pltpu
from jax.sharding import PartitionSpec as P

time_step = 0.25
PANEL = 64
SMALLEST_PIVOT = 1 / 64
HIGHEST = lax.Precision.HIGHEST


def bath_kernel(pattern_ref, bath_ref, own_ref, bathed_ref, gram_ref):
    bathed = jnp.dot(bath_ref[0], own_ref[...], preferred_element_type=jnp.float32).astype(jnp.bfloat16)
    bathed_ref[...] = bathed
    part = lax.dot_general(
        bathed, bathed, (((0,), (0,)), ((), ())), preferred_element_type=jnp.float32
    )

    @pl.when(pl.program_id(0) == 0)
    def _():
        gram_ref[...] = part

    @pl.when(pl.program_id(0) > 0)
    def _():
        gram_ref[...] += part


def bath_part(own, bath_pattern, bath_blocks):
    blocks = bath_pattern.shape[0]
    block_rows = bath_blocks.shape[1]
    rows, rank = own.shape
    tile = pl.BlockSpec((block_rows, rank), lambda b, kind: (b, 0))
    return pl.pallas_call(
        bath_kernel,
        grid_spec=pltpu.PrefetchScalarGridSpec(
            num_scalar_prefetch=1,
            grid=(blocks,),
            in_specs=[
                pl.BlockSpec((1, block_rows, block_rows), lambda b, kind: (kind[b], 0, 0)),
                tile,
            ],
            out_specs=[tile, pl.BlockSpec((rank, rank), lambda b, kind: (0, 0))],
        ),
        out_shape=[
            jax.ShapeDtypeStruct((rows, rank), jnp.bfloat16),
            jax.ShapeDtypeStruct((rank, rank), jnp.float32),
        ],
        compiler_params=pltpu.CompilerParams(vmem_limit_bytes=7 * 2**20),
        name="bath",
    )(bath_pattern, bath_blocks, own)


def gather_products(origin_ref, offset_ref, first_ref, count_ref, kind_ref, sources, coupling_ref, held, sems, total):
    blocks, slots = origin_ref.shape
    block_rows = held.shape[2]
    b = pl.program_id(0)
    group = 1
    while group * group < len(sources):
        group += 1

    def copy(source, block, slot):
        start = pl.multiple_of(offset_ref[block, slot] * block_rows, block_rows)
        return pltpu.make_async_copy(
            source.at[pl.ds(start, block_rows), :],
            held.at[lax.rem(block, 2), slot],
            sems.at[lax.rem(block, 2), slot],
        )

    def fetch(block):
        def one(slot, carry):
            origin = origin_ref[block, slot]
            for low in range(0, len(sources), group):
                high = min(low + group, len(sources))

                @pl.when((origin >= low) & (origin < high))
                def _():
                    for place in range(low, high):
                        @pl.when(origin == place)
                        def _():
                            copy(sources[place], block, slot).start()
            return carry

        lax.fori_loop(first_ref[block], first_ref[block] + count_ref[block], one, 0)

    @pl.when(b == 0)
    def _():
        fetch(0)

    @pl.when(b + 1 < blocks)
    def _():
        fetch(b + 1)

    def product(slot):
        copy(sources[0], b, slot).wait()
        return jnp.dot(
            coupling_ref[kind_ref[b, slot]],
            held[lax.rem(b, 2), slot],
            preferred_element_type=jnp.float32,
        )

    first, count = first_ref[b], count_ref[b]

    def add_two(pair, carry):
        slot = first + 2 * pair
        total[...] -= time_step * (product(slot) + product(slot + 1))
        return carry

    lax.fori_loop(0, count // 2, add_two, 0)

    @pl.when(lax.rem(count, 2) == 1)
    def _():
        total[...] -= time_step * product(first + count - 1)


def early_kernel(origin_ref, offset_ref, first_ref, count_ref, kind_ref, *refs):
    sources = refs[:-8]
    coupling_hbm, own_ref, energy_ref, total_ref, coupling, held, sems, coupling_sem = refs[-8:]
    block_rows = own_ref.shape[0]
    load = pltpu.make_async_copy(coupling_hbm, coupling, coupling_sem)

    @pl.when(pl.program_id(0) == 0)
    def _():
        load.start()

    row = energy_ref[pl.ds(pl.program_id(0), 1), :]
    energy = jnp.broadcast_to(row, (8, block_rows)).T[:, :1]
    wide = own_ref[...].astype(jnp.float32)
    total_ref[...] = wide - time_step * (energy * wide)

    @pl.when(pl.program_id(0) == 0)
    def _():
        load.wait()

    gather_products(
        origin_ref, offset_ref, first_ref, count_ref, kind_ref, sources, coupling, held, sems, total_ref
    )


def middle_kernel(origin_ref, offset_ref, first_ref, count_ref, kind_ref, *refs):
    sources = refs[:-5]
    coupling_ref, base_ref, total_ref, held, sems = refs[-5:]
    total_ref[...] = base_ref[...]
    gather_products(
        origin_ref, offset_ref, first_ref, count_ref, kind_ref, sources, coupling_ref, held, sems, total_ref
    )


def late_kernel(origin_ref, offset_ref, first_ref, count_ref, kind_ref, *refs):
    sources = refs[:-8]
    coupling_ref, base_ref, bathed_ref, moved_ref, gram_ref, total, held, sems = refs[-8:]
    b = pl.program_id(0)
    total[...] = base_ref[...]
    gather_products(
        origin_ref, offset_ref, first_ref, count_ref, kind_ref, sources, coupling_ref, held, sems, total
    )
    moved = total[...].astype(jnp.bfloat16)
    moved_ref[...] = moved
    both = jnp.concatenate([moved, bathed_ref[...]], axis=1)
    part = lax.dot_general(
        moved, both, (((0,), (0,)), ((), ())), preferred_element_type=jnp.float32
    )

    @pl.when(b == 0)
    def _():
        gram_ref[...] = part

    @pl.when(b > 0)
    def _():
        gram_ref[...] += part


def early_part(lists, sources, coupling_blocks, own, energy):
    blocks, slots = lists[0].shape
    kinds, block_rows, _ = coupling_blocks.shape
    rows, rank = own.shape
    tile = pl.BlockSpec((block_rows, rank), lambda b, *_: (b, 0))
    return pl.pallas_call(
        early_kernel,
        grid_spec=pltpu.PrefetchScalarGridSpec(
            num_scalar_prefetch=5,
            grid=(blocks,),
            in_specs=[
                *[pl.BlockSpec(memory_space=pltpu.HBM) for _ in sources],
                pl.BlockSpec(memory_space=pltpu.HBM),
                tile,
                pl.BlockSpec((blocks, block_rows), lambda b, *_: (0, 0)),
            ],
            out_specs=tile,
            scratch_shapes=[
                pltpu.VMEM((kinds, block_rows, block_rows), jnp.bfloat16),
                pltpu.VMEM((2, slots, block_rows, rank), jnp.bfloat16),
                pltpu.SemaphoreType.DMA((2, slots)),
                pltpu.SemaphoreType.DMA,
            ],
        ),
        out_shape=jax.ShapeDtypeStruct((rows, rank), jnp.float32),
        compiler_params=pltpu.CompilerParams(vmem_limit_bytes=12 * 2**20),
        cost_estimate=pl.CostEstimate(
            flops=blocks * slots * block_rows * block_rows * rank,
            bytes_accessed=blocks * slots * block_rows * rank * 2,
            transcendentals=0,
        ),
        name="couple_early",
    )(*lists, *sources, coupling_blocks, own, energy)


def middle_part(lists, sources, coupling_blocks, base):
    blocks, slots = lists[0].shape
    kinds, block_rows, _ = coupling_blocks.shape
    rows, rank = base.shape
    tile = pl.BlockSpec((block_rows, rank), lambda b, *_: (b, 0))
    return pl.pallas_call(
        middle_kernel,
        grid_spec=pltpu.PrefetchScalarGridSpec(
            num_scalar_prefetch=5,
            grid=(blocks,),
            in_specs=[
                *[pl.BlockSpec(memory_space=pl.ANY) for _ in sources],
                pl.BlockSpec((kinds, block_rows, block_rows), lambda b, *_: (0, 0, 0)),
                tile,
            ],
            out_specs=tile,
            scratch_shapes=[
                pltpu.VMEM((2, slots, block_rows, rank), jnp.bfloat16),
                pltpu.SemaphoreType.DMA((2, slots)),
            ],
        ),
        out_shape=jax.ShapeDtypeStruct((rows, rank), jnp.float32),
        compiler_params=pltpu.CompilerParams(vmem_limit_bytes=14 * 2**20),
        cost_estimate=pl.CostEstimate(
            flops=blocks * slots * block_rows * block_rows * rank,
            bytes_accessed=blocks * slots * block_rows * rank * 2,
            transcendentals=0,
        ),
        name="couple_middle",
    )(*lists, *sources, coupling_blocks, base)


def late_part(lists, sources, coupling_blocks, base, bathed):
    blocks, slots = lists[0].shape
    kinds, block_rows, _ = coupling_blocks.shape
    rows, rank = base.shape
    tile = pl.BlockSpec((block_rows, rank), lambda b, *_: (b, 0))
    return pl.pallas_call(
        late_kernel,
        grid_spec=pltpu.PrefetchScalarGridSpec(
            num_scalar_prefetch=5,
            grid=(blocks,),
            in_specs=[
                *[pl.BlockSpec(memory_space=pl.ANY) for _ in sources],
                pl.BlockSpec((kinds, block_rows, block_rows), lambda b, *_: (0, 0, 0)),
                tile,
                tile,
            ],
            out_specs=[tile, pl.BlockSpec((rank, 2 * rank), lambda b, *_: (0, 0))],
            scratch_shapes=[
                pltpu.VMEM((block_rows, rank), jnp.float32),
                pltpu.VMEM((2, slots, block_rows, rank), jnp.bfloat16),
                pltpu.SemaphoreType.DMA((2, slots)),
            ],
        ),
        out_shape=[
            jax.ShapeDtypeStruct((rows, rank), jnp.bfloat16),
            jax.ShapeDtypeStruct((rank, 2 * rank), jnp.float32),
        ],
        compiler_params=pltpu.CompilerParams(vmem_limit_bytes=14 * 2**20),
        name="couple_late",
    )(*lists, *sources, coupling_blocks, base, bathed)


def inverse_factor(square, start, lowest):
    n = square.shape[0]
    eye = (
        lax.broadcasted_iota(jnp.int32, (n, n), 0) == lax.broadcasted_iota(jnp.int32, (n, n), 1)
    ).astype(jnp.float32)
    work = jnp.concatenate([square, eye], axis=1)
    bands = [work[8 * i : 8 * i + 8, :] for i in range(n // 8)]
    sublane = lax.broadcasted_iota(jnp.int32, (8, 2 * n), 0)
    def spread(band, g):
        return [jnp.broadcast_to(band[:, 8 * g + r : 8 * g + r + 1], (8, 2 * n)) for r in range(8)]

    out = []
    for g in range(n // 8):
        band = bands[g]
        pivots = spread(band, g)
        diagonal = jnp.zeros((8, 2 * n), jnp.float32)
        scales = []
        for r in range(8):
            scales.append(pl.reciprocal(pivots[r][r : r + 1, :], approx=True))
            diagonal = jnp.where(sublane == r, pivots[r], diagonal)
            share = jnp.where(sublane > r, pivots[r] * scales[r], 0.0)
            for q in range(r + 1, 8):
                pivots[q] = pivots[q] - share * pivots[q][r : r + 1, :]
            band = band - share * band[r : r + 1, :]
        out.append(band[:, n:] * lax.rsqrt(diagonal)[:, n:])
        lowest[...] = jnp.minimum(lowest[...], diagonal / start[8 * g : 8 * g + 8, :])
        for i in range(g + 1, n // 8):
            columns = spread(bands[i], g)
            below = bands[i]
            for r in range(8):
                share = columns[r] * scales[r]
                for q in range(r + 1, 8):
                    columns[q] = columns[q] - share * pivots[q][r : r + 1, :]
                below = below - share * band[r : r + 1, :]
            bands[i] = below
    return jnp.concatenate(out, axis=0)


def eliminate(inner, image, start, lowest):
    rank = inner.shape[0]
    diagonal = lax.broadcasted_iota(jnp.int32, (rank, rank), 0) == lax.broadcasted_iota(jnp.int32, (rank, rank), 1)
    start[...] = jnp.broadcast_to(
        jnp.sum(jnp.where(diagonal, inner[...], 0.0), axis=1, keepdims=True), start.shape
    )
    lowest[...] = jnp.ones_like(lowest)

    def product(left, right, contract):
        return lax.dot_general(
            left, right, ((contract, (0,)), ((), ())),
            precision=HIGHEST, preferred_element_type=jnp.float32,
        )

    for low in range(0, rank, PANEL):
        high = low + PANEL
        here, first = low // 128 * 128, high // 128 * 128
        inverse = inverse_factor(inner[low:high, low:high], start[low:high, :], lowest)
        panel = product(inverse, inner[low:high, here:], (1,))
        inner[low:high, here:] = panel
        share = panel[:, high - here :]
        if high < rank:
            inner[high:, first:] -= product(share, panel[:, first - here :], (0,))
        side = product(inverse, image[low:high, :], (1,))
        image[low:high, :] = side
        if high < rank:
            image[high:, :] -= product(share, side, (0,))


def finish_kernel(
    order_ref, chunks_ref, moved_hbm, bathed_hbm, out_hbm,
    gram, inner, image, start, lowest, moved, bathed, out, in_sems, out_sems,
):
    rank = chunks_ref.shape[0]
    load_moved = pltpu.make_async_copy(moved_hbm, moved, in_sems.at[0])
    load_bathed = pltpu.make_async_copy(bathed_hbm, bathed, in_sems.at[1])
    load_moved.start()
    load_bathed.start()

    chunks = order_ref.shape[0]
    size = rank // chunks
    for i in range(chunks):
        rows = pl.ds(pl.multiple_of(order_ref[i] * size, size), size)
        chunk = chunks_ref[i * size : (i + 1) * size, :]
        gram[rows, :] = chunk[:, : 2 * rank]
        gram[pl.ds(pl.multiple_of(rank + order_ref[i] * size, size), size), rank:] = chunk[:, 2 * rank :]
    gram[rank:, :rank] = gram[:rank, rank:].T
    largest = jnp.max(jnp.max(jnp.abs(gram[...]), axis=0, keepdims=True), axis=1, keepdims=True)
    gram[...] = gram[...] * (1.0 / largest)
    product = jnp.dot(gram[:rank, :], gram[...], precision=HIGHEST, preferred_element_type=jnp.float32)

    def inner_product():
        rows = image[...]
        inner[...] = lax.dot_general(
            rows, rows, (((1,), (1,)), ((), ())),
            precision=HIGHEST, preferred_element_type=jnp.float32,
        )

    image[...] = product
    inner_product()
    eliminate(inner, image, start, lowest)
    safe = jnp.min(lowest[...]) >= SMALLEST_PIVOT

    @pl.when(jnp.logical_not(safe))
    def _():
        later = jnp.dot(gram[:rank, :], gram[...], precision=HIGHEST, preferred_element_type=jnp.float32)
        inner[...] = later[:, :rank]
        image[:, rank:] = later[:, rank:]
        eliminate(inner, image.at[:, rank:], start, lowest)
        upper = lax.broadcasted_iota(jnp.int32, (rank, rank), 0) <= lax.broadcasted_iota(jnp.int32, (rank, rank), 1)
        image[:, :rank] = jnp.where(upper, inner[...], 0.0)
        inner_product()
        eliminate(inner, image, start, lowest)

    rotation = image[...].T.astype(jnp.bfloat16)
    load_moved.wait()
    load_bathed.wait()
    pieces = out_sems.shape[0]
    size = moved.shape[0] // pieces

    def store(piece):
        rows = pl.ds(pl.multiple_of(piece * size, size), size)
        return pltpu.make_async_copy(out.at[rows, :], out_hbm.at[rows, :], out_sems.at[piece])

    def one(piece, carry):
        rows = pl.ds(pl.multiple_of(piece * size, size), size)
        stacked = jnp.concatenate([moved[rows, :], bathed[rows, :]], axis=1)
        value = jnp.dot(stacked, rotation, preferred_element_type=jnp.float32)
        out[rows, :] = value.astype(jnp.bfloat16)
        store(piece).start()
        return carry

    lax.fori_loop(0, pieces, one, 0)

    def drain(piece, carry):
        store(piece).wait()
        return carry

    lax.fori_loop(0, pieces, drain, 0)


def finish_part(order, chunks, moved, bathed):
    rows, rank = moved.shape
    return pl.pallas_call(
        finish_kernel,
        in_specs=[
            pl.BlockSpec(memory_space=pltpu.SMEM),
            pl.BlockSpec(memory_space=pltpu.VMEM),
            pl.BlockSpec(memory_space=pltpu.HBM),
            pl.BlockSpec(memory_space=pltpu.HBM),
        ],
        out_specs=pl.BlockSpec(memory_space=pl.ANY),
        out_shape=jax.ShapeDtypeStruct((rows, rank), jnp.bfloat16),
        scratch_shapes=[
            pltpu.VMEM((2 * rank, 2 * rank), jnp.float32),
            pltpu.VMEM((rank, rank), jnp.float32),
            pltpu.VMEM((rank, 2 * rank), jnp.float32),
            pltpu.VMEM((rank, 2 * PANEL), jnp.float32),
            pltpu.VMEM((8, 2 * PANEL), jnp.float32),
            pltpu.VMEM((rows, rank), jnp.bfloat16),
            pltpu.VMEM((rows, rank), jnp.bfloat16),
            pltpu.VMEM((rows, rank), jnp.bfloat16),
            pltpu.SemaphoreType.DMA((2,)),
            pltpu.SemaphoreType.DMA((8,)),
        ],
        compiler_params=pltpu.CompilerParams(vmem_limit_bytes=14 * 2**20),
        name="finish",
    )(order, chunks, moved, bathed)


def ring_order(count):
    wide = 2
    while 4 * wide * wide <= count:
        wide *= 2
    tall = count // wide
    walk = [0]
    for r in range(tall):
        across = range(1, wide)
        walk += [r * wide + c for c in (across if r % 2 == 0 else reversed(across))]
    return walk + [r * wide for r in range(tall - 1, 0, -1)]


PIECES = 4


def tie(one, other):
    return lax.optimization_barrier((one, other))


def cut_kernel(own_ref, *refs):
    pieces, sems = refs[:-1], refs[-1]
    size = pieces[0].shape[0]
    copies = [
        pltpu.make_async_copy(own_ref.at[pl.ds(i * size, size), :], piece, sems.at[i])
        for i, piece in enumerate(pieces)
    ]
    for copy in copies:
        copy.start()
    for copy in copies:
        copy.wait()


def cut(own):
    size = own.shape[0] // PIECES
    return pl.pallas_call(
        cut_kernel,
        in_specs=[pl.BlockSpec(memory_space=pl.ANY)],
        out_specs=[pl.BlockSpec(memory_space=pl.ANY)] * PIECES,
        out_shape=[jax.ShapeDtypeStruct((size, own.shape[1]), own.dtype)] * PIECES,
        scratch_shapes=[pltpu.SemaphoreType.DMA((PIECES,))],
        name="cut",
    )(own)


def early_steps():
    return lax.axis_size("col") // 2 - 1


def ring_gather(own, side, stages, small, early):
    order = ring_order(lax.axis_size("col"))
    following = order[1:] + order[:1]
    forward = list(zip(order, following))
    back = list(zip(following, order))
    pieces = cut(own)
    stages = list(stages)
    steps = []
    total = None
    for step in range(1, len(order)):
        if step > 1:
            pieces[-1], side = tie(pieces[-1], side)
        if step == 3:
            pieces[-1], small = tie(pieces[-1], small)
        if step == early_steps() + 3:
            total = early(small, [piece for done in steps[: early_steps()] for piece in done])
            pieces[-1], total = tie(pieces[-1], total)
        pieces = [
            lax.ppermute(piece, "col", forward if i < PIECES // 2 else back)
            for i, piece in enumerate(pieces)
        ]
        if step > 1 and stages:
            side = stages.pop(0)(side)
        steps.append(list(pieces))
    return steps, side, small, total


def slot_lists(ids, counts, kinds):
    blocks, slots = ids.shape
    count = lax.axis_size("col")
    order = ring_order(count)
    place = jnp.asarray([order.index(c) for c in range(count)], jnp.int32)
    col = jnp.arange(count, dtype=jnp.int32)
    mine = jnp.sum(jnp.where(col == lax.axis_index("col"), place, 0))
    owner, within = ids // blocks, ids % blocks
    theirs = jnp.sum(jnp.where(owner[..., None] == col, place, 0), axis=-1)
    in_piece = blocks // PIECES
    piece = within // in_piece
    step = jnp.where(piece >= PIECES // 2, theirs - mine, mine - theirs) % count
    before = early_steps()
    part = (step > before).astype(jnp.int32) + (step == count - 1).astype(jnp.int32)
    origin = jnp.where(
        part == 0,
        jnp.where(step == 0, 0, 1 + (step - 1) * PIECES + piece),
        jnp.where(part == 1, (step - before - 1) * PIECES + piece, piece),
    )
    offset = jnp.where(step == 0, within, within % in_piece)
    slot = jnp.arange(slots, dtype=jnp.int32)
    used = slot[None, :] < counts[:, None]
    key = jnp.where(used, part, 3) * slots + slot
    rank = jnp.sum((key[:, None, :] < key[:, :, None]).astype(jnp.int32), axis=-1)
    at = rank[:, :, None] == slot

    def arrange(values):
        return jnp.sum(jnp.where(at, values[:, :, None], 0), axis=1)

    origin, offset, kinds = arrange(origin), arrange(offset), arrange(kinds)
    parts = []
    first = jnp.zeros_like(counts)
    for i in range(3):
        number = jnp.sum((used & (part == i)).astype(jnp.int32), axis=1)
        parts.append((origin, offset, first, number, kinds))
        first = first + number
    return parts


def swap(value, axis, stride):
    count = lax.axis_size(axis)
    return lax.ppermute(value, axis, [(i, i ^ stride) for i in range(count)])


def strides(axis):
    return [1 << i for i in range(lax.axis_size(axis).bit_length() - 1)]


def halvings():
    return [("row", stride) for stride in strides("row")] + [("col", 1)]


def side_of(axis, stride):
    return (lax.axis_index(axis) >> (stride.bit_length() - 1)) & 1


def halve(value, swapped, lower):
    half = value.shape[0] // 2
    keep = jnp.where(lower, value[:half], value[half:])
    give = jnp.where(lower, value[half:], value[:half])
    return keep + swap(give, *swapped)


def sum_relative(value, lower):
    value = halve(value, ("col", 1), lower)
    for stride in strides("col")[1:]:
        value = value + swap(value, "col", stride)
    for axis, stride in reversed(halvings()):
        value = jnp.concatenate([value, swap(value, axis, stride)], axis=0)
    return value


def chunk_order():
    swaps = halvings()
    relative = jnp.arange(1 << len(swaps), dtype=jnp.int32)
    mine = jnp.zeros_like(relative)
    for i, (axis, stride) in enumerate(swaps):
        mine = mine + (side_of(axis, stride) << (len(swaps) - 1 - i))
    return relative ^ mine


def shards(
    density_factor,
    onsite,
    neighbour_ids,
    neighbour_count,
    coupling_type,
    coupling_blocks,
    bath_pattern,
    bath_blocks,
):
    blocks, slots = neighbour_ids.shape
    group_blocks = lax.axis_size("col") * blocks
    in_group = neighbour_ids - lax.axis_index("row") * group_blocks
    lists = slot_lists(in_group, neighbour_count, coupling_type)
    bathed, corner = bath_part(density_factor, bath_pattern, bath_blocks)
    energy = onsite.reshape(blocks, -1)
    swaps = halvings()
    lower = [side_of(axis, stride) == 0 for axis, stride in swaps]

    def over_row(value, lower):
        for swapped, chosen in zip(swaps[:-1], lower):
            value = halve(value, swapped, chosen)
        return value

    def early(small, pieces):
        lists, energy, _, _ = small
        return early_part(lists[0], [density_factor] + pieces, coupling_blocks, density_factor, energy)

    steps, corner, small, total = ring_gather(
        density_factor,
        corner,
        [lambda value: over_row(value, lower)],
        (lists, energy, chunk_order(), lower),
        early,
    )
    lists, _, order, lower = small
    between = [piece for step in steps[early_steps() : -1] for piece in step]
    total = middle_part(lists[1], between, coupling_blocks, total)
    moved, upper = late_part(lists[2], steps[-1], coupling_blocks, total, bathed)
    gram = jnp.concatenate([over_row(upper, lower), corner], axis=1)
    return finish_part(order, sum_relative(gram, lower[-1]), moved, bathed)


def solution(mesh):
    placed = (
        P(("row", "col"), None),
        P(("row", "col")),
        P(("row", "col"), None),
        P(("row", "col")),
        P(("row", "col"), None),
        P(),
        P(("row", "col")),
        P(),
    )
    return jax.shard_map(
        shards, mesh=mesh, in_specs=placed, out_specs=P(("row", "col"), None), check_vma=False
    )
```

```python
import jax
import jax.numpy as jnp
from jax import lax
from jax.experimental import pallas as pl
from jax.experimental.pallas import tpu as pltpu
from jax.sharding import PartitionSpec as P

time_step = 0.25
PANEL = 64
SMALLEST_PIVOT = 1 / 64
HIGHEST = lax.Precision.HIGHEST


def bath_kernel(pattern_ref, bath_ref, own_ref, bathed_ref, gram_ref):
    bathed = jnp.dot(bath_ref[0], own_ref[...], preferred_element_type=jnp.float32).astype(jnp.bfloat16)
    bathed_ref[...] = bathed
    part = lax.dot_general(
        bathed, bathed, (((0,), (0,)), ((), ())), preferred_element_type=jnp.float32
    )

    @pl.when(pl.program_id(0) == 0)
    def _():
        gram_ref[...] = part

    @pl.when(pl.program_id(0) > 0)
    def _():
        gram_ref[...] += part


def bath_part(own, bath_pattern, bath_blocks):
    blocks = bath_pattern.shape[0]
    block_rows = bath_blocks.shape[1]
    rows, rank = own.shape
    tile = pl.BlockSpec((block_rows, rank), lambda b, kind: (b, 0))
    return pl.pallas_call(
        bath_kernel,
        grid_spec=pltpu.PrefetchScalarGridSpec(
            num_scalar_prefetch=1,
            grid=(blocks,),
            in_specs=[
                pl.BlockSpec((1, block_rows, block_rows), lambda b, kind: (kind[b], 0, 0)),
                tile,
            ],
            out_specs=[tile, pl.BlockSpec((rank, rank), lambda b, kind: (0, 0))],
        ),
        out_shape=[
            jax.ShapeDtypeStruct((rows, rank), jnp.bfloat16),
            jax.ShapeDtypeStruct((rank, rank), jnp.float32),
        ],
        compiler_params=pltpu.CompilerParams(vmem_limit_bytes=7 * 2**20),
        name="bath",
    )(bath_pattern, bath_blocks, own)


def gather_products(origin_ref, offset_ref, first_ref, count_ref, kind_ref, sources, coupling_ref, held, sems, total):
    blocks, slots = origin_ref.shape
    block_rows = held.shape[2]
    b = pl.program_id(0)
    group = 1
    while group * group < len(sources):
        group += 1

    def copy(source, block, slot):
        start = pl.multiple_of(offset_ref[block, slot] * block_rows, block_rows)
        return pltpu.make_async_copy(
            source.at[pl.ds(start, block_rows), :],
            held.at[lax.rem(block, 2), slot],
            sems.at[lax.rem(block, 2), slot],
        )

    def fetch(block):
        def one(slot, carry):
            origin = origin_ref[block, slot]
            for low in range(0, len(sources), group):
                high = min(low + group, len(sources))

                @pl.when((origin >= low) & (origin < high))
                def _():
                    for place in range(low, high):
                        @pl.when(origin == place)
                        def _():
                            copy(sources[place], block, slot).start()
            return carry

        lax.fori_loop(first_ref[block], first_ref[block] + count_ref[block], one, 0)

    @pl.when(b == 0)
    def _():
        fetch(0)

    @pl.when(b + 1 < blocks)
    def _():
        fetch(b + 1)

    def product(slot):
        copy(sources[0], b, slot).wait()
        return jnp.dot(
            coupling_ref[kind_ref[b, slot]],
            held[lax.rem(b, 2), slot],
            preferred_element_type=jnp.float32,
        )

    first, count = first_ref[b], count_ref[b]

    def add_two(pair, carry):
        slot = first + 2 * pair
        total[...] -= time_step * (product(slot) + product(slot + 1))
        return carry

    lax.fori_loop(0, count // 2, add_two, 0)

    @pl.when(lax.rem(count, 2) == 1)
    def _():
        total[...] -= time_step * product(first + count - 1)


def early_kernel(origin_ref, offset_ref, first_ref, count_ref, kind_ref, *refs):
    sources = refs[:-8]
    coupling_hbm, own_ref, energy_ref, total_ref, coupling, held, sems, coupling_sem = refs[-8:]
    block_rows = own_ref.shape[0]
    load = pltpu.make_async_copy(coupling_hbm, coupling, coupling_sem)

    @pl.when(pl.program_id(0) == 0)
    def _():
        load.start()

    row = energy_ref[pl.ds(pl.program_id(0), 1), :]
    energy = jnp.broadcast_to(row, (8, block_rows)).T[:, :1]
    wide = own_ref[...].astype(jnp.float32)
    total_ref[...] = wide - time_step * (energy * wide)

    @pl.when(pl.program_id(0) == 0)
    def _():
        load.wait()

    gather_products(
        origin_ref, offset_ref, first_ref, count_ref, kind_ref, sources, coupling, held, sems, total_ref
    )


def middle_kernel(origin_ref, offset_ref, first_ref, count_ref, kind_ref, *refs):
    sources = refs[:-5]
    coupling_ref, base_ref, total_ref, held, sems = refs[-5:]
    total_ref[...] = base_ref[...]
    gather_products(
        origin_ref, offset_ref, first_ref, count_ref, kind_ref, sources, coupling_ref, held, sems, total_ref
    )


def late_kernel(origin_ref, offset_ref, first_ref, count_ref, kind_ref, *refs):
    sources = refs[:-8]
    coupling_ref, base_ref, bathed_ref, moved_ref, gram_ref, total, held, sems = refs[-8:]
    b = pl.program_id(0)
    total[...] = base_ref[...]
    gather_products(
        origin_ref, offset_ref, first_ref, count_ref, kind_ref, sources, coupling_ref, held, sems, total
    )
    moved = total[...].astype(jnp.bfloat16)
    moved_ref[...] = moved
    both = jnp.concatenate([moved, bathed_ref[...]], axis=1)
    part = lax.dot_general(
        moved, both, (((0,), (0,)), ((), ())), preferred_element_type=jnp.float32
    )

    @pl.when(b == 0)
    def _():
        gram_ref[...] = part

    @pl.when(b > 0)
    def _():
        gram_ref[...] += part


def early_part(lists, sources, coupling_blocks, own, energy):
    blocks, slots = lists[0].shape
    kinds, block_rows, _ = coupling_blocks.shape
    rows, rank = own.shape
    tile = pl.BlockSpec((block_rows, rank), lambda b, *_: (b, 0))
    return pl.pallas_call(
        early_kernel,
        grid_spec=pltpu.PrefetchScalarGridSpec(
            num_scalar_prefetch=5,
            grid=(blocks,),
            in_specs=[
                *[pl.BlockSpec(memory_space=pltpu.HBM) for _ in sources],
                pl.BlockSpec(memory_space=pltpu.HBM),
                tile,
                pl.BlockSpec((blocks, block_rows), lambda b, *_: (0, 0)),
            ],
            out_specs=tile,
            scratch_shapes=[
                pltpu.VMEM((kinds, block_rows, block_rows), jnp.bfloat16),
                pltpu.VMEM((2, slots, block_rows, rank), jnp.bfloat16),
                pltpu.SemaphoreType.DMA((2, slots)),
                pltpu.SemaphoreType.DMA,
            ],
        ),
        out_shape=jax.ShapeDtypeStruct((rows, rank), jnp.float32),
        compiler_params=pltpu.CompilerParams(vmem_limit_bytes=12 * 2**20),
        cost_estimate=pl.CostEstimate(
            flops=blocks * slots * block_rows * block_rows * rank,
            bytes_accessed=blocks * slots * block_rows * rank * 2,
            transcendentals=0,
        ),
        name="couple_early",
    )(*lists, *sources, coupling_blocks, own, energy)


def middle_part(lists, sources, coupling_blocks, base):
    blocks, slots = lists[0].shape
    kinds, block_rows, _ = coupling_blocks.shape
    rows, rank = base.shape
    tile = pl.BlockSpec((block_rows, rank), lambda b, *_: (b, 0))
    return pl.pallas_call(
        middle_kernel,
        grid_spec=pltpu.PrefetchScalarGridSpec(
            num_scalar_prefetch=5,
            grid=(blocks,),
            in_specs=[
                *[pl.BlockSpec(memory_space=pl.ANY) for _ in sources],
                pl.BlockSpec((kinds, block_rows, block_rows), lambda b, *_: (0, 0, 0)),
                tile,
            ],
            out_specs=tile,
            scratch_shapes=[
                pltpu.VMEM((2, slots, block_rows, rank), jnp.bfloat16),
                pltpu.SemaphoreType.DMA((2, slots)),
            ],
        ),
        out_shape=jax.ShapeDtypeStruct((rows, rank), jnp.float32),
        compiler_params=pltpu.CompilerParams(vmem_limit_bytes=14 * 2**20),
        cost_estimate=pl.CostEstimate(
            flops=blocks * slots * block_rows * block_rows * rank,
            bytes_accessed=blocks * slots * block_rows * rank * 2,
            transcendentals=0,
        ),
        name="couple_middle",
    )(*lists, *sources, coupling_blocks, base)


def late_part(lists, sources, coupling_blocks, base, bathed):
    blocks, slots = lists[0].shape
    kinds, block_rows, _ = coupling_blocks.shape
    rows, rank = base.shape
    tile = pl.BlockSpec((block_rows, rank), lambda b, *_: (b, 0))
    return pl.pallas_call(
        late_kernel,
        grid_spec=pltpu.PrefetchScalarGridSpec(
            num_scalar_prefetch=5,
            grid=(blocks,),
            in_specs=[
                *[pl.BlockSpec(memory_space=pl.ANY) for _ in sources],
                pl.BlockSpec((kinds, block_rows, block_rows), lambda b, *_: (0, 0, 0)),
                tile,
                tile,
            ],
            out_specs=[tile, pl.BlockSpec((rank, 2 * rank), lambda b, *_: (0, 0))],
            scratch_shapes=[
                pltpu.VMEM((block_rows, rank), jnp.float32),
                pltpu.VMEM((2, slots, block_rows, rank), jnp.bfloat16),
                pltpu.SemaphoreType.DMA((2, slots)),
            ],
        ),
        out_shape=[
            jax.ShapeDtypeStruct((rows, rank), jnp.bfloat16),
            jax.ShapeDtypeStruct((rank, 2 * rank), jnp.float32),
        ],
        compiler_params=pltpu.CompilerParams(vmem_limit_bytes=14 * 2**20),
        name="couple_late",
    )(*lists, *sources, coupling_blocks, base, bathed)


def inverse_factor(square, start, lowest):
    n = square.shape[0]
    eye = (
        lax.broadcasted_iota(jnp.int32, (n, n), 0) == lax.broadcasted_iota(jnp.int32, (n, n), 1)
    ).astype(jnp.float32)
    work = jnp.concatenate([square, eye], axis=1)
    bands = [work[8 * i : 8 * i + 8, :] for i in range(n // 8)]
    sublane = lax.broadcasted_iota(jnp.int32, (8, 2 * n), 0)
    def spread(band, g):
        return [jnp.broadcast_to(band[:, 8 * g + r : 8 * g + r + 1], (8, 2 * n)) for r in range(8)]

    out = []
    for g in range(n // 8):
        band = bands[g]
        pivots = spread(band, g)
        diagonal = jnp.zeros((8, 2 * n), jnp.float32)
        scales = []
        for r in range(8):
            scales.append(pl.reciprocal(pivots[r][r : r + 1, :], approx=True))
            diagonal = jnp.where(sublane == r, pivots[r], diagonal)
            share = jnp.where(sublane > r, pivots[r] * scales[r], 0.0)
            for q in range(r + 1, 8):
                pivots[q] = pivots[q] - share * pivots[q][r : r + 1, :]
            band = band - share * band[r : r + 1, :]
        out.append(band[:, n:] * lax.rsqrt(diagonal)[:, n:])
        lowest[...] = jnp.minimum(lowest[...], diagonal / start[8 * g : 8 * g + 8, :])
        for i in range(g + 1, n // 8):
            columns = spread(bands[i], g)
            below = bands[i]
            for r in range(8):
                share = columns[r] * scales[r]
                for q in range(r + 1, 8):
                    columns[q] = columns[q] - share * pivots[q][r : r + 1, :]
                below = below - share * band[r : r + 1, :]
            bands[i] = below
    return jnp.concatenate(out, axis=0)


def eliminate(inner, image, start, lowest):
    rank = inner.shape[0]
    diagonal = lax.broadcasted_iota(jnp.int32, (rank, rank), 0) == lax.broadcasted_iota(jnp.int32, (rank, rank), 1)
    start[...] = jnp.broadcast_to(
        jnp.sum(jnp.where(diagonal, inner[...], 0.0), axis=1, keepdims=True), start.shape
    )
    lowest[...] = jnp.ones_like(lowest)

    def product(left, right, contract):
        return lax.dot_general(
            left, right, ((contract, (0,)), ((), ())),
            precision=HIGHEST, preferred_element_type=jnp.float32,
        )

    for low in range(0, rank, PANEL):
        high = low + PANEL
        here, first = low // 128 * 128, high // 128 * 128
        inverse = inverse_factor(inner[low:high, low:high], start[low:high, :], lowest)
        panel = product(inverse, inner[low:high, here:], (1,))
        inner[low:high, here:] = panel
        share = panel[:, high - here :]
        if high < rank:
            inner[high:, first:] -= product(share, panel[:, first - here :], (0,))
        side = product(inverse, image[low:high, :], (1,))
        image[low:high, :] = side
        if high < rank:
            image[high:, :] -= product(share, side, (0,))


def finish_kernel(
    order_ref, chunks_ref, moved_hbm, bathed_hbm, out_hbm,
    gram, inner, image, start, lowest, moved, bathed, out, in_sems, out_sems,
):
    rank = chunks_ref.shape[0]
    load_moved = pltpu.make_async_copy(moved_hbm, moved, in_sems.at[0])
    load_bathed = pltpu.make_async_copy(bathed_hbm, bathed, in_sems.at[1])
    load_moved.start()
    load_bathed.start()

    chunks = order_ref.shape[0]
    size = rank // chunks
    half = rank // 2
    for i in range(chunks):
        rows = pl.ds(pl.multiple_of(order_ref[i] * size, size), size)
        below = pl.ds(pl.multiple_of(rank + order_ref[i] * size, size), size)
        chunk = chunks_ref[i * size : (i + 1) * size, :]

        @pl.when(order_ref[i] < chunks // 2)
        def _():
            gram[rows, :] = chunk[:, : 2 * rank]
            gram[below, rank : rank + half] = chunk[:, 2 * rank :]

        @pl.when(order_ref[i] >= chunks // 2)
        def _():
            gram[rows, half:] = chunk[:, : rank + half]
            gram[below, rank:] = chunk[:, rank + half :]

    gram[half:rank, :half] = gram[:half, half:rank].T
    gram[rank : rank + half, rank + half :] = gram[rank + half :, rank : rank + half].T
    gram[rank:, :rank] = gram[:rank, rank:].T
    largest = jnp.max(jnp.max(jnp.abs(gram[...]), axis=0, keepdims=True), axis=1, keepdims=True)
    gram[...] = gram[...] * (1.0 / largest)
    product = jnp.dot(gram[:rank, :], gram[...], precision=HIGHEST, preferred_element_type=jnp.float32)

    def inner_product():
        rows = image[...]
        inner[...] = lax.dot_general(
            rows, rows, (((1,), (1,)), ((), ())),
            precision=HIGHEST, preferred_element_type=jnp.float32,
        )

    image[...] = product
    inner_product()
    eliminate(inner, image, start, lowest)
    safe = jnp.min(lowest[...]) >= SMALLEST_PIVOT

    @pl.when(jnp.logical_not(safe))
    def _():
        later = jnp.dot(gram[:rank, :], gram[...], precision=HIGHEST, preferred_element_type=jnp.float32)
        inner[...] = later[:, :rank]
        image[:, rank:] = later[:, rank:]
        eliminate(inner, image.at[:, rank:], start, lowest)
        upper = lax.broadcasted_iota(jnp.int32, (rank, rank), 0) <= lax.broadcasted_iota(jnp.int32, (rank, rank), 1)
        image[:, :rank] = jnp.where(upper, inner[...], 0.0)
        inner_product()
        eliminate(inner, image, start, lowest)

    rotation = image[...].T.astype(jnp.bfloat16)
    load_moved.wait()
    load_bathed.wait()
    pieces = out_sems.shape[0]
    size = moved.shape[0] // pieces

    def store(piece):
        rows = pl.ds(pl.multiple_of(piece * size, size), size)
        return pltpu.make_async_copy(out.at[rows, :], out_hbm.at[rows, :], out_sems.at[piece])

    def one(piece, carry):
        rows = pl.ds(pl.multiple_of(piece * size, size), size)
        stacked = jnp.concatenate([moved[rows, :], bathed[rows, :]], axis=1)
        value = jnp.dot(stacked, rotation, preferred_element_type=jnp.float32)
        out[rows, :] = value.astype(jnp.bfloat16)
        store(piece).start()
        return carry

    lax.fori_loop(0, pieces, one, 0)

    def drain(piece, carry):
        store(piece).wait()
        return carry

    lax.fori_loop(0, pieces, drain, 0)


def finish_part(order, chunks, moved, bathed):
    rows, rank = moved.shape
    return pl.pallas_call(
        finish_kernel,
        in_specs=[
            pl.BlockSpec(memory_space=pltpu.SMEM),
            pl.BlockSpec(memory_space=pltpu.VMEM),
            pl.BlockSpec(memory_space=pltpu.HBM),
            pl.BlockSpec(memory_space=pltpu.HBM),
        ],
        out_specs=pl.BlockSpec(memory_space=pl.ANY),
        out_shape=jax.ShapeDtypeStruct((rows, rank), jnp.bfloat16),
        scratch_shapes=[
            pltpu.VMEM((2 * rank, 2 * rank), jnp.float32),
            pltpu.VMEM((rank, rank), jnp.float32),
            pltpu.VMEM((rank, 2 * rank), jnp.float32),
            pltpu.VMEM((rank, 2 * PANEL), jnp.float32),
            pltpu.VMEM((8, 2 * PANEL), jnp.float32),
            pltpu.VMEM((rows, rank), jnp.bfloat16),
            pltpu.VMEM((rows, rank), jnp.bfloat16),
            pltpu.VMEM((rows, rank), jnp.bfloat16),
            pltpu.SemaphoreType.DMA((2,)),
            pltpu.SemaphoreType.DMA((8,)),
        ],
        compiler_params=pltpu.CompilerParams(vmem_limit_bytes=14 * 2**20),
        name="finish",
    )(order, chunks, moved, bathed)


def ring_order(count):
    wide = 2
    while 4 * wide * wide <= count:
        wide *= 2
    tall = count // wide
    walk = [0]
    for r in range(tall):
        across = range(1, wide)
        walk += [r * wide + c for c in (across if r % 2 == 0 else reversed(across))]
    return walk + [r * wide for r in range(tall - 1, 0, -1)]


PIECES = 4


def tie(one, other):
    return lax.optimization_barrier((one, other))


def early_steps():
    return lax.axis_size("col") // 2 - 1


def ring_gather(own, side, stages, small, early):
    order = ring_order(lax.axis_size("col"))
    following = order[1:] + order[:1]
    forward = list(zip(order, following))
    back = list(zip(following, order))
    size = own.shape[0] // PIECES
    pieces = [own[i * size : (i + 1) * size] for i in range(PIECES)]
    stages = list(stages)
    steps = []
    total = None
    for step in range(1, len(order)):
        if step > 1:
            pieces[-1], side = tie(pieces[-1], side)
        if step == 3:
            pieces[-1], small = tie(pieces[-1], small)
        if step == early_steps() + 3:
            total = early(small, [piece for done in steps[: early_steps()] for piece in done])
            pieces[-1], total = tie(pieces[-1], total)
        pieces = [
            lax.ppermute(piece, "col", forward if i < PIECES // 2 else back)
            for i, piece in enumerate(pieces)
        ]
        if step > 1 and stages:
            side = stages.pop(0)(side)
        steps.append(list(pieces))
    return steps, side, small, total


def slot_lists(ids, counts, kinds):
    blocks, slots = ids.shape
    count = lax.axis_size("col")
    order = ring_order(count)
    place = jnp.asarray([order.index(c) for c in range(count)], jnp.int32)
    col = jnp.arange(count, dtype=jnp.int32)
    mine = jnp.sum(jnp.where(col == lax.axis_index("col"), place, 0))
    owner, within = ids // blocks, ids % blocks
    theirs = jnp.sum(jnp.where(owner[..., None] == col, place, 0), axis=-1)
    in_piece = blocks // PIECES
    piece = within // in_piece
    step = jnp.where(piece >= PIECES // 2, theirs - mine, mine - theirs) % count
    before = early_steps()
    part = (step > before).astype(jnp.int32) + (step == count - 1).astype(jnp.int32)
    origin = jnp.where(
        part == 0,
        jnp.where(step == 0, 0, 1 + (step - 1) * PIECES + piece),
        jnp.where(part == 1, (step - before - 1) * PIECES + piece, piece),
    )
    offset = jnp.where(step == 0, within, within % in_piece)
    slot = jnp.arange(slots, dtype=jnp.int32)
    used = slot[None, :] < counts[:, None]
    key = jnp.where(used, part, 3) * slots + slot
    rank = jnp.sum((key[:, None, :] < key[:, :, None]).astype(jnp.int32), axis=-1)
    at = rank[:, :, None] == slot

    def arrange(values):
        return jnp.sum(jnp.where(at, values[:, :, None], 0), axis=1)

    origin, offset, kinds = arrange(origin), arrange(offset), arrange(kinds)
    parts = []
    first = jnp.zeros_like(counts)
    for i in range(3):
        number = jnp.sum((used & (part == i)).astype(jnp.int32), axis=1)
        parts.append((origin, offset, first, number, kinds))
        first = first + number
    return parts


def swap(value, axis, stride):
    count = lax.axis_size(axis)
    return lax.ppermute(value, axis, [(i, i ^ stride) for i in range(count)])


def strides(axis):
    return [1 << i for i in range(lax.axis_size(axis).bit_length() - 1)]


def halvings():
    return [("row", stride) for stride in strides("row")] + [("col", 1)]


def side_of(axis, stride):
    return (lax.axis_index(axis) >> (stride.bit_length() - 1)) & 1


def halve(value, swapped, lower):
    half = value.shape[0] // 2
    keep = jnp.where(lower, value[:half], value[half:])
    give = jnp.where(lower, value[half:], value[:half])
    return keep + swap(give, *swapped)


def sum_relative(value, lower):
    value = halve(value, ("col", 1), lower)
    for stride in strides("col")[1:]:
        value = value + swap(value, "col", stride)
    for axis, stride in reversed(halvings()):
        value = jnp.concatenate([value, swap(value, axis, stride)], axis=0)
    return value


def pack(upper, corner, lower):
    half = corner.shape[1] // 2
    return jnp.where(
        lower,
        jnp.concatenate([upper, corner[:, :half]], axis=1),
        jnp.concatenate([upper[:, half:], corner], axis=1),
    )


def chunk_order():
    swaps = halvings()
    relative = jnp.arange(1 << len(swaps), dtype=jnp.int32)
    mine = jnp.zeros_like(relative)
    for i, (axis, stride) in enumerate(swaps):
        mine = mine + (side_of(axis, stride) << (len(swaps) - 1 - i))
    return relative ^ mine


def shards(
    density_factor,
    onsite,
    neighbour_ids,
    neighbour_count,
    coupling_type,
    coupling_blocks,
    bath_pattern,
    bath_blocks,
):
    blocks, slots = neighbour_ids.shape
    group_blocks = lax.axis_size("col") * blocks
    in_group = neighbour_ids - lax.axis_index("row") * group_blocks
    lists = slot_lists(in_group, neighbour_count, coupling_type)
    bathed, corner = bath_part(density_factor, bath_pattern, bath_blocks)
    energy = onsite.reshape(blocks, -1)
    swaps = halvings()
    lower = [side_of(axis, stride) == 0 for axis, stride in swaps]

    def over_row(value, lower):
        for swapped, chosen in zip(swaps[:-1], lower):
            value = halve(value, swapped, chosen)
        return value

    def early(small, pieces):
        lists, energy, _, _ = small
        return early_part(lists[0], [density_factor] + pieces, coupling_blocks, density_factor, energy)

    steps, corner, small, total = ring_gather(
        density_factor,
        corner,
        [lambda value: over_row(value, lower)],
        (lists, energy, chunk_order(), lower),
        early,
    )
    lists, _, order, lower = small
    between = [piece for step in steps[early_steps() : -1] for piece in step]
    total = middle_part(lists[1], between, coupling_blocks, total)
    moved, upper = late_part(lists[2], steps[-1], coupling_blocks, total, bathed)
    gram = pack(over_row(upper, lower), corner, lower[0])
    return finish_part(order, sum_relative(gram, lower[-1]), moved, bathed)


def solution(mesh):
    placed = (
        P(("row", "col"), None),
        P(("row", "col")),
        P(("row", "col"), None),
        P(("row", "col")),
        P(("row", "col"), None),
        P(),
        P(("row", "col")),
        P(),
    )
    return jax.shard_map(
        shards, mesh=mesh, in_specs=placed, out_specs=P(("row", "col"), None), check_vma=False
    )
```

```python
import jax
import jax.numpy as jnp
from jax import lax
from jax.experimental import pallas as pl
from jax.experimental.pallas import tpu as pltpu
from jax.sharding import PartitionSpec as P

time_step = 0.25
PANEL = 64
SMALLEST_PIVOT = 1 / 64
HIGHEST = lax.Precision.HIGHEST


def bath_kernel(pattern_ref, bath_ref, own_ref, bathed_ref, gram_ref):
    bathed = jnp.dot(bath_ref[0], own_ref[...], preferred_element_type=jnp.float32).astype(jnp.bfloat16)
    bathed_ref[...] = bathed
    part = lax.dot_general(
        bathed, bathed, (((0,), (0,)), ((), ())), preferred_element_type=jnp.float32
    )

    @pl.when(pl.program_id(0) == 0)
    def _():
        gram_ref[...] = part

    @pl.when(pl.program_id(0) > 0)
    def _():
        gram_ref[...] += part


def bath_part(own, bath_pattern, bath_blocks):
    blocks = bath_pattern.shape[0]
    block_rows = bath_blocks.shape[1]
    rows, rank = own.shape
    tile = pl.BlockSpec((block_rows, rank), lambda b, kind: (b, 0))
    return pl.pallas_call(
        bath_kernel,
        grid_spec=pltpu.PrefetchScalarGridSpec(
            num_scalar_prefetch=1,
            grid=(blocks,),
            in_specs=[
                pl.BlockSpec((1, block_rows, block_rows), lambda b, kind: (kind[b], 0, 0)),
                tile,
            ],
            out_specs=[tile, pl.BlockSpec((rank, rank), lambda b, kind: (0, 0))],
        ),
        out_shape=[
            jax.ShapeDtypeStruct((rows, rank), jnp.bfloat16),
            jax.ShapeDtypeStruct((rank, rank), jnp.float32),
        ],
        compiler_params=pltpu.CompilerParams(vmem_limit_bytes=7 * 2**20),
        name="bath",
    )(bath_pattern, bath_blocks, own)


def gather_products(origin_ref, offset_ref, first_ref, count_ref, kind_ref, sources, coupling_ref, held, sems, total):
    blocks, slots = origin_ref.shape
    block_rows = held.shape[2]
    b = pl.program_id(0)
    group = 1
    while group * group < len(sources):
        group += 1

    def copy(source, block, slot):
        start = pl.multiple_of(offset_ref[block, slot] * block_rows, block_rows)
        return pltpu.make_async_copy(
            source.at[pl.ds(start, block_rows), :],
            held.at[lax.rem(block, 2), slot],
            sems.at[lax.rem(block, 2), slot],
        )

    def fetch(block):
        def one(slot, carry):
            origin = origin_ref[block, slot]
            for low in range(0, len(sources), group):
                high = min(low + group, len(sources))

                @pl.when((origin >= low) & (origin < high))
                def _():
                    for place in range(low, high):
                        @pl.when(origin == place)
                        def _():
                            copy(sources[place], block, slot).start()
            return carry

        lax.fori_loop(first_ref[block], first_ref[block] + count_ref[block], one, 0)

    @pl.when(b == 0)
    def _():
        fetch(0)

    @pl.when(b + 1 < blocks)
    def _():
        fetch(b + 1)

    def product(slot):
        copy(sources[0], b, slot).wait()
        return jnp.dot(
            coupling_ref[kind_ref[b, slot]],
            held[lax.rem(b, 2), slot],
            preferred_element_type=jnp.float32,
        )

    first, count = first_ref[b], count_ref[b]

    def add_two(pair, carry):
        slot = first + 2 * pair
        total[...] -= time_step * (product(slot) + product(slot + 1))
        return carry

    lax.fori_loop(0, count // 2, add_two, 0)

    @pl.when(lax.rem(count, 2) == 1)
    def _():
        total[...] -= time_step * product(first + count - 1)


def early_kernel(origin_ref, offset_ref, first_ref, count_ref, kind_ref, *refs):
    sources = refs[:-8]
    coupling_hbm, own_ref, energy_ref, total_ref, coupling, held, sems, coupling_sem = refs[-8:]
    block_rows = own_ref.shape[0]
    load = pltpu.make_async_copy(coupling_hbm, coupling, coupling_sem)

    @pl.when(pl.program_id(0) == 0)
    def _():
        load.start()

    row = energy_ref[pl.ds(pl.program_id(0), 1), :]
    energy = jnp.broadcast_to(row, (8, block_rows)).T[:, :1]
    wide = own_ref[...].astype(jnp.float32)
    total_ref[...] = wide - time_step * (energy * wide)

    @pl.when(pl.program_id(0) == 0)
    def _():
        load.wait()

    gather_products(
        origin_ref, offset_ref, first_ref, count_ref, kind_ref, sources, coupling, held, sems, total_ref
    )


def middle_kernel(origin_ref, offset_ref, first_ref, count_ref, kind_ref, *refs):
    sources = refs[:-5]
    coupling_ref, base_ref, total_ref, held, sems = refs[-5:]
    total_ref[...] = base_ref[...]
    gather_products(
        origin_ref, offset_ref, first_ref, count_ref, kind_ref, sources, coupling_ref, held, sems, total_ref
    )


def late_kernel(origin_ref, offset_ref, first_ref, count_ref, kind_ref, *refs):
    sources = refs[:-8]
    coupling_ref, base_ref, bathed_ref, moved_ref, gram_ref, total, held, sems = refs[-8:]
    b = pl.program_id(0)
    total[...] = base_ref[...]
    gather_products(
        origin_ref, offset_ref, first_ref, count_ref, kind_ref, sources, coupling_ref, held, sems, total
    )
    moved = total[...].astype(jnp.bfloat16)
    moved_ref[...] = moved
    both = jnp.concatenate([moved, bathed_ref[...]], axis=1)
    part = lax.dot_general(
        moved, both, (((0,), (0,)), ((), ())), preferred_element_type=jnp.float32
    )

    @pl.when(b == 0)
    def _():
        gram_ref[...] = part

    @pl.when(b > 0)
    def _():
        gram_ref[...] += part


def early_part(lists, sources, coupling_blocks, own, energy):
    blocks, slots = lists[0].shape
    kinds, block_rows, _ = coupling_blocks.shape
    rows, rank = own.shape
    tile = pl.BlockSpec((block_rows, rank), lambda b, *_: (b, 0))
    return pl.pallas_call(
        early_kernel,
        grid_spec=pltpu.PrefetchScalarGridSpec(
            num_scalar_prefetch=5,
            grid=(blocks,),
            in_specs=[
                *[pl.BlockSpec(memory_space=pltpu.HBM) for _ in sources],
                pl.BlockSpec(memory_space=pltpu.HBM),
                tile,
                pl.BlockSpec((blocks, block_rows), lambda b, *_: (0, 0)),
            ],
            out_specs=tile,
            scratch_shapes=[
                pltpu.VMEM((kinds, block_rows, block_rows), jnp.bfloat16),
                pltpu.VMEM((2, slots, block_rows, rank), jnp.bfloat16),
                pltpu.SemaphoreType.DMA((2, slots)),
                pltpu.SemaphoreType.DMA,
            ],
        ),
        out_shape=jax.ShapeDtypeStruct((rows, rank), jnp.float32),
        compiler_params=pltpu.CompilerParams(vmem_limit_bytes=12 * 2**20),
        cost_estimate=pl.CostEstimate(
            flops=blocks * slots * block_rows * block_rows * rank,
            bytes_accessed=blocks * slots * block_rows * rank * 2,
            transcendentals=0,
        ),
        name="couple_early",
    )(*lists, *sources, coupling_blocks, own, energy)


def middle_part(lists, sources, coupling_blocks, base):
    blocks, slots = lists[0].shape
    kinds, block_rows, _ = coupling_blocks.shape
    rows, rank = base.shape
    tile = pl.BlockSpec((block_rows, rank), lambda b, *_: (b, 0))
    return pl.pallas_call(
        middle_kernel,
        grid_spec=pltpu.PrefetchScalarGridSpec(
            num_scalar_prefetch=5,
            grid=(blocks,),
            in_specs=[
                *[pl.BlockSpec(memory_space=pl.ANY) for _ in sources],
                pl.BlockSpec((kinds, block_rows, block_rows), lambda b, *_: (0, 0, 0)),
                tile,
            ],
            out_specs=tile,
            scratch_shapes=[
                pltpu.VMEM((2, slots, block_rows, rank), jnp.bfloat16),
                pltpu.SemaphoreType.DMA((2, slots)),
            ],
        ),
        out_shape=jax.ShapeDtypeStruct((rows, rank), jnp.float32),
        compiler_params=pltpu.CompilerParams(vmem_limit_bytes=14 * 2**20),
        cost_estimate=pl.CostEstimate(
            flops=blocks * slots * block_rows * block_rows * rank,
            bytes_accessed=blocks * slots * block_rows * rank * 2,
            transcendentals=0,
        ),
        name="couple_middle",
    )(*lists, *sources, coupling_blocks, base)


def late_part(lists, sources, coupling_blocks, base, bathed):
    blocks, slots = lists[0].shape
    kinds, block_rows, _ = coupling_blocks.shape
    rows, rank = base.shape
    tile = pl.BlockSpec((block_rows, rank), lambda b, *_: (b, 0))
    return pl.pallas_call(
        late_kernel,
        grid_spec=pltpu.PrefetchScalarGridSpec(
            num_scalar_prefetch=5,
            grid=(blocks,),
            in_specs=[
                *[pl.BlockSpec(memory_space=pl.ANY) for _ in sources],
                pl.BlockSpec((kinds, block_rows, block_rows), lambda b, *_: (0, 0, 0)),
                tile,
                tile,
            ],
            out_specs=[tile, pl.BlockSpec((rank, 2 * rank), lambda b, *_: (0, 0))],
            scratch_shapes=[
                pltpu.VMEM((block_rows, rank), jnp.float32),
                pltpu.VMEM((2, slots, block_rows, rank), jnp.bfloat16),
                pltpu.SemaphoreType.DMA((2, slots)),
            ],
        ),
        out_shape=[
            jax.ShapeDtypeStruct((rows, rank), jnp.bfloat16),
            jax.ShapeDtypeStruct((rank, 2 * rank), jnp.float32),
        ],
        compiler_params=pltpu.CompilerParams(vmem_limit_bytes=14 * 2**20),
        name="couple_late",
    )(*lists, *sources, coupling_blocks, base, bathed)


def inverse_factor(square, start, lowest):
    n = square.shape[0]
    eye = (
        lax.broadcasted_iota(jnp.int32, (n, n), 0) == lax.broadcasted_iota(jnp.int32, (n, n), 1)
    ).astype(jnp.float32)
    work = jnp.concatenate([square, eye], axis=1)
    bands = [work[8 * i : 8 * i + 8, :] for i in range(n // 8)]
    sublane = lax.broadcasted_iota(jnp.int32, (8, 2 * n), 0)
    def spread(band, g):
        return [jnp.broadcast_to(band[:, 8 * g + r : 8 * g + r + 1], (8, 2 * n)) for r in range(8)]

    out = []
    for g in range(n // 8):
        band = bands[g]
        pivots = spread(band, g)
        diagonal = jnp.zeros((8, 2 * n), jnp.float32)
        scales = []
        for r in range(8):
            scales.append(pl.reciprocal(pivots[r][r : r + 1, :], approx=True))
            diagonal = jnp.where(sublane == r, pivots[r], diagonal)
            share = jnp.where(sublane > r, pivots[r] * scales[r], 0.0)
            for q in range(r + 1, 8):
                pivots[q] = pivots[q] - share * pivots[q][r : r + 1, :]
            band = band - share * band[r : r + 1, :]
        out.append(band[:, n:] * lax.rsqrt(diagonal)[:, n:])
        lowest[...] = jnp.minimum(lowest[...], diagonal / start[8 * g : 8 * g + 8, :])
        for i in range(g + 1, n // 8):
            columns = spread(bands[i], g)
            below = bands[i]
            for r in range(8):
                share = columns[r] * scales[r]
                for q in range(r + 1, 8):
                    columns[q] = columns[q] - share * pivots[q][r : r + 1, :]
                below = below - share * band[r : r + 1, :]
            bands[i] = below
    return jnp.concatenate(out, axis=0)


def eliminate(inner, image, start, lowest):
    rank = inner.shape[0]
    diagonal = lax.broadcasted_iota(jnp.int32, (rank, rank), 0) == lax.broadcasted_iota(jnp.int32, (rank, rank), 1)
    start[...] = jnp.broadcast_to(
        jnp.sum(jnp.where(diagonal, inner[...], 0.0), axis=1, keepdims=True), start.shape
    )
    lowest[...] = jnp.ones_like(lowest)

    def product(left, right, contract):
        return lax.dot_general(
            left, right, ((contract, (0,)), ((), ())),
            precision=HIGHEST, preferred_element_type=jnp.float32,
        )

    for low in range(0, rank, PANEL):
        high = low + PANEL
        here, first = low // 128 * 128, high // 128 * 128
        inverse = inverse_factor(inner[low:high, low:high], start[low:high, :], lowest)
        panel = product(inverse, inner[low:high, here:], (1,))
        inner[low:high, here:] = panel
        share = panel[:, high - here :]
        if high < rank:
            inner[high:, first:] -= product(share, panel[:, first - here :], (0,))
        side = product(inverse, image[low:high, :], (1,))
        image[low:high, :] = side
        if high < rank:
            image[high:, :] -= product(share, side, (0,))


def finish_kernel(
    order_ref, left_ref, right_ref, moved_hbm, bathed_hbm, out_hbm,
    gram, inner, image, start, lowest, moved, bathed, out, in_sems, out_sems,
):
    rank = left_ref.shape[0]
    load_moved = pltpu.make_async_copy(moved_hbm, moved, in_sems.at[0])
    load_bathed = pltpu.make_async_copy(bathed_hbm, bathed, in_sems.at[1])
    load_moved.start()
    load_bathed.start()

    chunks = order_ref.shape[0]
    size = rank // chunks
    half = rank // 2
    for i in range(chunks):
        rows = pl.ds(pl.multiple_of(order_ref[i] * size, size), size)
        below = pl.ds(pl.multiple_of(rank + order_ref[i] * size, size), size)
        chunk = jnp.concatenate(
            [left_ref[i * size : (i + 1) * size, :], right_ref[i * size : (i + 1) * size, :]], axis=1
        )

        @pl.when(order_ref[i] < chunks // 2)
        def _():
            gram[rows, :] = chunk[:, : 2 * rank]
            gram[below, rank : rank + half] = chunk[:, 2 * rank :]

        @pl.when(order_ref[i] >= chunks // 2)
        def _():
            gram[rows, half:] = chunk[:, : rank + half]
            gram[below, rank:] = chunk[:, rank + half :]

    gram[half:rank, :half] = gram[:half, half:rank].T
    gram[rank : rank + half, rank + half :] = gram[rank + half :, rank : rank + half].T
    gram[rank:, :rank] = gram[:rank, rank:].T
    largest = jnp.max(jnp.max(jnp.abs(gram[...]), axis=0, keepdims=True), axis=1, keepdims=True)
    gram[...] = gram[...] * (1.0 / largest)
    product = jnp.dot(gram[:rank, :], gram[...], precision=HIGHEST, preferred_element_type=jnp.float32)

    def inner_product():
        rows = image[...]
        inner[...] = lax.dot_general(
            rows, rows, (((1,), (1,)), ((), ())),
            precision=HIGHEST, preferred_element_type=jnp.float32,
        )

    image[...] = product
    inner_product()
    eliminate(inner, image, start, lowest)
    safe = jnp.min(lowest[...]) >= SMALLEST_PIVOT

    @pl.when(jnp.logical_not(safe))
    def _():
        later = jnp.dot(gram[:rank, :], gram[...], precision=HIGHEST, preferred_element_type=jnp.float32)
        inner[...] = later[:, :rank]
        image[:, rank:] = later[:, rank:]
        eliminate(inner, image.at[:, rank:], start, lowest)
        upper = lax.broadcasted_iota(jnp.int32, (rank, rank), 0) <= lax.broadcasted_iota(jnp.int32, (rank, rank), 1)
        image[:, :rank] = jnp.where(upper, inner[...], 0.0)
        inner_product()
        eliminate(inner, image, start, lowest)

    rotation = image[...].T.astype(jnp.bfloat16)
    load_moved.wait()
    load_bathed.wait()
    pieces = out_sems.shape[0]
    size = moved.shape[0] // pieces

    def store(piece):
        rows = pl.ds(pl.multiple_of(piece * size, size), size)
        return pltpu.make_async_copy(out.at[rows, :], out_hbm.at[rows, :], out_sems.at[piece])

    def one(piece, carry):
        rows = pl.ds(pl.multiple_of(piece * size, size), size)
        stacked = jnp.concatenate([moved[rows, :], bathed[rows, :]], axis=1)
        value = jnp.dot(stacked, rotation, preferred_element_type=jnp.float32)
        out[rows, :] = value.astype(jnp.bfloat16)
        store(piece).start()
        return carry

    lax.fori_loop(0, pieces, one, 0)

    def drain(piece, carry):
        store(piece).wait()
        return carry

    lax.fori_loop(0, pieces, drain, 0)


def finish_part(order, left, right, moved, bathed):
    rows, rank = moved.shape
    return pl.pallas_call(
        finish_kernel,
        in_specs=[
            pl.BlockSpec(memory_space=pltpu.SMEM),
            pl.BlockSpec(memory_space=pltpu.VMEM),
            pl.BlockSpec(memory_space=pltpu.VMEM),
            pl.BlockSpec(memory_space=pltpu.HBM),
            pl.BlockSpec(memory_space=pltpu.HBM),
        ],
        out_specs=pl.BlockSpec(memory_space=pl.ANY),
        out_shape=jax.ShapeDtypeStruct((rows, rank), jnp.bfloat16),
        scratch_shapes=[
            pltpu.VMEM((2 * rank, 2 * rank), jnp.float32),
            pltpu.VMEM((rank, rank), jnp.float32),
            pltpu.VMEM((rank, 2 * rank), jnp.float32),
            pltpu.VMEM((rank, 2 * PANEL), jnp.float32),
            pltpu.VMEM((8, 2 * PANEL), jnp.float32),
            pltpu.VMEM((rows, rank), jnp.bfloat16),
            pltpu.VMEM((rows, rank), jnp.bfloat16),
            pltpu.VMEM((rows, rank), jnp.bfloat16),
            pltpu.SemaphoreType.DMA((2,)),
            pltpu.SemaphoreType.DMA((8,)),
        ],
        compiler_params=pltpu.CompilerParams(vmem_limit_bytes=14 * 2**20),
        name="finish",
    )(order, left, right, moved, bathed)


def ring_order(count):
    wide = 2
    while 4 * wide * wide <= count:
        wide *= 2
    tall = count // wide
    walk = [0]
    for r in range(tall):
        across = range(1, wide)
        walk += [r * wide + c for c in (across if r % 2 == 0 else reversed(across))]
    return walk + [r * wide for r in range(tall - 1, 0, -1)]


PIECES = 4


def tie(one, other):
    return lax.optimization_barrier((one, other))


def early_steps():
    return lax.axis_size("col") // 2 - 1


def ring_gather(own, side, stages, small, early):
    order = ring_order(lax.axis_size("col"))
    following = order[1:] + order[:1]
    forward = list(zip(order, following))
    back = list(zip(following, order))
    size = own.shape[0] // PIECES
    pieces = [own[i * size : (i + 1) * size] for i in range(PIECES)]
    stages = list(stages)
    steps = []
    total = None
    for step in range(1, len(order)):
        if step > 1:
            pieces[-1], side = tie(pieces[-1], side)
        if step == 3:
            pieces[-1], small = tie(pieces[-1], small)
        if step == early_steps() + 3:
            total = early(small, [piece for done in steps[: early_steps()] for piece in done])
            pieces[-1], total = tie(pieces[-1], total)
        pieces = [
            lax.ppermute(piece, "col", forward if i < PIECES // 2 else back)
            for i, piece in enumerate(pieces)
        ]
        if step > 1 and stages:
            side = stages.pop(0)(side)
        steps.append(list(pieces))
    return steps, side, small, total


def slot_lists(ids, counts, kinds):
    blocks, slots = ids.shape
    count = lax.axis_size("col")
    order = ring_order(count)
    place = jnp.asarray([order.index(c) for c in range(count)], jnp.int32)
    col = jnp.arange(count, dtype=jnp.int32)
    mine = jnp.sum(jnp.where(col == lax.axis_index("col"), place, 0))
    owner, within = ids // blocks, ids % blocks
    theirs = jnp.sum(jnp.where(owner[..., None] == col, place, 0), axis=-1)
    in_piece = blocks // PIECES
    piece = within // in_piece
    step = jnp.where(piece >= PIECES // 2, theirs - mine, mine - theirs) % count
    before = early_steps()
    part = (step > before).astype(jnp.int32) + (step == count - 1).astype(jnp.int32)
    origin = jnp.where(
        part == 0,
        jnp.where(step == 0, 0, 1 + (step - 1) * PIECES + piece),
        jnp.where(part == 1, (step - before - 1) * PIECES + piece, piece),
    )
    offset = jnp.where(step == 0, within, within % in_piece)
    slot = jnp.arange(slots, dtype=jnp.int32)
    used = slot[None, :] < counts[:, None]
    key = jnp.where(used, part, 3) * slots + slot
    rank = jnp.sum((key[:, None, :] < key[:, :, None]).astype(jnp.int32), axis=-1)
    at = rank[:, :, None] == slot

    def arrange(values):
        return jnp.sum(jnp.where(at, values[:, :, None], 0), axis=1)

    origin, offset, kinds = arrange(origin), arrange(offset), arrange(kinds)
    parts = []
    first = jnp.zeros_like(counts)
    for i in range(3):
        number = jnp.sum((used & (part == i)).astype(jnp.int32), axis=1)
        parts.append((origin, offset, first, number, kinds))
        first = first + number
    return parts


def swap(value, axis, stride):
    count = lax.axis_size(axis)
    return lax.ppermute(value, axis, [(i, i ^ stride) for i in range(count)])


def strides(axis):
    return [1 << i for i in range(lax.axis_size(axis).bit_length() - 1)]


def side_of(axis, stride):
    return (lax.axis_index(axis) >> (stride.bit_length() - 1)) & 1


def halve(value, swapped, lower):
    half = value.shape[0] // 2
    keep = jnp.where(lower, value[:half], value[half:])
    give = jnp.where(lower, value[half:], value[:half])
    return keep + swap(give, *swapped)


def sum_relative(value, col_strides):
    for stride in col_strides:
        value = value + swap(value, "col", stride)
    for stride in reversed(strides("row")):
        value = jnp.concatenate([value, swap(value, "row", stride)], axis=0)
    return value


def pack(upper, corner, lower):
    half = corner.shape[1] // 2
    left = jnp.where(lower, upper[:, : 3 * half], upper[:, half:])
    right = jnp.where(lower, jnp.concatenate([upper[:, 3 * half :], corner[:, :half]], axis=1), corner)
    return left, right


def chunk_order():
    swaps = strides("row")
    relative = jnp.arange(1 << len(swaps), dtype=jnp.int32)
    mine = jnp.zeros_like(relative)
    for i, stride in enumerate(swaps):
        mine = mine + (side_of("row", stride) << (len(swaps) - 1 - i))
    return relative ^ mine


def shards(
    density_factor,
    onsite,
    neighbour_ids,
    neighbour_count,
    coupling_type,
    coupling_blocks,
    bath_pattern,
    bath_blocks,
):
    blocks, slots = neighbour_ids.shape
    group_blocks = lax.axis_size("col") * blocks
    in_group = neighbour_ids - lax.axis_index("row") * group_blocks
    lists = slot_lists(in_group, neighbour_count, coupling_type)
    bathed, corner = bath_part(density_factor, bath_pattern, bath_blocks)
    energy = onsite.reshape(blocks, -1)
    swaps = strides("row")
    lower = [side_of("row", stride) == 0 for stride in swaps]

    def over_row(value, lower):
        for stride, chosen in zip(swaps, lower):
            value = halve(value, ("row", stride), chosen)
        return value

    def early(small, pieces):
        lists, energy, _, _ = small
        return early_part(lists[0], [density_factor] + pieces, coupling_blocks, density_factor, energy)

    steps, corner, small, total = ring_gather(
        density_factor,
        corner,
        [lambda value: over_row(value, lower)],
        (lists, energy, chunk_order(), lower),
        early,
    )
    lists, _, order, lower = small
    between = [piece for step in steps[early_steps() : -1] for piece in step]
    total = middle_part(lists[1], between, coupling_blocks, total)
    moved, upper = late_part(lists[2], steps[-1], coupling_blocks, total, bathed)
    left, right = pack(over_row(upper, lower), corner, lower[0])
    col_strides = strides("col")
    left = sum_relative(left, col_strides)
    right = sum_relative(right, col_strides[1:] + col_strides[:1])
    return finish_part(order, left, right, moved, bathed)


def solution(mesh):
    placed = (
        P(("row", "col"), None),
        P(("row", "col")),
        P(("row", "col"), None),
        P(("row", "col")),
        P(("row", "col"), None),
        P(),
        P(("row", "col")),
        P(),
    )
    return jax.shard_map(
        shards, mesh=mesh, in_specs=placed, out_specs=P(("row", "col"), None), check_vma=False
    )
```

```python
import jax
import jax.numpy as jnp
from jax import lax
from jax.experimental import pallas as pl
from jax.experimental.pallas import tpu as pltpu
from jax.sharding import PartitionSpec as P

time_step = 0.25
PANEL = 64
SMALLEST_PIVOT = 1 / 64
HIGHEST = lax.Precision.HIGHEST


def bath_kernel(pattern_ref, bath_ref, own_ref, bathed_ref, gram_ref):
    bathed = jnp.dot(bath_ref[0], own_ref[...], preferred_element_type=jnp.float32).astype(jnp.bfloat16)
    bathed_ref[...] = bathed
    part = lax.dot_general(
        bathed, bathed, (((0,), (0,)), ((), ())), preferred_element_type=jnp.float32
    )

    @pl.when(pl.program_id(0) == 0)
    def _():
        gram_ref[...] = part

    @pl.when(pl.program_id(0) > 0)
    def _():
        gram_ref[...] += part


def bath_part(own, bath_pattern, bath_blocks):
    blocks = bath_pattern.shape[0]
    block_rows = bath_blocks.shape[1]
    rows, rank = own.shape
    tile = pl.BlockSpec((block_rows, rank), lambda b, kind: (b, 0))
    return pl.pallas_call(
        bath_kernel,
        grid_spec=pltpu.PrefetchScalarGridSpec(
            num_scalar_prefetch=1,
            grid=(blocks,),
            in_specs=[
                pl.BlockSpec((1, block_rows, block_rows), lambda b, kind: (kind[b], 0, 0)),
                tile,
            ],
            out_specs=[tile, pl.BlockSpec((rank, rank), lambda b, kind: (0, 0))],
        ),
        out_shape=[
            jax.ShapeDtypeStruct((rows, rank), jnp.bfloat16),
            jax.ShapeDtypeStruct((rank, rank), jnp.float32),
        ],
        compiler_params=pltpu.CompilerParams(vmem_limit_bytes=7 * 2**20),
        name="bath",
    )(bath_pattern, bath_blocks, own)


def gather_products(
    origin_ref, offset_ref, first_ref, count_ref, kind_ref, sources, coupling_ref, held, sems, total, visits=None
):
    blocks, slots = origin_ref.shape
    block_rows = held.shape[2]
    here = pl.program_id(0)
    last = blocks if visits is None else visits[1][0]
    group = 1
    while group * group < len(sources):
        group += 1

    def block_of(step):
        return step if visits is None else visits[0][step]

    def copy(source, step, slot):
        start = pl.multiple_of(offset_ref[block_of(step), slot] * block_rows, block_rows)
        return pltpu.make_async_copy(
            source.at[pl.ds(start, block_rows), :],
            held.at[lax.rem(step, 2), slot],
            sems.at[lax.rem(step, 2), slot],
        )

    def fetch(step):
        block = block_of(step)

        def one(slot, carry):
            origin = origin_ref[block, slot]
            for low in range(0, len(sources), group):
                high = min(low + group, len(sources))

                @pl.when((origin >= low) & (origin < high))
                def _():
                    for place in range(low, high):
                        @pl.when(origin == place)
                        def _():
                            copy(sources[place], step, slot).start()
            return carry

        lax.fori_loop(first_ref[block], first_ref[block] + count_ref[block], one, 0)

    @pl.when(here == 0)
    def _():
        fetch(0)

    @pl.when(here + 1 < last)
    def _():
        fetch(here + 1)

    b = block_of(here)

    def product(slot):
        copy(sources[0], here, slot).wait()
        return jnp.dot(
            coupling_ref[kind_ref[b, slot]],
            held[lax.rem(here, 2), slot],
            preferred_element_type=jnp.float32,
        )

    first, count = first_ref[b], count_ref[b]

    def add_two(pair, carry):
        slot = first + 2 * pair
        total[...] -= time_step * (product(slot) + product(slot + 1))
        return carry

    lax.fori_loop(0, count // 2, add_two, 0)

    @pl.when(lax.rem(count, 2) == 1)
    def _():
        total[...] -= time_step * product(first + count - 1)


def early_kernel(origin_ref, offset_ref, first_ref, count_ref, kind_ref, *refs):
    sources = refs[:-8]
    coupling_hbm, own_ref, energy_ref, total_ref, coupling, held, sems, coupling_sem = refs[-8:]
    block_rows = own_ref.shape[0]
    load = pltpu.make_async_copy(coupling_hbm, coupling, coupling_sem)

    @pl.when(pl.program_id(0) == 0)
    def _():
        load.start()

    row = energy_ref[pl.ds(pl.program_id(0), 1), :]
    energy = jnp.broadcast_to(row, (8, block_rows)).T[:, :1]
    wide = own_ref[...].astype(jnp.float32)
    total_ref[...] = wide - time_step * (energy * wide)

    @pl.when(pl.program_id(0) == 0)
    def _():
        load.wait()

    gather_products(
        origin_ref, offset_ref, first_ref, count_ref, kind_ref, sources, coupling, held, sems, total_ref
    )


def middle_kernel(origin_ref, offset_ref, first_ref, count_ref, kind_ref, *refs):
    sources = refs[:-5]
    coupling_ref, base_ref, total_ref, held, sems = refs[-5:]
    total_ref[...] = base_ref[...]
    gather_products(
        origin_ref, offset_ref, first_ref, count_ref, kind_ref, sources, coupling_ref, held, sems, total_ref
    )


def gram_part(moved, bathed):
    both = jnp.concatenate([moved, bathed], axis=1)
    return lax.dot_general(moved, both, (((0,), (0,)), ((), ())), preferred_element_type=jnp.float32)


def settle_kernel(origin_ref, offset_ref, first_ref, count_ref, kind_ref, settled_ref, *refs):
    sources = refs[:-8]
    coupling_ref, base_ref, bathed_ref, total_ref, moved_ref, gram_ref, held, sems = refs[-8:]
    b = pl.program_id(0)
    total_ref[...] = base_ref[...]
    gather_products(
        origin_ref, offset_ref, first_ref, count_ref, kind_ref, sources, coupling_ref, held, sems, total_ref
    )
    moved = total_ref[...].astype(jnp.bfloat16)
    moved_ref[...] = moved

    @pl.when(b == 0)
    def _():
        gram_ref[...] = jnp.zeros_like(gram_ref)

    @pl.when(settled_ref[b] == 1)
    def _():
        gram_ref[...] += gram_part(moved, bathed_ref[...])


def late_kernel(origin_ref, offset_ref, first_ref, count_ref, kind_ref, visit_ref, number_ref, *refs):
    sources = refs[:-10]
    coupling_ref, base_ref, bathed_ref, _, before_ref, moved_ref, gram_ref, total, held, sems = refs[-10:]
    b = pl.program_id(0)

    @pl.when(b == 0)
    def _():
        gram_ref[...] = before_ref[...]

    @pl.when(b < number_ref[0])
    def _():
        total[...] = base_ref[...]
        gather_products(
            origin_ref, offset_ref, first_ref, count_ref, kind_ref, sources, coupling_ref, held, sems, total,
            visits=(visit_ref, number_ref),
        )
        moved = total[...].astype(jnp.bfloat16)
        moved_ref[...] = moved
        gram_ref[...] += gram_part(moved, bathed_ref[...])


def early_part(lists, sources, coupling_blocks, own, energy):
    blocks, slots = lists[0].shape
    kinds, block_rows, _ = coupling_blocks.shape
    rows, rank = own.shape
    tile = pl.BlockSpec((block_rows, rank), lambda b, *_: (b, 0))
    return pl.pallas_call(
        early_kernel,
        grid_spec=pltpu.PrefetchScalarGridSpec(
            num_scalar_prefetch=5,
            grid=(blocks,),
            in_specs=[
                *[pl.BlockSpec(memory_space=pltpu.HBM) for _ in sources],
                pl.BlockSpec(memory_space=pltpu.HBM),
                tile,
                pl.BlockSpec((blocks, block_rows), lambda b, *_: (0, 0)),
            ],
            out_specs=tile,
            scratch_shapes=[
                pltpu.VMEM((kinds, block_rows, block_rows), jnp.bfloat16),
                pltpu.VMEM((2, slots, block_rows, rank), jnp.bfloat16),
                pltpu.SemaphoreType.DMA((2, slots)),
                pltpu.SemaphoreType.DMA,
            ],
        ),
        out_shape=jax.ShapeDtypeStruct((rows, rank), jnp.float32),
        compiler_params=pltpu.CompilerParams(vmem_limit_bytes=12 * 2**20),
        cost_estimate=pl.CostEstimate(
            flops=blocks * slots * block_rows * block_rows * rank,
            bytes_accessed=blocks * slots * block_rows * rank * 2,
            transcendentals=0,
        ),
        name="couple_early",
    )(*lists, *sources, coupling_blocks, own, energy)


def middle_part(lists, sources, coupling_blocks, base):
    blocks, slots = lists[0].shape
    kinds, block_rows, _ = coupling_blocks.shape
    rows, rank = base.shape
    tile = pl.BlockSpec((block_rows, rank), lambda b, *_: (b, 0))
    return pl.pallas_call(
        middle_kernel,
        grid_spec=pltpu.PrefetchScalarGridSpec(
            num_scalar_prefetch=5,
            grid=(blocks,),
            in_specs=[
                *[pl.BlockSpec(memory_space=pl.ANY) for _ in sources],
                pl.BlockSpec((kinds, block_rows, block_rows), lambda b, *_: (0, 0, 0)),
                tile,
            ],
            out_specs=tile,
            scratch_shapes=[
                pltpu.VMEM((2, slots, block_rows, rank), jnp.bfloat16),
                pltpu.SemaphoreType.DMA((2, slots)),
            ],
        ),
        out_shape=jax.ShapeDtypeStruct((rows, rank), jnp.float32),
        compiler_params=pltpu.CompilerParams(vmem_limit_bytes=14 * 2**20),
        cost_estimate=pl.CostEstimate(
            flops=blocks * slots * block_rows * block_rows * rank,
            bytes_accessed=blocks * slots * block_rows * rank * 2,
            transcendentals=0,
        ),
        name="couple_middle",
    )(*lists, *sources, coupling_blocks, base)


def settle_part(lists, settled, sources, coupling_blocks, base, bathed):
    blocks, slots = lists[0].shape
    kinds, block_rows, _ = coupling_blocks.shape
    rows, rank = base.shape
    tile = pl.BlockSpec((block_rows, rank), lambda b, *_: (b, 0))
    return pl.pallas_call(
        settle_kernel,
        grid_spec=pltpu.PrefetchScalarGridSpec(
            num_scalar_prefetch=6,
            grid=(blocks,),
            in_specs=[
                *[pl.BlockSpec(memory_space=pl.ANY) for _ in sources],
                pl.BlockSpec((kinds, block_rows, block_rows), lambda b, *_: (0, 0, 0)),
                tile,
                tile,
            ],
            out_specs=[tile, tile, pl.BlockSpec((rank, 2 * rank), lambda b, *_: (0, 0))],
            scratch_shapes=[
                pltpu.VMEM((2, slots, block_rows, rank), jnp.bfloat16),
                pltpu.SemaphoreType.DMA((2, slots)),
            ],
        ),
        out_shape=[
            jax.ShapeDtypeStruct((rows, rank), jnp.float32),
            jax.ShapeDtypeStruct((rows, rank), jnp.bfloat16),
            jax.ShapeDtypeStruct((rank, 2 * rank), jnp.float32),
        ],
        compiler_params=pltpu.CompilerParams(vmem_limit_bytes=16 * 2**20),
        cost_estimate=pl.CostEstimate(
            flops=blocks * slots * block_rows * block_rows * rank,
            bytes_accessed=blocks * slots * block_rows * rank * 2,
            transcendentals=0,
        ),
        name="couple_settle",
    )(*lists, settled, *sources, coupling_blocks, base, bathed)


def late_part(lists, visits, number, sources, coupling_blocks, base, bathed, moved, gram):
    blocks, slots = lists[0].shape
    kinds, block_rows, _ = coupling_blocks.shape
    rows, rank = base.shape

    def visited(b, *scalars):
        return scalars[5][jnp.minimum(b, scalars[6][0] - 1)], 0

    tile = pl.BlockSpec((block_rows, rank), visited)
    whole = pl.BlockSpec((rank, 2 * rank), lambda b, *_: (0, 0))
    return pl.pallas_call(
        late_kernel,
        grid_spec=pltpu.PrefetchScalarGridSpec(
            num_scalar_prefetch=7,
            grid=(blocks,),
            in_specs=[
                *[pl.BlockSpec(memory_space=pl.ANY) for _ in sources],
                pl.BlockSpec((kinds, block_rows, block_rows), lambda b, *_: (0, 0, 0)),
                tile,
                tile,
                pl.BlockSpec(memory_space=pl.ANY),
                whole,
            ],
            out_specs=[tile, whole],
            scratch_shapes=[
                pltpu.VMEM((block_rows, rank), jnp.float32),
                pltpu.VMEM((2, slots, block_rows, rank), jnp.bfloat16),
                pltpu.SemaphoreType.DMA((2, slots)),
            ],
        ),
        out_shape=[
            jax.ShapeDtypeStruct((rows, rank), jnp.bfloat16),
            jax.ShapeDtypeStruct((rank, 2 * rank), jnp.float32),
        ],
        input_output_aliases={7 + len(sources) + 3: 0},
        compiler_params=pltpu.CompilerParams(vmem_limit_bytes=16 * 2**20),
        name="couple_late",
    )(*lists, visits, number, *sources, coupling_blocks, base, bathed, moved, gram)


def inverse_factor(square, start, lowest):
    n = square.shape[0]
    eye = (
        lax.broadcasted_iota(jnp.int32, (n, n), 0) == lax.broadcasted_iota(jnp.int32, (n, n), 1)
    ).astype(jnp.float32)
    work = jnp.concatenate([square, eye], axis=1)
    bands = [work[8 * i : 8 * i + 8, :] for i in range(n // 8)]
    sublane = lax.broadcasted_iota(jnp.int32, (8, 2 * n), 0)
    def spread(band, g):
        return [jnp.broadcast_to(band[:, 8 * g + r : 8 * g + r + 1], (8, 2 * n)) for r in range(8)]

    out = []
    for g in range(n // 8):
        band = bands[g]
        pivots = spread(band, g)
        diagonal = jnp.zeros((8, 2 * n), jnp.float32)
        scales = []
        for r in range(8):
            scales.append(pl.reciprocal(pivots[r][r : r + 1, :], approx=True))
            diagonal = jnp.where(sublane == r, pivots[r], diagonal)
            share = jnp.where(sublane > r, pivots[r] * scales[r], 0.0)
            for q in range(r + 1, 8):
                pivots[q] = pivots[q] - share * pivots[q][r : r + 1, :]
            band = band - share * band[r : r + 1, :]
        out.append(band[:, n:] * lax.rsqrt(diagonal)[:, n:])
        lowest[...] = jnp.minimum(lowest[...], diagonal / start[8 * g : 8 * g + 8, :])
        for i in range(g + 1, n // 8):
            columns = spread(bands[i], g)
            below = bands[i]
            for r in range(8):
                share = columns[r] * scales[r]
                for q in range(r + 1, 8):
                    columns[q] = columns[q] - share * pivots[q][r : r + 1, :]
                below = below - share * band[r : r + 1, :]
            bands[i] = below
    return jnp.concatenate(out, axis=0)


def eliminate(inner, image, start, lowest):
    rank = inner.shape[0]
    diagonal = lax.broadcasted_iota(jnp.int32, (rank, rank), 0) == lax.broadcasted_iota(jnp.int32, (rank, rank), 1)
    start[...] = jnp.broadcast_to(
        jnp.sum(jnp.where(diagonal, inner[...], 0.0), axis=1, keepdims=True), start.shape
    )
    lowest[...] = jnp.ones_like(lowest)

    def product(left, right, contract):
        return lax.dot_general(
            left, right, ((contract, (0,)), ((), ())),
            precision=HIGHEST, preferred_element_type=jnp.float32,
        )

    for low in range(0, rank, PANEL):
        high = low + PANEL
        here, first = low // 128 * 128, high // 128 * 128
        inverse = inverse_factor(inner[low:high, low:high], start[low:high, :], lowest)
        panel = product(inverse, inner[low:high, here:], (1,))
        inner[low:high, here:] = panel
        share = panel[:, high - here :]
        if high < rank:
            inner[high:, first:] -= product(share, panel[:, first - here :], (0,))
        side = product(inverse, image[low:high, :], (1,))
        image[low:high, :] = side
        if high < rank:
            image[high:, :] -= product(share, side, (0,))


def finish_kernel(
    order_ref, left_ref, right_ref, moved_hbm, bathed_hbm, out_hbm,
    gram, inner, image, start, lowest, moved, bathed, out, in_sems, out_sems,
):
    rank = left_ref.shape[0]
    load_moved = pltpu.make_async_copy(moved_hbm, moved, in_sems.at[0])
    load_bathed = pltpu.make_async_copy(bathed_hbm, bathed, in_sems.at[1])
    load_moved.start()
    load_bathed.start()

    chunks = order_ref.shape[0]
    size = rank // chunks
    half = rank // 2
    for i in range(chunks):
        rows = pl.ds(pl.multiple_of(order_ref[i] * size, size), size)
        below = pl.ds(pl.multiple_of(rank + order_ref[i] * size, size), size)
        chunk = jnp.concatenate(
            [left_ref[i * size : (i + 1) * size, :], right_ref[i * size : (i + 1) * size, :]], axis=1
        )

        @pl.when(order_ref[i] < chunks // 2)
        def _():
            gram[rows, :] = chunk[:, : 2 * rank]
            gram[below, rank : rank + half] = chunk[:, 2 * rank :]

        @pl.when(order_ref[i] >= chunks // 2)
        def _():
            gram[rows, half:] = chunk[:, : rank + half]
            gram[below, rank:] = chunk[:, rank + half :]

    gram[half:rank, :half] = gram[:half, half:rank].T
    gram[rank : rank + half, rank + half :] = gram[rank + half :, rank : rank + half].T
    gram[rank:, :rank] = gram[:rank, rank:].T
    largest = jnp.max(jnp.max(jnp.abs(gram[...]), axis=0, keepdims=True), axis=1, keepdims=True)
    gram[...] = gram[...] * (1.0 / largest)
    product = jnp.dot(gram[:rank, :], gram[...], precision=HIGHEST, preferred_element_type=jnp.float32)

    def inner_product():
        rows = image[...]
        inner[...] = lax.dot_general(
            rows, rows, (((1,), (1,)), ((), ())),
            precision=HIGHEST, preferred_element_type=jnp.float32,
        )

    image[...] = product
    inner_product()
    eliminate(inner, image, start, lowest)
    safe = jnp.min(lowest[...]) >= SMALLEST_PIVOT

    @pl.when(jnp.logical_not(safe))
    def _():
        later = jnp.dot(gram[:rank, :], gram[...], precision=HIGHEST, preferred_element_type=jnp.float32)
        inner[...] = later[:, :rank]
        image[:, rank:] = later[:, rank:]
        eliminate(inner, image.at[:, rank:], start, lowest)
        upper = lax.broadcasted_iota(jnp.int32, (rank, rank), 0) <= lax.broadcasted_iota(jnp.int32, (rank, rank), 1)
        image[:, :rank] = jnp.where(upper, inner[...], 0.0)
        inner_product()
        eliminate(inner, image, start, lowest)

    rotation = image[...].T.astype(jnp.bfloat16)
    load_moved.wait()
    load_bathed.wait()
    pieces = out_sems.shape[0]
    size = moved.shape[0] // pieces

    def store(piece):
        rows = pl.ds(pl.multiple_of(piece * size, size), size)
        return pltpu.make_async_copy(out.at[rows, :], out_hbm.at[rows, :], out_sems.at[piece])

    def one(piece, carry):
        rows = pl.ds(pl.multiple_of(piece * size, size), size)
        stacked = jnp.concatenate([moved[rows, :], bathed[rows, :]], axis=1)
        value = jnp.dot(stacked, rotation, preferred_element_type=jnp.float32)
        out[rows, :] = value.astype(jnp.bfloat16)
        store(piece).start()
        return carry

    lax.fori_loop(0, pieces, one, 0)

    def drain(piece, carry):
        store(piece).wait()
        return carry

    lax.fori_loop(0, pieces, drain, 0)


def finish_part(order, left, right, moved, bathed):
    rows, rank = moved.shape
    return pl.pallas_call(
        finish_kernel,
        in_specs=[
            pl.BlockSpec(memory_space=pltpu.SMEM),
            pl.BlockSpec(memory_space=pltpu.VMEM),
            pl.BlockSpec(memory_space=pltpu.VMEM),
            pl.BlockSpec(memory_space=pltpu.HBM),
            pl.BlockSpec(memory_space=pltpu.HBM),
        ],
        out_specs=pl.BlockSpec(memory_space=pl.ANY),
        out_shape=jax.ShapeDtypeStruct((rows, rank), jnp.bfloat16),
        scratch_shapes=[
            pltpu.VMEM((2 * rank, 2 * rank), jnp.float32),
            pltpu.VMEM((rank, rank), jnp.float32),
            pltpu.VMEM((rank, 2 * rank), jnp.float32),
            pltpu.VMEM((rank, 2 * PANEL), jnp.float32),
            pltpu.VMEM((8, 2 * PANEL), jnp.float32),
            pltpu.VMEM((rows, rank), jnp.bfloat16),
            pltpu.VMEM((rows, rank), jnp.bfloat16),
            pltpu.VMEM((rows, rank), jnp.bfloat16),
            pltpu.SemaphoreType.DMA((2,)),
            pltpu.SemaphoreType.DMA((8,)),
        ],
        compiler_params=pltpu.CompilerParams(vmem_limit_bytes=14 * 2**20),
        name="finish",
    )(order, left, right, moved, bathed)


def ring_order(count):
    wide = 2
    while 4 * wide * wide <= count:
        wide *= 2
    tall = count // wide
    walk = [0]
    for r in range(tall):
        across = range(1, wide)
        walk += [r * wide + c for c in (across if r % 2 == 0 else reversed(across))]
    return walk + [r * wide for r in range(tall - 1, 0, -1)]


PIECES = 4


def tie(one, other):
    return lax.optimization_barrier((one, other))


def early_steps():
    return lax.axis_size("col") // 2 - 1


def ring_gather(own, side, stages, small, early):
    order = ring_order(lax.axis_size("col"))
    following = order[1:] + order[:1]
    forward = list(zip(order, following))
    back = list(zip(following, order))
    size = own.shape[0] // PIECES
    pieces = [own[i * size : (i + 1) * size] for i in range(PIECES)]
    stages = list(stages)
    steps = []
    total = None
    for step in range(1, len(order)):
        if step > 1:
            pieces[-1], side = tie(pieces[-1], side)
        if step == 3:
            pieces[-1], small = tie(pieces[-1], small)
        if step == early_steps() + 3:
            total = early(small, [piece for done in steps[: early_steps()] for piece in done])
            pieces[-1], total = tie(pieces[-1], total)
        pieces = [
            lax.ppermute(piece, "col", forward if i < PIECES // 2 else back)
            for i, piece in enumerate(pieces)
        ]
        if step > 1 and stages:
            side = stages.pop(0)(side)
        steps.append(list(pieces))
    return steps, side, small, total


def slot_lists(ids, counts, kinds):
    blocks, slots = ids.shape
    count = lax.axis_size("col")
    order = ring_order(count)
    place = jnp.asarray([order.index(c) for c in range(count)], jnp.int32)
    col = jnp.arange(count, dtype=jnp.int32)
    mine = jnp.sum(jnp.where(col == lax.axis_index("col"), place, 0))
    owner, within = ids // blocks, ids % blocks
    theirs = jnp.sum(jnp.where(owner[..., None] == col, place, 0), axis=-1)
    in_piece = blocks // PIECES
    piece = within // in_piece
    step = jnp.where(piece >= PIECES // 2, theirs - mine, mine - theirs) % count
    before = early_steps()
    last = step == count - 1
    outer = (piece == 0) | (piece == PIECES - 1)
    part = (step > before).astype(jnp.int32) + last.astype(jnp.int32) + (last & ~outer).astype(jnp.int32)
    origin = jnp.where(
        part == 0,
        jnp.where(step == 0, 0, 1 + (step - 1) * PIECES + piece),
        jnp.where(part == 1, (step - before - 1) * PIECES + piece, jnp.where(outer, piece // (PIECES - 1), piece - 1)),
    )
    offset = jnp.where(step == 0, within, within % in_piece)
    slot = jnp.arange(slots, dtype=jnp.int32)
    used = slot[None, :] < counts[:, None]
    key = jnp.where(used, part, 4) * slots + slot
    rank = jnp.sum((key[:, None, :] < key[:, :, None]).astype(jnp.int32), axis=-1)
    at = rank[:, :, None] == slot

    def arrange(values):
        return jnp.sum(jnp.where(at, values[:, :, None], 0), axis=1)

    origin, offset, kinds = arrange(origin), arrange(offset), arrange(kinds)
    parts = []
    first = jnp.zeros_like(counts)
    for i in range(4):
        number = jnp.sum((used & (part == i)).astype(jnp.int32), axis=1)
        parts.append((origin, offset, first, number, kinds))
        first = first + number
    block = jnp.arange(blocks, dtype=jnp.int32)
    key = jnp.where(parts[3][3] > 0, 0, blocks) + block
    turn = jnp.sum((key[None, :] < key[:, None]).astype(jnp.int32), axis=1)
    number = jnp.maximum(jnp.sum((parts[3][3] > 0).astype(jnp.int32), keepdims=True), 1)
    visits = jnp.sum(jnp.where(turn[:, None] == block, block[:, None], 0), axis=0)
    settled = (turn >= number).astype(jnp.int32)
    return parts, settled, visits, number


def swap(value, axis, stride):
    count = lax.axis_size(axis)
    return lax.ppermute(value, axis, [(i, i ^ stride) for i in range(count)])


def strides(axis):
    return [1 << i for i in range(lax.axis_size(axis).bit_length() - 1)]


def side_of(axis, stride):
    return (lax.axis_index(axis) >> (stride.bit_length() - 1)) & 1


def halve(value, swapped, lower):
    half = value.shape[0] // 2
    keep = jnp.where(lower, value[:half], value[half:])
    give = jnp.where(lower, value[half:], value[:half])
    return keep + swap(give, *swapped)


def sum_relative(value, col_strides):
    for stride in col_strides:
        value = value + swap(value, "col", stride)
    for stride in reversed(strides("row")):
        value = jnp.concatenate([value, swap(value, "row", stride)], axis=0)
    return value


def pack(upper, corner, lower):
    half = corner.shape[1] // 2
    left = jnp.where(lower, upper[:, : 3 * half], upper[:, half:])
    right = jnp.where(lower, jnp.concatenate([upper[:, 3 * half :], corner[:, :half]], axis=1), corner)
    return left, right


def chunk_order():
    swaps = strides("row")
    relative = jnp.arange(1 << len(swaps), dtype=jnp.int32)
    mine = jnp.zeros_like(relative)
    for i, stride in enumerate(swaps):
        mine = mine + (side_of("row", stride) << (len(swaps) - 1 - i))
    return relative ^ mine


def shards(
    density_factor,
    onsite,
    neighbour_ids,
    neighbour_count,
    coupling_type,
    coupling_blocks,
    bath_pattern,
    bath_blocks,
):
    blocks, slots = neighbour_ids.shape
    group_blocks = lax.axis_size("col") * blocks
    in_group = neighbour_ids - lax.axis_index("row") * group_blocks
    lists = slot_lists(in_group, neighbour_count, coupling_type)
    bathed, corner = bath_part(density_factor, bath_pattern, bath_blocks)
    energy = onsite.reshape(blocks, -1)
    swaps = strides("row")
    lower = [side_of("row", stride) == 0 for stride in swaps]

    def over_row(value, lower):
        for stride, chosen in zip(swaps, lower):
            value = halve(value, ("row", stride), chosen)
        return value

    def early(small, pieces):
        (lists, _, _, _), energy, _, _ = small
        return early_part(lists[0], [density_factor] + pieces, coupling_blocks, density_factor, energy)

    steps, corner, small, total = ring_gather(
        density_factor,
        corner,
        [lambda value: over_row(value, lower)],
        (lists, energy, chunk_order(), lower),
        early,
    )
    (lists, settled, visits, number), _, order, lower = small
    between = [piece for step in steps[early_steps() : -1] for piece in step]
    total = middle_part(lists[1], between, coupling_blocks, total)
    outer, inner = [steps[-1][0], steps[-1][-1]], steps[-1][1:-1]
    total, moved, upper = settle_part(lists[2], settled, outer, coupling_blocks, total, bathed)
    moved, upper = late_part(lists[3], visits, number, inner, coupling_blocks, total, bathed, moved, upper)
    left, right = pack(over_row(upper, lower), corner, lower[0])
    col_strides = strides("col")
    left = sum_relative(left, col_strides)
    right = sum_relative(right, col_strides[1:] + col_strides[:1])
    return finish_part(order, left, right, moved, bathed)


def solution(mesh):
    placed = (
        P(("row", "col"), None),
        P(("row", "col")),
        P(("row", "col"), None),
        P(("row", "col")),
        P(("row", "col"), None),
        P(),
        P(("row", "col")),
        P(),
    )
    return jax.shard_map(
        shards, mesh=mesh, in_specs=placed, out_specs=P(("row", "col"), None), check_vma=False
    )
```

```python
import jax
import jax.numpy as jnp
from jax import lax
from jax.experimental import pallas as pl
from jax.experimental.pallas import tpu as pltpu
from jax.sharding import PartitionSpec as P

time_step = 0.25
PANEL = 64
SMALLEST_PIVOT = 1 / 64
HIGHEST = lax.Precision.HIGHEST


def bath_kernel(pattern_ref, bath_ref, own_ref, bathed_ref, gram_ref):
    bathed = jnp.dot(bath_ref[0], own_ref[...], preferred_element_type=jnp.float32).astype(jnp.bfloat16)
    bathed_ref[...] = bathed
    part = lax.dot_general(
        bathed, bathed, (((0,), (0,)), ((), ())), preferred_element_type=jnp.float32
    )

    @pl.when(pl.program_id(0) == 0)
    def _():
        gram_ref[...] = part

    @pl.when(pl.program_id(0) > 0)
    def _():
        gram_ref[...] += part


def bath_part(own, bath_pattern, bath_blocks):
    blocks = bath_pattern.shape[0]
    block_rows = bath_blocks.shape[1]
    rows, rank = own.shape
    tile = pl.BlockSpec((block_rows, rank), lambda b, kind: (b, 0))
    return pl.pallas_call(
        bath_kernel,
        grid_spec=pltpu.PrefetchScalarGridSpec(
            num_scalar_prefetch=1,
            grid=(blocks,),
            in_specs=[
                pl.BlockSpec((1, block_rows, block_rows), lambda b, kind: (kind[b], 0, 0)),
                tile,
            ],
            out_specs=[tile, pl.BlockSpec((rank, rank), lambda b, kind: (0, 0))],
        ),
        out_shape=[
            jax.ShapeDtypeStruct((rows, rank), jnp.bfloat16),
            jax.ShapeDtypeStruct((rank, rank), jnp.float32),
        ],
        compiler_params=pltpu.CompilerParams(vmem_limit_bytes=7 * 2**20),
        name="bath",
    )(bath_pattern, bath_blocks, own)


def gather_products(
    origin_ref, offset_ref, first_ref, count_ref, kind_ref, sources, coupling_ref, held, sems, total, visits=None
):
    blocks, slots = origin_ref.shape
    block_rows = held.shape[2]
    here = pl.program_id(0)
    last = blocks if visits is None else visits[1][0]
    group = 1
    while group * group < len(sources):
        group += 1

    def block_of(step):
        return step if visits is None else visits[0][step]

    def copy(source, step, slot):
        start = pl.multiple_of(offset_ref[block_of(step), slot] * block_rows, block_rows)
        return pltpu.make_async_copy(
            source.at[pl.ds(start, block_rows), :],
            held.at[lax.rem(step, 2), slot],
            sems.at[lax.rem(step, 2), slot],
        )

    def fetch(step):
        block = block_of(step)

        def one(slot, carry):
            origin = origin_ref[block, slot]
            for low in range(0, len(sources), group):
                high = min(low + group, len(sources))

                @pl.when((origin >= low) & (origin < high))
                def _():
                    for place in range(low, high):
                        @pl.when(origin == place)
                        def _():
                            copy(sources[place], step, slot).start()
            return carry

        lax.fori_loop(first_ref[block], first_ref[block] + count_ref[block], one, 0)

    @pl.when(here == 0)
    def _():
        fetch(0)

    @pl.when(here + 1 < last)
    def _():
        fetch(here + 1)

    b = block_of(here)

    def product(slot):
        copy(sources[0], here, slot).wait()
        return jnp.dot(
            coupling_ref[kind_ref[b, slot]],
            held[lax.rem(here, 2), slot],
            preferred_element_type=jnp.float32,
        )

    first, count = first_ref[b], count_ref[b]

    def add_two(pair, carry):
        slot = first + 2 * pair
        total[...] -= time_step * (product(slot) + product(slot + 1))
        return carry

    lax.fori_loop(0, count // 2, add_two, 0)

    @pl.when(lax.rem(count, 2) == 1)
    def _():
        total[...] -= time_step * product(first + count - 1)


def early_kernel(origin_ref, offset_ref, first_ref, count_ref, kind_ref, *refs):
    sources = refs[:-8]
    coupling_hbm, own_ref, energy_ref, total_ref, coupling, held, sems, coupling_sem = refs[-8:]
    block_rows = own_ref.shape[0]
    load = pltpu.make_async_copy(coupling_hbm, coupling, coupling_sem)

    @pl.when(pl.program_id(0) == 0)
    def _():
        load.start()

    row = energy_ref[pl.ds(pl.program_id(0), 1), :]
    energy = jnp.broadcast_to(row, (8, block_rows)).T[:, :1]
    wide = own_ref[...].astype(jnp.float32)
    total_ref[...] = wide - time_step * (energy * wide)

    @pl.when(pl.program_id(0) == 0)
    def _():
        load.wait()

    gather_products(
        origin_ref, offset_ref, first_ref, count_ref, kind_ref, sources, coupling, held, sems, total_ref
    )


def middle_kernel(origin_ref, offset_ref, first_ref, count_ref, kind_ref, *refs):
    sources = refs[:-5]
    coupling_ref, base_ref, total_ref, held, sems = refs[-5:]
    total_ref[...] = base_ref[...]
    gather_products(
        origin_ref, offset_ref, first_ref, count_ref, kind_ref, sources, coupling_ref, held, sems, total_ref
    )


def gram_part(moved, bathed):
    both = jnp.concatenate([moved, bathed], axis=1)
    return lax.dot_general(moved, both, (((0,), (0,)), ((), ())), preferred_element_type=jnp.float32)


def settle_kernel(origin_ref, offset_ref, first_ref, count_ref, kind_ref, settled_ref, *refs):
    sources = refs[:-8]
    coupling_ref, base_ref, bathed_ref, total_ref, moved_ref, gram_ref, held, sems = refs[-8:]
    b = pl.program_id(0)
    total_ref[...] = base_ref[...]
    gather_products(
        origin_ref, offset_ref, first_ref, count_ref, kind_ref, sources, coupling_ref, held, sems, total_ref
    )
    moved = total_ref[...].astype(jnp.bfloat16)
    moved_ref[...] = moved

    @pl.when(b == 0)
    def _():
        gram_ref[...] = jnp.zeros_like(gram_ref)

    @pl.when(settled_ref[b] == 1)
    def _():
        gram_ref[...] += gram_part(moved, bathed_ref[...])


def late_kernel(origin_ref, offset_ref, first_ref, count_ref, kind_ref, visit_ref, number_ref, *refs):
    sources = refs[:-10]
    coupling_ref, base_ref, bathed_ref, _, before_ref, moved_ref, gram_ref, total, held, sems = refs[-10:]
    b = pl.program_id(0)

    @pl.when(b == 0)
    def _():
        gram_ref[...] = before_ref[...]

    @pl.when(b < number_ref[0])
    def _():
        total[...] = base_ref[...]
        gather_products(
            origin_ref, offset_ref, first_ref, count_ref, kind_ref, sources, coupling_ref, held, sems, total,
            visits=(visit_ref, number_ref),
        )
        moved = total[...].astype(jnp.bfloat16)
        moved_ref[...] = moved
        gram_ref[...] += gram_part(moved, bathed_ref[...])


def early_part(lists, sources, coupling_blocks, own, energy):
    blocks, slots = lists[0].shape
    kinds, block_rows, _ = coupling_blocks.shape
    rows, rank = own.shape
    tile = pl.BlockSpec((block_rows, rank), lambda b, *_: (b, 0))
    return pl.pallas_call(
        early_kernel,
        grid_spec=pltpu.PrefetchScalarGridSpec(
            num_scalar_prefetch=5,
            grid=(blocks,),
            in_specs=[
                *[pl.BlockSpec(memory_space=pltpu.HBM) for _ in sources],
                pl.BlockSpec(memory_space=pltpu.HBM),
                tile,
                pl.BlockSpec((blocks, block_rows), lambda b, *_: (0, 0)),
            ],
            out_specs=tile,
            scratch_shapes=[
                pltpu.VMEM((kinds, block_rows, block_rows), jnp.bfloat16),
                pltpu.VMEM((2, slots, block_rows, rank), jnp.bfloat16),
                pltpu.SemaphoreType.DMA((2, slots)),
                pltpu.SemaphoreType.DMA,
            ],
        ),
        out_shape=jax.ShapeDtypeStruct((rows, rank), jnp.float32),
        compiler_params=pltpu.CompilerParams(vmem_limit_bytes=12 * 2**20),
        cost_estimate=pl.CostEstimate(
            flops=blocks * slots * block_rows * block_rows * rank,
            bytes_accessed=blocks * slots * block_rows * rank * 2,
            transcendentals=0,
        ),
        name="couple_early",
    )(*lists, *sources, coupling_blocks, own, energy)


def middle_part(lists, sources, coupling_blocks, base):
    blocks, slots = lists[0].shape
    kinds, block_rows, _ = coupling_blocks.shape
    rows, rank = base.shape
    tile = pl.BlockSpec((block_rows, rank), lambda b, *_: (b, 0))
    return pl.pallas_call(
        middle_kernel,
        grid_spec=pltpu.PrefetchScalarGridSpec(
            num_scalar_prefetch=5,
            grid=(blocks,),
            in_specs=[
                *[pl.BlockSpec(memory_space=pl.ANY) for _ in sources],
                pl.BlockSpec((kinds, block_rows, block_rows), lambda b, *_: (0, 0, 0)),
                tile,
            ],
            out_specs=tile,
            scratch_shapes=[
                pltpu.VMEM((2, slots, block_rows, rank), jnp.bfloat16),
                pltpu.SemaphoreType.DMA((2, slots)),
            ],
        ),
        out_shape=jax.ShapeDtypeStruct((rows, rank), jnp.float32),
        compiler_params=pltpu.CompilerParams(vmem_limit_bytes=14 * 2**20),
        cost_estimate=pl.CostEstimate(
            flops=blocks * slots * block_rows * block_rows * rank,
            bytes_accessed=blocks * slots * block_rows * rank * 2,
            transcendentals=0,
        ),
        name="couple_middle",
    )(*lists, *sources, coupling_blocks, base)


def settle_part(lists, settled, sources, coupling_blocks, base, bathed):
    blocks, slots = lists[0].shape
    kinds, block_rows, _ = coupling_blocks.shape
    rows, rank = base.shape
    tile = pl.BlockSpec((block_rows, rank), lambda b, *_: (b, 0))
    return pl.pallas_call(
        settle_kernel,
        grid_spec=pltpu.PrefetchScalarGridSpec(
            num_scalar_prefetch=6,
            grid=(blocks,),
            in_specs=[
                *[pl.BlockSpec(memory_space=pl.ANY) for _ in sources],
                pl.BlockSpec((kinds, block_rows, block_rows), lambda b, *_: (0, 0, 0)),
                tile,
                tile,
            ],
            out_specs=[tile, tile, pl.BlockSpec((rank, 2 * rank), lambda b, *_: (0, 0))],
            scratch_shapes=[
                pltpu.VMEM((2, slots, block_rows, rank), jnp.bfloat16),
                pltpu.SemaphoreType.DMA((2, slots)),
            ],
        ),
        out_shape=[
            jax.ShapeDtypeStruct((rows, rank), jnp.float32),
            jax.ShapeDtypeStruct((rows, rank), jnp.bfloat16),
            jax.ShapeDtypeStruct((rank, 2 * rank), jnp.float32),
        ],
        compiler_params=pltpu.CompilerParams(vmem_limit_bytes=16 * 2**20),
        cost_estimate=pl.CostEstimate(
            flops=blocks * slots * block_rows * block_rows * rank,
            bytes_accessed=blocks * slots * block_rows * rank * 2,
            transcendentals=0,
        ),
        name="couple_settle",
    )(*lists, settled, *sources, coupling_blocks, base, bathed)


def late_part(lists, visits, number, sources, coupling_blocks, base, bathed, moved, gram):
    blocks, slots = lists[0].shape
    kinds, block_rows, _ = coupling_blocks.shape
    rows, rank = base.shape

    def visited(b, *scalars):
        return scalars[5][jnp.minimum(b, scalars[6][0] - 1)], 0

    tile = pl.BlockSpec((block_rows, rank), visited)
    whole = pl.BlockSpec((rank, 2 * rank), lambda b, *_: (0, 0))
    return pl.pallas_call(
        late_kernel,
        grid_spec=pltpu.PrefetchScalarGridSpec(
            num_scalar_prefetch=7,
            grid=(blocks,),
            in_specs=[
                *[pl.BlockSpec(memory_space=pl.ANY) for _ in sources],
                pl.BlockSpec((kinds, block_rows, block_rows), lambda b, *_: (0, 0, 0)),
                tile,
                tile,
                pl.BlockSpec(memory_space=pl.ANY),
                whole,
            ],
            out_specs=[tile, whole],
            scratch_shapes=[
                pltpu.VMEM((block_rows, rank), jnp.float32),
                pltpu.VMEM((2, slots, block_rows, rank), jnp.bfloat16),
                pltpu.SemaphoreType.DMA((2, slots)),
            ],
        ),
        out_shape=[
            jax.ShapeDtypeStruct((rows, rank), jnp.bfloat16),
            jax.ShapeDtypeStruct((rank, 2 * rank), jnp.float32),
        ],
        input_output_aliases={7 + len(sources) + 3: 0},
        compiler_params=pltpu.CompilerParams(vmem_limit_bytes=16 * 2**20),
        name="couple_late",
    )(*lists, visits, number, *sources, coupling_blocks, base, bathed, moved, gram)


def inverse_factor(square, start, lowest):
    n = square.shape[0]
    eye = (
        lax.broadcasted_iota(jnp.int32, (n, n), 0) == lax.broadcasted_iota(jnp.int32, (n, n), 1)
    ).astype(jnp.float32)
    work = jnp.concatenate([square, eye], axis=1)
    bands = [work[8 * i : 8 * i + 8, :] for i in range(n // 8)]
    sublane = lax.broadcasted_iota(jnp.int32, (8, 2 * n), 0)
    def spread(band, g):
        return [jnp.broadcast_to(band[:, 8 * g + r : 8 * g + r + 1], (8, 2 * n)) for r in range(8)]

    out = []
    for g in range(n // 8):
        band = bands[g]
        pivots = spread(band, g)
        diagonal = jnp.zeros((8, 2 * n), jnp.float32)
        scales = []
        for r in range(8):
            scales.append(pl.reciprocal(pivots[r][r : r + 1, :], approx=True))
            diagonal = jnp.where(sublane == r, pivots[r], diagonal)
            share = jnp.where(sublane > r, pivots[r] * scales[r], 0.0)
            for q in range(r + 1, 8):
                pivots[q] = pivots[q] - share * pivots[q][r : r + 1, :]
            band = band - share * band[r : r + 1, :]
        out.append(band[:, n:] * lax.rsqrt(diagonal)[:, n:])
        lowest[...] = jnp.minimum(lowest[...], diagonal / start[8 * g : 8 * g + 8, :])
        for i in range(g + 1, n // 8):
            columns = spread(bands[i], g)
            below = bands[i]
            for r in range(8):
                share = columns[r] * scales[r]
                for q in range(r + 1, 8):
                    columns[q] = columns[q] - share * pivots[q][r : r + 1, :]
                below = below - share * band[r : r + 1, :]
            bands[i] = below
    return jnp.concatenate(out, axis=0)


def eliminate(inner, image, start, lowest):
    rank = inner.shape[0]
    diagonal = lax.broadcasted_iota(jnp.int32, (rank, rank), 0) == lax.broadcasted_iota(jnp.int32, (rank, rank), 1)
    start[...] = jnp.broadcast_to(
        jnp.sum(jnp.where(diagonal, inner[...], 0.0), axis=1, keepdims=True), start.shape
    )
    lowest[...] = jnp.ones_like(lowest)

    def product(left, right, contract):
        return lax.dot_general(
            left, right, ((contract, (0,)), ((), ())),
            precision=HIGHEST, preferred_element_type=jnp.float32,
        )

    for low in range(0, rank, PANEL):
        high = low + PANEL
        here, first = low // 128 * 128, high // 128 * 128
        inverse = inverse_factor(inner[low:high, low:high], start[low:high, :], lowest)
        panel = product(inverse, inner[low:high, here:], (1,))
        inner[low:high, here:] = panel
        share = panel[:, high - here :]
        if high < rank:
            inner[high:, first:] -= product(share, panel[:, first - here :], (0,))
        side = image[low:high, :]
        if low > 0:
            side = side - product(inner[:low, low:high], image[:low, :], (0,))
        image[low:high, :] = product(inverse, side, (1,))


def finish_kernel(
    order_ref, left_ref, right_ref, moved_hbm, bathed_hbm, out_hbm,
    gram, inner, image, start, lowest, moved, bathed, out, in_sems, out_sems,
):
    rank = left_ref.shape[0]
    load_moved = pltpu.make_async_copy(moved_hbm, moved, in_sems.at[0])
    load_bathed = pltpu.make_async_copy(bathed_hbm, bathed, in_sems.at[1])
    load_moved.start()
    load_bathed.start()

    chunks = order_ref.shape[0]
    size = rank // chunks
    half = rank // 2
    for i in range(chunks):
        rows = pl.ds(pl.multiple_of(order_ref[i] * size, size), size)
        below = pl.ds(pl.multiple_of(rank + order_ref[i] * size, size), size)
        chunk = jnp.concatenate(
            [left_ref[i * size : (i + 1) * size, :], right_ref[i * size : (i + 1) * size, :]], axis=1
        )

        @pl.when(order_ref[i] < chunks // 2)
        def _():
            gram[rows, :] = chunk[:, : 2 * rank]
            gram[below, rank : rank + half] = chunk[:, 2 * rank :]

        @pl.when(order_ref[i] >= chunks // 2)
        def _():
            gram[rows, half:] = chunk[:, : rank + half]
            gram[below, rank:] = chunk[:, rank + half :]

    gram[half:rank, :half] = gram[:half, half:rank].T
    gram[rank : rank + half, rank + half :] = gram[rank + half :, rank : rank + half].T
    gram[rank:, :rank] = gram[:rank, rank:].T
    largest = jnp.max(jnp.max(jnp.abs(gram[...]), axis=0, keepdims=True), axis=1, keepdims=True)
    gram[...] = gram[...] * (1.0 / largest)
    product = jnp.dot(gram[:rank, :], gram[...], precision=HIGHEST, preferred_element_type=jnp.float32)

    def inner_product():
        rows = image[...]
        inner[...] = lax.dot_general(
            rows, rows, (((1,), (1,)), ((), ())),
            precision=HIGHEST, preferred_element_type=jnp.float32,
        )

    image[...] = product
    inner_product()
    eliminate(inner, image, start, lowest)
    safe = jnp.min(lowest[...]) >= SMALLEST_PIVOT

    @pl.when(jnp.logical_not(safe))
    def _():
        later = jnp.dot(gram[:rank, :], gram[...], precision=HIGHEST, preferred_element_type=jnp.float32)
        inner[...] = later[:, :rank]
        image[:, rank:] = later[:, rank:]
        eliminate(inner, image.at[:, rank:], start, lowest)
        upper = lax.broadcasted_iota(jnp.int32, (rank, rank), 0) <= lax.broadcasted_iota(jnp.int32, (rank, rank), 1)
        image[:, :rank] = jnp.where(upper, inner[...], 0.0)
        inner_product()
        eliminate(inner, image, start, lowest)

    rotation = image[...].T.astype(jnp.bfloat16)
    load_moved.wait()
    load_bathed.wait()
    pieces = out_sems.shape[0]
    size = moved.shape[0] // pieces

    def store(piece):
        rows = pl.ds(pl.multiple_of(piece * size, size), size)
        return pltpu.make_async_copy(out.at[rows, :], out_hbm.at[rows, :], out_sems.at[piece])

    def one(piece, carry):
        rows = pl.ds(pl.multiple_of(piece * size, size), size)
        stacked = jnp.concatenate([moved[rows, :], bathed[rows, :]], axis=1)
        value = jnp.dot(stacked, rotation, preferred_element_type=jnp.float32)
        out[rows, :] = value.astype(jnp.bfloat16)
        store(piece).start()
        return carry

    lax.fori_loop(0, pieces, one, 0)

    def drain(piece, carry):
        store(piece).wait()
        return carry

    lax.fori_loop(0, pieces, drain, 0)


def finish_part(order, left, right, moved, bathed):
    rows, rank = moved.shape
    return pl.pallas_call(
        finish_kernel,
        in_specs=[
            pl.BlockSpec(memory_space=pltpu.SMEM),
            pl.BlockSpec(memory_space=pltpu.VMEM),
            pl.BlockSpec(memory_space=pltpu.VMEM),
            pl.BlockSpec(memory_space=pltpu.HBM),
            pl.BlockSpec(memory_space=pltpu.HBM),
        ],
        out_specs=pl.BlockSpec(memory_space=pl.ANY),
        out_shape=jax.ShapeDtypeStruct((rows, rank), jnp.bfloat16),
        scratch_shapes=[
            pltpu.VMEM((2 * rank, 2 * rank), jnp.float32),
            pltpu.VMEM((rank, rank), jnp.float32),
            pltpu.VMEM((rank, 2 * rank), jnp.float32),
            pltpu.VMEM((rank, 2 * PANEL), jnp.float32),
            pltpu.VMEM((8, 2 * PANEL), jnp.float32),
            pltpu.VMEM((rows, rank), jnp.bfloat16),
            pltpu.VMEM((rows, rank), jnp.bfloat16),
            pltpu.VMEM((rows, rank), jnp.bfloat16),
            pltpu.SemaphoreType.DMA((2,)),
            pltpu.SemaphoreType.DMA((8,)),
        ],
        compiler_params=pltpu.CompilerParams(vmem_limit_bytes=14 * 2**20),
        name="finish",
    )(order, left, right, moved, bathed)


def ring_order(count):
    wide = 2
    while 4 * wide * wide <= count:
        wide *= 2
    tall = count // wide
    walk = [0]
    for r in range(tall):
        across = range(1, wide)
        walk += [r * wide + c for c in (across if r % 2 == 0 else reversed(across))]
    return walk + [r * wide for r in range(tall - 1, 0, -1)]


PIECES = 4


def tie(one, other):
    return lax.optimization_barrier((one, other))


def early_steps():
    return lax.axis_size("col") // 2 - 1


def ring_gather(own, side, stages, small, early):
    order = ring_order(lax.axis_size("col"))
    following = order[1:] + order[:1]
    forward = list(zip(order, following))
    back = list(zip(following, order))
    size = own.shape[0] // PIECES
    pieces = [own[i * size : (i + 1) * size] for i in range(PIECES)]
    stages = list(stages)
    steps = []
    total = None
    for step in range(1, len(order)):
        if step > 1:
            pieces[-1], side = tie(pieces[-1], side)
        if step == 3:
            pieces[-1], small = tie(pieces[-1], small)
        if step == early_steps() + 3:
            total = early(small, [piece for done in steps[: early_steps()] for piece in done])
            pieces[-1], total = tie(pieces[-1], total)
        pieces = [
            lax.ppermute(piece, "col", forward if i < PIECES // 2 else back)
            for i, piece in enumerate(pieces)
        ]
        if step > 1 and stages:
            side = stages.pop(0)(side)
        steps.append(list(pieces))
    return steps, side, small, total


def slot_lists(ids, counts, kinds):
    blocks, slots = ids.shape
    count = lax.axis_size("col")
    order = ring_order(count)
    place = jnp.asarray([order.index(c) for c in range(count)], jnp.int32)
    col = jnp.arange(count, dtype=jnp.int32)
    mine = jnp.sum(jnp.where(col == lax.axis_index("col"), place, 0))
    owner, within = ids // blocks, ids % blocks
    theirs = jnp.sum(jnp.where(owner[..., None] == col, place, 0), axis=-1)
    in_piece = blocks // PIECES
    piece = within // in_piece
    step = jnp.where(piece >= PIECES // 2, theirs - mine, mine - theirs) % count
    before = early_steps()
    last = step == count - 1
    outer = (piece == 0) | (piece == PIECES - 1)
    part = (step > before).astype(jnp.int32) + last.astype(jnp.int32) + (last & ~outer).astype(jnp.int32)
    origin = jnp.where(
        part == 0,
        jnp.where(step == 0, 0, 1 + (step - 1) * PIECES + piece),
        jnp.where(part == 1, (step - before - 1) * PIECES + piece, jnp.where(outer, piece // (PIECES - 1), piece - 1)),
    )
    offset = jnp.where(step == 0, within, within % in_piece)
    slot = jnp.arange(slots, dtype=jnp.int32)
    used = slot[None, :] < counts[:, None]
    key = jnp.where(used, part, 4) * slots + slot
    rank = jnp.sum((key[:, None, :] < key[:, :, None]).astype(jnp.int32), axis=-1)
    at = rank[:, :, None] == slot

    def arrange(values):
        return jnp.sum(jnp.where(at, values[:, :, None], 0), axis=1)

    origin, offset, kinds = arrange(origin), arrange(offset), arrange(kinds)
    parts = []
    first = jnp.zeros_like(counts)
    for i in range(4):
        number = jnp.sum((used & (part == i)).astype(jnp.int32), axis=1)
        parts.append((origin, offset, first, number, kinds))
        first = first + number
    block = jnp.arange(blocks, dtype=jnp.int32)
    key = jnp.where(parts[3][3] > 0, 0, blocks) + block
    turn = jnp.sum((key[None, :] < key[:, None]).astype(jnp.int32), axis=1)
    number = jnp.maximum(jnp.sum((parts[3][3] > 0).astype(jnp.int32), keepdims=True), 1)
    visits = jnp.sum(jnp.where(turn[:, None] == block, block[:, None], 0), axis=0)
    settled = (turn >= number).astype(jnp.int32)
    return parts, settled, visits, number


def swap(value, axis, stride):
    count = lax.axis_size(axis)
    return lax.ppermute(value, axis, [(i, i ^ stride) for i in range(count)])


def strides(axis):
    return [1 << i for i in range(lax.axis_size(axis).bit_length() - 1)]


def side_of(axis, stride):
    return (lax.axis_index(axis) >> (stride.bit_length() - 1)) & 1


def halve(value, swapped, lower):
    half = value.shape[0] // 2
    keep = jnp.where(lower, value[:half], value[half:])
    give = jnp.where(lower, value[half:], value[:half])
    return keep + swap(give, *swapped)


def sum_relative(value, col_strides):
    for stride in col_strides:
        value = value + swap(value, "col", stride)
    for stride in reversed(strides("row")):
        value = jnp.concatenate([value, swap(value, "row", stride)], axis=0)
    return value


def pack(upper, corner, lower):
    half = corner.shape[1] // 2
    left = jnp.where(lower, upper[:, : 3 * half], upper[:, half:])
    right = jnp.where(lower, jnp.concatenate([upper[:, 3 * half :], corner[:, :half]], axis=1), corner)
    return left, right


def chunk_order():
    swaps = strides("row")
    relative = jnp.arange(1 << len(swaps), dtype=jnp.int32)
    mine = jnp.zeros_like(relative)
    for i, stride in enumerate(swaps):
        mine = mine + (side_of("row", stride) << (len(swaps) - 1 - i))
    return relative ^ mine


def shards(
    density_factor,
    onsite,
    neighbour_ids,
    neighbour_count,
    coupling_type,
    coupling_blocks,
    bath_pattern,
    bath_blocks,
):
    blocks, slots = neighbour_ids.shape
    group_blocks = lax.axis_size("col") * blocks
    in_group = neighbour_ids - lax.axis_index("row") * group_blocks
    lists = slot_lists(in_group, neighbour_count, coupling_type)
    bathed, corner = bath_part(density_factor, bath_pattern, bath_blocks)
    energy = onsite.reshape(blocks, -1)
    swaps = strides("row")
    lower = [side_of("row", stride) == 0 for stride in swaps]

    def over_row(value, lower):
        for stride, chosen in zip(swaps, lower):
            value = halve(value, ("row", stride), chosen)
        return value

    def early(small, pieces):
        (lists, _, _, _), energy, _, _ = small
        return early_part(lists[0], [density_factor] + pieces, coupling_blocks, density_factor, energy)

    steps, corner, small, total = ring_gather(
        density_factor,
        corner,
        [lambda value: over_row(value, lower)],
        (lists, energy, chunk_order(), lower),
        early,
    )
    (lists, settled, visits, number), _, order, lower = small
    between = [piece for step in steps[early_steps() : -1] for piece in step]
    total = middle_part(lists[1], between, coupling_blocks, total)
    outer, inner = [steps[-1][0], steps[-1][-1]], steps[-1][1:-1]
    total, moved, upper = settle_part(lists[2], settled, outer, coupling_blocks, total, bathed)
    moved, upper = late_part(lists[3], visits, number, inner, coupling_blocks, total, bathed, moved, upper)
    left, right = pack(over_row(upper, lower), corner, lower[0])
    col_strides = strides("col")
    left = sum_relative(left, col_strides)
    right = sum_relative(right, col_strides[1:] + col_strides[:1])
    return finish_part(order, left, right, moved, bathed)


def solution(mesh):
    placed = (
        P(("row", "col"), None),
        P(("row", "col")),
        P(("row", "col"), None),
        P(("row", "col")),
        P(("row", "col"), None),
        P(),
        P(("row", "col")),
        P(),
    )
    return jax.shard_map(
        shards, mesh=mesh, in_specs=placed, out_specs=P(("row", "col"), None), check_vma=False
    )
```
